32 devices in a mesh: seq: 8 (over y, x, core), col: 4 (over z).
Axes of the slice: x: 2, y: 2, z: 4, core: 2. Of those that a mesh axis runs over, the one named last changes fastest.
Arguments:
- inputs: bfloat16 [16384, 2048], P(('seq', 'col'))
- norm_gain: float32 [2048], replicated, may hold values from 0.5 to 1.5
- norm_bias: float32 [2048], replicated, may hold values from -3 to 3
- weight: bfloat16 [2048, 6144], P(None, 'col'), may hold values from -0.125 to 0.125
- forget_peep: float32 [2048], P('col'), may hold values from -1 to 1
- reset_peep: float32 [2048], P('col'), may hold values from -1.5 to 1.5
- forget_bias: float32 [2048], P('col')
- reset_bias: float32 [2048], P('col'), may hold values from -4 to 4
- seq_lengths: int32 [4], replicated, may hold values from 1 to 15701, as said below
- out_grad: bfloat16 [16384, 2048], P('seq', 'col'), may hold values from -6 to 6
Outputs:
- output: bfloat16 [16384, 2048], P('seq', 'col')
- input_grad: float32 [16384, 2048], P(('seq', 'col'))
- weight_grad: float32 [2048, 6144], P(None, 'col')
- gain_grad: float32 [2048], replicated
- bias_grad: float32 [2048], replicated
- forget_peep_grad: float32 [2048], P('col')
- reset_peep_grad: float32 [2048], P('col')
- forget_bias_grad: float32 [2048], P('col')
- reset_bias_grad: float32 [2048], P('col')
The draws below stay inside these ranges and needn't reach their ends.
Inputs may be any that keep to these rules, and one draw needn't show every extreme that they name: `seq_lengths`: the 4 sequences fill all 16384 tokens end to end. One of them, at a place drawn from the seed, begins within the first 2048 tokens and ends within the last 2048; each other one is shorter than 682.
All inputs are finite; a program needn't handle non-finite values.
Results may differ from the reference program's by a relative error of at most 0.014.
Values may be sent and summed in bfloat16 or wider, within the bound.
No kernel may reach another device: no remote copies, remote signals or barrier semaphores. Data moves between devices by JAX's collectives and lax.ppermute only.
A program may use at most 192 MiB of HBM per device.

```python
import jax
import jax.numpy as jnp
from jax import lax

D = 2048
NSEQS = 4
TOK_SPAN = 2048
TOKENS = 16384
N_SEQ = 8


def draw_inputs(key, part):
    key = jax.random.fold_in(key, 11)
    common_key, noise_key = jax.random.split(key)
    common = jax.random.normal(common_key, (1, D), jnp.float32)
    row_noise = jax.random.normal(noise_key, (TOKENS, D), jnp.float32)
    values = common + row_noise
    return values.astype(jnp.bfloat16)


def draw_forget_bias(key, part):
    key = jax.random.fold_in(key, 23)
    pick_key, slow_key, fast_key = jax.random.split(key, 3)
    slow_share = 0.5
    chosen = jax.random.uniform(pick_key, (D,), jnp.float32) < slow_share
    slow_level = jnp.log(TOKENS * 1.0) + jax.random.uniform(slow_key, (D,), jnp.float32, -1.0, 1.0)
    fast_level = jax.random.uniform(fast_key, (D,), jnp.float32, 2.0, 4.0)
    return jnp.where(chosen, slow_level, fast_level).astype(jnp.float32)


def draw_seq_lengths(key, part):
    key = jax.random.fold_in(key, 37)
    length_key, order_key, place_key = jax.random.split(key, 3)
    longest_short = TOK_SPAN // 3 - 1
    offset = jax.random.randint(length_key, (), 0, longest_short)
    shorter = jnp.stack([jnp.int32(1), (1 + offset).astype(jnp.int32), (longest_short - offset).astype(jnp.int32)])
    shorter = jax.random.permutation(order_key, shorter)
    place = jax.random.randint(place_key, (), 0, NSEQS)
    long_length = TOKENS - jnp.sum(shorter)
    order = jnp.arange(NSEQS)
    source = jnp.clip(jnp.where(order < place, order, order - 1), 0, NSEQS - 2)
    return jnp.where(order == place, long_length, shorter[source]).astype(jnp.int32)


def shard_levels(key, extent, pieces, least, largest):
    gain, own = 1.0, jax.random.fold_in(key, 6)
    for axis_at, parts in pieces:
        draws = jnp.exp(jax.random.uniform(jax.random.fold_in(own, axis_at), (parts,), jnp.float32, least / len(pieces), largest / len(pieces)))
        gain = gain * jnp.repeat(draws, extent[axis_at] // parts).reshape([-1 if axis == axis_at else 1 for axis in range(len(extent))])
    return gain


def noise(own_key, dims, scale, limit, cuts=(), kind=jnp.bfloat16):
    values = scale * jax.random.normal(own_key, dims, jnp.float32)
    if cuts:
        values = values * shard_levels(own_key, dims, cuts, -0.22, 0.18)
    return jnp.clip(values, -limit, limit).astype(kind)


def setup_inputs(seed: int = 0) -> dict:
    streams_of = jax.random.split(jax.random.key(seed), 11)
    return {
        "inputs": draw_inputs(jax.random.fold_in(streams_of[10], 71), 0),
        "norm_gain": jnp.clip(1.0 + 0.1 * jax.random.normal(streams_of[1], (D,), jnp.float32), 0.5, 1.5),
        "norm_bias": noise(streams_of[2], (D,), 0.5, 3.0, (), jnp.float32),
        "weight": noise(streams_of[3], (D, 3 * D), D ** -0.5, 0.125, ((1, 4),)),
        "forget_peep": jnp.clip(jax.random.uniform(streams_of[4], (D,), jnp.float32, -1.0, 1.0) * shard_levels(streams_of[4], (D,), ((0, 4),), -0.4, 0.0), -1.0, 1.0),
        "reset_peep": jnp.clip(jax.random.uniform(streams_of[5], (D,), jnp.float32, -1.5, 1.5) * shard_levels(streams_of[5], (D,), ((0, 4),), -0.4, 0.0), -1.5, 1.5),
        "forget_bias": draw_forget_bias(jax.random.fold_in(streams_of[10], 71), 0),
        "reset_bias": noise(streams_of[7], (D,), 1.0, 4.0, ((0, 4),), jnp.float32),
        "seq_lengths": draw_seq_lengths(jax.random.fold_in(streams_of[10], 71), 0),
        "out_grad": noise(streams_of[9], (TOKENS, D), 1.0, 6.0, ((0, 8), (1, 4))),
    }


EPSILON = 1e-05

@jax.custom_vjp
def low(v):
    return lax.optimization_barrier(v.astype(jnp.bfloat16)).astype(jnp.float32)

@jax.custom_vjp
def low_back(v):
    return v

def low_keep(v):
    return (low(v), None)

def low_pass(kept, grad):
    return (grad,)

def back_keep(v):
    return (v, None)

def back_low(kept, grad):
    return (low(grad),)
low.defvjp(low_keep, low_pass)
low_back.defvjp(back_keep, back_low)

def layer_norm(row_values, norm_gain, norm_bias):
    average = lax.optimization_barrier(jnp.mean(row_values, axis=-1, keepdims=True))
    centred = row_values - average
    inv_scale = lax.rsqrt(lax.optimization_barrier(jnp.mean(centred * centred, axis=-1, keepdims=True)) + EPSILON)
    return centred * inv_scale * norm_gain + norm_bias

def run_block(cell_state, block_pair):

    def advance(running, pair_now):
        updated = pair_now[0] * running + pair_now[1]
        return (updated, (updated, running))
    return lax.scan(advance, cell_state, block_pair)

def forward(row_values, norm_gain, norm_bias, weight, forget_peep, reset_peep, forget_bias, reset_bias, kept_mask):
    normed = low(layer_norm(row_values, norm_gain, norm_bias))
    mixed = low_back(low(jnp.dot(normed, weight, precision=lax.Precision.HIGHEST)))
    candidate = mixed[:, :D]
    forget_pre = mixed[:, D:2 * D]
    reset_pre = mixed[:, 2 * D:]
    highway = low_back(row_values)
    forget = jax.nn.sigmoid(forget_pre + forget_peep * candidate + forget_bias)
    decay = (forget * kept_mask).reshape(N_SEQ, TOK_SPAN, D)
    inject = ((1.0 - forget) * candidate).reshape(N_SEQ, TOK_SPAN, D)
    initial = jnp.zeros((D,), jnp.float32)
    states, previous = lax.scan(jax.checkpoint(run_block), initial, (decay, inject))[1]
    states = states.reshape(TOKENS, D)
    previous = previous.reshape(TOKENS, D) * kept_mask
    reset = jax.nn.sigmoid(reset_pre + reset_peep * previous + reset_bias)
    return reset * states + (1.0 - reset) * highway

def reference(inputs, norm_gain, norm_bias, weight, forget_peep, reset_peep, forget_bias, reset_bias, seq_lengths, out_grad):
    positions = jnp.arange(TOKENS, dtype=jnp.int32)
    bounds = (jnp.cumsum(seq_lengths) - seq_lengths).astype(jnp.int32)
    starts = jnp.any(positions[:, None] == bounds[None, :], axis=1)
    kept_mask = 1.0 - starts.astype(jnp.float32)[:, None]
    primals = (inputs.astype(jnp.float32), norm_gain, norm_bias, weight.astype(jnp.float32), forget_peep, reset_peep, forget_bias, reset_bias)

    def closed(*values):
        return forward(*values, kept_mask)
    output, pullback = jax.vjp(closed, *primals)
    grads = pullback(out_grad.astype(jnp.float32))
    return (output.astype(jnp.bfloat16), grads[0], grads[3], grads[1], grads[2], grads[4], grads[5], grads[6], grads[7])
```

```python
import functools

import jax
import jax.numpy as jnp
import numpy as np
from jax import lax
from jax.experimental import pallas as pl
from jax.experimental.pallas import tpu as pltpu
from jax.sharding import PartitionSpec as P

EPSILON = 1e-05
F32 = jnp.float32
BF16 = jnp.bfloat16
LANES = 128
SUB = 8
VMEM_LIMIT = 56 * 1024 * 1024


def bits_of(count):
    return [1 << b for b in range(count.bit_length() - 1)]


def colour(edges, count):
    degree = max([sum(e[0] == n for e in edges) for n in range(count)] + [sum(e[1] == n for e in edges) for n in range(count)])
    out = [[None] * degree for _ in range(count)]
    into = [[None] * degree for _ in range(count)]
    taken = {}
    for at, edge in enumerate(edges):
        src, dst = edge[0], edge[1]
        first = next(c for c in range(degree) if out[src][c] is None)
        second = next(c for c in range(degree) if into[dst][c] is None)
        if first != second:
            path, node, at_dst, look = [], dst, True, first
            while True:
                found = (into if at_dst else out)[node][look]
                if found is None:
                    break
                path.append(found)
                node = edges[found][0] if at_dst else edges[found][1]
                at_dst = not at_dst
                look = second if look == first else first
            for found in path:
                old = taken[found]
                out[edges[found][0]][old] = None
                into[edges[found][1]][old] = None
            for found in path:
                new = second if taken[found] == first else first
                taken[found] = new
                out[edges[found][0]][new] = found
                into[edges[found][1]][new] = found
        taken[at] = first
        out[src][first] = at
        into[dst][first] = at
    rounds = [[] for _ in range(degree)]
    for at, edge in enumerate(edges):
        rounds[taken[at]].append(edge)
    return rounds


def routes(groups):
    low = groups // 2
    plans = []
    for core in range(2):
        local, edges = [], []
        for dst in range(groups):
            for stream in range(3):
                block = stream * groups + dst % low + low * core
                src, at = block // 3, block % 3
                (local if src == dst else edges).append((src, dst, stream, at))
        plans.append((local, colour(edges, groups)))
    count = max(len(rounds) for _, rounds in plans)
    return [(local, rounds + [[]] * (count - len(rounds))) for local, rounds in plans], count


def row_order(rows):
    seg = rows // SUB
    matrix = np.zeros((rows, rows), np.float32)
    for i in range(seg):
        for j in range(SUB):
            matrix[i * SUB + j, j * seg + i] = 1.0
    return matrix


def gate(value):
    small = jnp.exp(-jnp.abs(value))
    minor = small / (1.0 + small)
    major = 1.0 - minor
    up = value >= 0.0
    return jnp.where(up, major, minor), jnp.where(up, minor, major)


def kept_of(base, step, seg, bounds, channels):
    at = lax.broadcasted_iota(jnp.int32, (SUB, LANES), 0) * seg + (base + step)
    starts = at == bounds[0]
    for bound in bounds[1:]:
        starts = starts | (at == bound)
    kept = jnp.where(starts, 0.0, 1.0)
    return jnp.concatenate([kept] * (channels // LANES), axis=1)


class Info:
    P, K, ZHI, ZLO, G, BASE = 0, 1, 2, 3, 4, 5

    def __init__(self, chunks, sequences):
        self.chunks = chunks
        self.sequences = sequences

    def base(self, ref, chunk):
        return ref[self.BASE + chunk]

    def bounds(self, ref):
        return [ref[self.BASE + self.chunks + n] for n in range(self.sequences)]


def forward_kernel(
    info, chunk, seg, first, s, x_ref, gain_ref, bias_ref, w_ref, fp_ref, fb_ref, *refs
):
    normed_ref, mixed_ref, hx_ref, stat_ref, map_ref = refs if first else refs[5:]
    channels = w_ref.shape[2]
    x = x_ref[...].astype(F32)
    average = jnp.mean(x, axis=1, keepdims=True)
    centred = x - average
    inv = lax.rsqrt(jnp.mean(centred * centred, axis=1, keepdims=True) + EPSILON)
    normed = (centred * inv * gain_ref[...] + bias_ref[...]).astype(BF16)
    normed_ref[0] = normed
    lane = lax.broadcasted_iota(jnp.int32, (x.shape[0], LANES), 1)
    stat_ref[0] = jnp.where(lane == 0, average, inv)
    hx_ref[0] = x_ref[:, pl.ds(pl.multiple_of(s[info.G] * channels, channels), channels)]
    for stream in range(3):
        mixed_ref[0, stream] = jnp.dot(normed, w_ref[stream], preferred_element_type=F32).astype(BF16)

    @pl.when(pl.program_id(0) == 0)
    def _():
        map_ref[0, 0] = jnp.ones((SUB, channels), F32)
        map_ref[0, 1] = jnp.zeros((SUB, channels), F32)

    candidate_all = mixed_ref[0, 0].astype(F32)
    pre_all = mixed_ref[0, 1].astype(F32)
    steps = x.shape[0] // SUB
    start = pl.program_id(0) * steps
    base = info.base(s, chunk)
    bounds = info.bounds(s)
    run_decay, run_state = map_ref[0, 0], map_ref[0, 1]
    for i in range(steps):
        candidate = candidate_all[i * SUB : (i + 1) * SUB]
        pre = pre_all[i * SUB : (i + 1) * SUB]
        forget, rest = gate(pre + fp_ref[...] * candidate + fb_ref[...])
        decay = forget * kept_of(base, start + i, seg, bounds, channels)
        run_state = decay * run_state + rest * candidate
        run_decay = decay * run_decay
    map_ref[0, 0] = run_decay
    map_ref[0, 1] = run_state


def run_map_kernel(info, low, s, map_ref, out_ref):
    channels = map_ref.shape[3]
    rows = []
    for dk in range(2):
        decay = jnp.ones((1, channels), F32)
        state = jnp.zeros((1, channels), F32)
        for zl in range(low):
            c = dk * low + (zl ^ s[info.ZLO])
            for j in range(SUB):
                d, b = map_ref[c, 0, j : j + 1, :], map_ref[c, 1, j : j + 1, :]
                state = d * state + b
                decay = d * decay
        rows += [decay, state]
    out_ref[...] = jnp.concatenate(rows + [jnp.zeros((4, channels), F32)], axis=0)


def state_kernel(
    info, low, planes, seg,
    s, gathered_ref, map_ref, mixed_ref, hx_ref, og_ref, order_ref, back_order_ref, fp_ref, rp_ref, fb_ref, rb_ref,
    out_ref, prev_ref, direct_ref, rz_ref, rzb_ref, skip_ref, binj_ref, sums_ref, runb_ref,
    cell_ref, prod_ref, kept_out_ref,
):
    chunks, channels = map_ref.shape[0], map_ref.shape[3]
    step = pl.program_id(0)
    last = pl.num_programs(0) - 1
    k, zlo = s[info.K], s[info.ZLO]

    @pl.when(step == 0)
    def _():
        carry = jnp.zeros((1, channels), F32)
        own = [carry, carry]
        for plane in range(planes):
            for core in range(2):
                for zh in range(2):
                    e = (zh ^ s[info.ZHI]) * planes + (plane ^ s[info.P])
                    mine = (plane == s[info.P]) & (zh == s[info.ZHI])
                    own[core] = jnp.where(mine, carry, own[core])
                    decay = jnp.where(k == core, gathered_ref[e, 0:1, :], gathered_ref[e, 2:3, :])
                    state = jnp.where(k == core, gathered_ref[e, 1:2, :], gathered_ref[e, 3:4, :])
                    carry = decay * carry + state
        for dk in range(2):
            carry = jnp.where(k == 0, own[dk], own[1 - dk])
            for zl in range(low):
                c = dk * low + (zl ^ zlo)
                for j in range(SUB):
                    cell_ref[c, j : j + 1, :] = carry
                    carry = map_ref[c, 0, j : j + 1, :] * carry + map_ref[c, 1, j : j + 1, :]
        prod_ref[...] = jnp.ones_like(prod_ref)
        binj_ref[...] = jnp.zeros_like(binj_ref)
        sums_ref[...] = jnp.zeros_like(sums_ref)

    rows = hx_ref.shape[1]
    steps = rows // SUB
    bounds = info.bounds(s)
    fp, rp, fb, rb = fp_ref[...], rp_ref[...], fb_ref[...], rb_ref[...]
    rz_sum, peep_sum = sums_ref[0], sums_ref[1]
    for c in range(chunks):
        dk, dz = c // low, c % low
        grad = jnp.dot(order_ref[...], og_ref[dk, dz ^ zlo], preferred_element_type=F32)
        base = info.base(s, c)
        cell, prod, binj = cell_ref[c], prod_ref[c], binj_ref[c]
        for i in range(steps):
            at = slice(i * SUB, (i + 1) * SUB)
            candidate = mixed_ref[c, 0, at].astype(F32)
            forget, rest = gate(mixed_ref[c, 1, at].astype(F32) + fp * candidate + fb)
            kept = kept_of(base, step * steps + i, seg, bounds, channels)
            previous = kept * cell
            decay = forget * kept
            cell = forget * previous + rest * candidate
            reset, skip = gate(mixed_ref[c, 2, at].astype(F32) + rp * previous + rb)
            x = hx_ref[c, at].astype(F32)
            g = grad[at]
            kept_out_ref[c, pl.ds(pl.multiple_of(step * rows + i * SUB, SUB), SUB), :] = reset * cell + skip * x
            direct = g * reset
            g_skip = g * skip
            rz = direct * skip * (cell - x)
            prev_ref[c, at] = previous
            direct_ref[c, at] = direct
            rz_ref[c, at] = rz
            rzb_ref[c, at] = rz.astype(BF16)
            skip_ref[c, at] = g_skip.astype(BF16)
            binj = binj + prod * (decay * direct + kept * (rz * rp))
            prod = prod * decay
            rz_sum = rz_sum + rz
            peep_sum = peep_sum + rz * previous
        cell_ref[c] = cell
        prod_ref[c] = prod
        binj_ref[c] = binj
    sums_ref[0] = rz_sum
    sums_ref[1] = peep_sum

    @pl.when(step == last)
    def _():
        for c in range(chunks):
            dk, dz = c // low, c % low
            out_ref[dk, dz ^ zlo] = jnp.dot(
                back_order_ref[...], kept_out_ref[c].astype(BF16), preferred_element_type=F32
            ).astype(BF16)
        runs = []
        for dk in range(2):
            acc = jnp.zeros((1, channels), F32)
            for zl in reversed(range(low)):
                c = dk * low + (zl ^ zlo)
                for j in reversed(range(SUB)):
                    acc = binj_ref[c, j : j + 1, :] + map_ref[c, 0, j : j + 1, :] * acc
            runs.append(acc)
        runb_ref[...] = jnp.concatenate(runs + [jnp.zeros((6, channels), F32)], axis=0)


def back_kernel(
    info, low, planes, seg,
    s, gathered_ref, back_ref, map_ref, binj_ref, mixed_ref, prev_ref, direct_ref, rz_ref, fp_ref, rp_ref, fb_ref,
    grads_ref, sums_ref,
    carry_ref,
):
    chunks, channels = map_ref.shape[0], map_ref.shape[3]
    step = pl.program_id(0)
    count = pl.num_programs(0)
    k, zlo = s[info.K], s[info.ZLO]

    @pl.when(step == 0)
    def _():
        carry = jnp.zeros((1, channels), F32)
        own = [carry, carry]
        for plane in reversed(range(planes)):
            for core in (1, 0):
                for zh in (1, 0):
                    e = (zh ^ s[info.ZHI]) * planes + (plane ^ s[info.P])
                    mine = (plane == s[info.P]) & (zh == s[info.ZHI])
                    own[core] = jnp.where(mine, carry, own[core])
                    decay = jnp.where(k == core, gathered_ref[e, 0:1, :], gathered_ref[e, 2:3, :])
                    inject = jnp.where(k == core, back_ref[e, 0:1, :], back_ref[e, 1:2, :])
                    carry = decay * carry + inject
        for dk in range(2):
            carry = jnp.where(k == 0, own[dk], own[1 - dk])
            for zl in reversed(range(low)):
                c = dk * low + (zl ^ zlo)
                for j in reversed(range(SUB)):
                    carry_ref[c, j : j + 1, :] = carry
                    carry = map_ref[c, 0, j : j + 1, :] * carry + binj_ref[c, j : j + 1, :]
        sums_ref[...] = jnp.zeros_like(sums_ref)

    rows = prev_ref.shape[1]
    steps = rows // SUB
    bounds = info.bounds(s)
    fp, rp, fb = fp_ref[...], rp_ref[...], fb_ref[...]
    fz_sum, peep_sum = sums_ref[0], sums_ref[1]
    for c in range(chunks):
        base = info.base(s, c)
        back = carry_ref[c]
        for i in reversed(range(steps)):
            at = slice(i * SUB, (i + 1) * SUB)
            candidate = mixed_ref[c, 0, at].astype(F32)
            forget, rest = gate(mixed_ref[c, 1, at].astype(F32) + fp * candidate + fb)
            kept = kept_of(base, (count - 1 - step) * steps + i, seg, bounds, channels)
            cell_grad = direct_ref[c, at] + back
            back = kept * (forget * cell_grad + rz_ref[c, at] * rp)
            held = cell_grad * rest
            forget_z = held * forget * (prev_ref[c, at] - candidate)
            grads_ref[c, 0, at] = (held + forget_z * fp).astype(BF16)
            grads_ref[c, 1, at] = forget_z.astype(BF16)
            fz_sum = fz_sum + forget_z
            peep_sum = peep_sum + forget_z * candidate
        carry_ref[c] = back
    sums_ref[0] = fz_sum
    sums_ref[1] = peep_sum


def input_kernel(info, groups, joined, s, grads_ref, rzb_ref, w_ref, gain_ref, x_ref, stat_ref, skip_ref, *refs):
    v_ref, s_ref, gb_ref = refs[1:] if joined else refs
    channels = rzb_ref.shape[2]
    nt = (((1,), (1,)), ((), ()))
    grad = lax.dot_general(grads_ref[0, 0], w_ref[0], nt, preferred_element_type=F32)
    grad = grad + lax.dot_general(grads_ref[0, 1], w_ref[1], nt, preferred_element_type=F32)
    grad = grad + lax.dot_general(rzb_ref[0], w_ref[2], nt, preferred_element_type=F32)
    average = stat_ref[0][:, 0:1]
    inv = stat_ref[0][:, 1:2]
    hat = (x_ref[...].astype(F32) - average) * inv
    scaled = grad * gain_ref[...]
    first = jnp.sum(scaled, axis=1, keepdims=True)
    second = jnp.sum(scaled * hat, axis=1, keepdims=True)
    rows = grad.shape[0]
    lane = lax.broadcasted_iota(jnp.int32, (rows, LANES), 1)
    s_ref[...] = jnp.where(lane == 0, first, jnp.where(lane == 1, second, 0.0)).T[:SUB]

    @pl.when(pl.program_id(0) == 0)
    def _():
        gb_ref[...] = jnp.zeros_like(gb_ref)

    width = grad.shape[1]
    gb_ref[0] += jnp.sum((grad * hat).reshape(rows // SUB, SUB, width), axis=0)
    gb_ref[1] += jnp.sum(grad.reshape(rows // SUB, SUB, width), axis=0)
    skip = skip_ref[0].astype(F32)
    value = scaled * inv
    for group in range(groups):
        at = slice(group * channels, (group + 1) * channels)
        part = value[:, at] + skip * jnp.where(s[info.G] == group, 1.0, 0.0)
        if joined:
            part = part + refs[0][:, at].astype(F32)
        v_ref[:, at] = part.astype(BF16)


def last_kernel(x_ref, order_ref, own_ref, far_ref, s_ref, s_far_ref, out_ref):
    width = x_ref.shape[1]
    x = x_ref[...].astype(F32)
    average = jnp.mean(x, axis=1, keepdims=True)
    centred = x - average
    inv = lax.rsqrt(jnp.mean(centred * centred, axis=1, keepdims=True) + EPSILON)
    order = order_ref[...]
    value = jnp.dot(order, own_ref[...], preferred_element_type=F32)
    value = value + jnp.dot(order, far_ref[...], preferred_element_type=F32)
    sums = lax.dot_general(
        order.astype(F32), s_ref[...] + s_far_ref[...], (((1,), (1,)), ((), ())),
        precision=lax.Precision.HIGHEST, preferred_element_type=F32,
    )
    first = sums[:, 0:1] * (1.0 / width)
    second = sums[:, 1:2] * (1.0 / width)
    out_ref[...] = value - inv * (first + centred * inv * second)


def weight_grad_kernel(streams, s, normed_ref, grads_ref, out_ref):
    chunks = normed_ref.shape[0]
    channels = grads_ref.shape[-1]
    tn = (((0,), (0,)), ((), ()))
    for stream in range(streams):
        total = None
        for c in range(chunks):
            grads = grads_ref[c, stream] if len(grads_ref.shape) == 4 else grads_ref[c]
            part = lax.dot_general(normed_ref[c], grads, tn, preferred_element_type=F32)
            total = part if total is None else total + part
        out_ref[0, :, stream * channels : (stream + 1) * channels] = total.astype(BF16)


def place_kernel(s, first_ref, second_ref, out_ref):
    half = first_ref.shape[2]
    out_ref[0, :half] = first_ref[0, 0]
    out_ref[0, half:] = second_ref[0, 0]


def spread_kernel(info, s, a0_ref, b0_ref, a1_ref, b1_ref, out_ref):
    quarter, channels = a0_ref.shape[2], a0_ref.shape[3]
    k = s[info.K]
    for core, refs in ((k, (a0_ref, b0_ref)), (1 - k, (a1_ref, b1_ref))):
        for half in range(2):
            rows = pl.ds(pl.multiple_of(core * (2 * quarter) + half * quarter, quarter), quarter)
            for block in range(3):
                out_ref[rows, block * channels : (block + 1) * channels] = refs[half][0, block].astype(F32)


def cost(flops, moved, exps=0):
    return pl.CostEstimate(flops=int(flops), bytes_accessed=int(moved), transcendentals=int(exps))


def per_device(
    inputs, norm_gain, norm_bias, weight, forget_peep, reset_peep, forget_bias, reset_bias, seq_lengths, out_grad
):
    rows, width = inputs.shape
    seqs, groups = lax.axis_size("seq"), lax.axis_size("col")
    planes, low = seqs // 2, groups // 2
    channels = width // groups
    chunks = groups
    seg = rows // SUB
    part = width // planes
    seq, z = lax.axis_index("seq"), lax.axis_index("col")
    p, k, zhi, zlo = seq // 2, seq % 2, z // low, z % low
    g = zlo + low * k
    info = Info(chunks, seq_lengths.shape[0])
    params = functools.partial(pltpu.CompilerParams, vmem_limit_bytes=VMEM_LIMIT)

    def move(value, to):
        pairs = []
        for a in range(seqs):
            for b in range(groups):
                target = to(a // 2, a % 2, b)
                if target is not None:
                    pairs.append((a * groups + b, (target[0] * 2 + target[1]) * groups + target[2]))
        return lax.ppermute(value, ("seq", "col"), pairs)

    def cross_core(value):
        return move(value, lambda p, k, z: (p, 1 - k, z))

    def cross_low(value, dz):
        return move(value, lambda p, k, z: (p, k, z ^ dz))

    def cross_high(value):
        return move(value, lambda p, k, z: (p, k, (z + low) % groups))

    def cross_plane(value, dp):
        return move(value, lambda p, k, z: (p ^ dp, k, z))

    def gather_maps(value):
        gathered = value[None]
        for bit in bits_of(planes):
            gathered = jnp.concatenate([gathered, cross_plane(gathered, bit)], axis=0)
        return jnp.concatenate([gathered, cross_high(gathered)], axis=0)

    bases = [((2 * p + (k ^ (c // low))) * groups + zhi * low + (zlo ^ (c % low))) * rows for c in range(chunks)]
    bounds = jnp.cumsum(seq_lengths) - seq_lengths
    scalars = jnp.concatenate([jnp.stack([p, k, zhi, zlo, g] + bases).astype(jnp.int32), bounds.astype(jnp.int32)])

    order = jnp.asarray(row_order(rows), BF16)
    back_order = jnp.asarray(row_order(rows).T.copy(), BF16)

    plans, rounds = routes(groups)
    send_at = np.zeros((rounds, 2, groups), np.int32)
    send_stream = np.zeros((rounds, 2, groups), np.int32)
    sent = np.zeros((rounds, 2, groups), np.bool_)
    chosen = np.zeros((3, 2, groups), np.int32)
    local_at = np.zeros((3, 2, groups), np.int32)
    for core, (local, plan) in enumerate(plans):
        for src, dst, stream, at in local:
            local_at[stream, core, dst] = at
        for r, edges in enumerate(plan):
            for src, dst, stream, at in edges:
                send_at[r, core, src] = at
                sent[r, core, src] = True
                send_stream[r, core, dst] = stream
                chosen[stream, core, dst] = 1 + r

    def look(table):
        return jnp.asarray(table.reshape(table.shape[0], -1))[:, k * groups + z]

    here_send_at, here_send_stream, here_sent = look(send_at), look(send_stream), look(sent)
    here_chosen, here_local = look(chosen), look(local_at)

    def round_to(r):
        targets = {}
        for core, (_, plan) in enumerate(plans):
            for src, dst, _, _ in plan[r]:
                targets[(core, src)] = dst
        return targets

    my_part = lax.dynamic_slice_in_dim(weight, p * part, part, 0)

    def own_block(at):
        return lax.dynamic_slice_in_dim(my_part, at * channels, channels, 1)

    arrived = []
    for r in range(rounds):
        targets = round_to(r)
        arrived.append(
            move(own_block(here_send_at[r]), lambda p, k, z: (p, k, targets[(k, z)]) if (k, z) in targets else None)
        )
    streams = []
    for stream in range(3):
        block = own_block(here_local[stream])
        for r in range(rounds):
            block = jnp.where(here_chosen[stream] == 1 + r, arrived[r], block)
        streams.append(block)
    own_weight = jnp.stack(streams)

    def gather_plane(value, bits):
        held, names = value[None], [0]
        for bit in bits:
            held = jnp.concatenate([held, cross_plane(held, bit)], axis=0)
            names = names + [n ^ bit for n in names]
        return held, names

    bits = bits_of(planes)

    def gather_halves(value):
        half = value.shape[1] // 2
        first, first_names = gather_plane(value[:, :half], bits)
        second, second_names = gather_plane(value[:, half:], bits[::-1])
        spots = np.array([second_names.index(n) for n in first_names], np.int32)
        return first, second, spots, first_names

    first, second, spots, names = gather_halves(own_weight)
    assert names == list(range(planes))
    spot_scalars = jnp.concatenate([scalars, jnp.asarray(spots)])
    spot_at = info.BASE + chunks + info.sequences
    full_weight = pl.pallas_call(
        place_kernel,
        grid_spec=pltpu.PrefetchScalarGridSpec(
            num_scalar_prefetch=1,
            grid=(planes, 3),
            in_specs=[
                pl.BlockSpec((1, 1, part // 2, channels), lambda d, j, s: (d, j, 0, 0)),
                pl.BlockSpec((1, 1, part // 2, channels), lambda d, j, s: (s[spot_at + d], j, 0, 0)),
            ],
            out_specs=pl.BlockSpec((1, part, channels), lambda d, j, s: (j, d ^ s[info.P], 0)),
        ),
        out_shape=jax.ShapeDtypeStruct((3, width, channels), BF16),
        compiler_params=params(),
        cost_estimate=cost(0, 12 * width * channels),
        name="place_weight",
    )(spot_scalars, first, second)

    permuted = jnp.dot(order, inputs, preferred_element_type=F32).astype(BF16)
    xs = [permuted] + [cross_low(permuted, dz) for dz in range(1, low)]
    xs = xs + [cross_core(value) for value in xs]

    gain2, bias2 = norm_gain[None, :], norm_bias[None, :]
    fp2, rp2, fb2, rb2 = forget_peep, reset_peep, forget_bias, reset_bias
    gates = jnp.stack([forget_peep, reset_peep, forget_bias, reset_bias])

    def to_group(value):
        other = cross_high(value)
        keep = jnp.where(zhi == k, value, other)
        give = jnp.where(zhi == k, other, value)
        return keep, give

    keep, _ = to_group(gates)
    fp2, rp2, fb2, rb2 = (keep[n : n + 1] for n in range(4))

    tile = 128 if rows % 128 == 0 else rows
    tiles = rows // tile
    full = lambda shape: pl.BlockSpec(shape, lambda *_: (0,) * len(shape))
    shapes = (
        jax.ShapeDtypeStruct((chunks, rows, width), BF16),
        jax.ShapeDtypeStruct((chunks, 3, rows, channels), BF16),
        jax.ShapeDtypeStruct((chunks, rows, channels), BF16),
        jax.ShapeDtypeStruct((chunks, rows, LANES), F32),
        jax.ShapeDtypeStruct((chunks, 2, SUB, channels), F32),
    )
    held = ()
    for c in [dk * low + dz for dz in range(low) for dk in range(2)]:
        first_call = not held
        held = pl.pallas_call(
            functools.partial(forward_kernel, info, c, seg, first_call),
            grid_spec=pltpu.PrefetchScalarGridSpec(
                num_scalar_prefetch=1,
                grid=(tiles,),
                in_specs=[
                    pl.BlockSpec((tile, width), lambda t, s: (t, 0)),
                    full((1, width)),
                    full((1, width)),
                    full((3, width, channels)),
                    full((1, channels)),
                    full((1, channels)),
                ]
                + [pl.BlockSpec(memory_space=pl.ANY)] * len(held),
                out_specs=[
                    pl.BlockSpec((1, tile, width), lambda t, s, c=c: (c, t, 0)),
                    pl.BlockSpec((1, 3, tile, channels), lambda t, s, c=c: (c, 0, t, 0)),
                    pl.BlockSpec((1, tile, channels), lambda t, s, c=c: (c, t, 0)),
                    pl.BlockSpec((1, tile, LANES), lambda t, s, c=c: (c, t, 0)),
                    pl.BlockSpec((1, 2, SUB, channels), lambda t, s, c=c: (c, 0, 0, 0)),
                ],
            ),
            out_shape=shapes,
            input_output_aliases={7 + n: n for n in range(len(held))},
            compiler_params=params(),
            cost_estimate=cost(6 * rows * width * channels, 8 * rows * width + 6 * width * channels),
            name="forward_chunk",
        )(scalars, xs[c], gain2, bias2, full_weight, fp2, fb2, *held)
    normed, mixed, highway, stats, maps = held

    run_maps = pl.pallas_call(
        functools.partial(run_map_kernel, info, low),
        grid_spec=pltpu.PrefetchScalarGridSpec(
            num_scalar_prefetch=1,
            grid=(1,),
            in_specs=[full((chunks, 2, SUB, channels))],
            out_specs=full((SUB, channels)),
        ),
        out_shape=jax.ShapeDtypeStruct((SUB, channels), F32),
        compiler_params=params(),
        name="run_maps",
    )(scalars, maps)
    gathered = gather_maps(run_maps)

    half_rows = low * rows
    own_half = lax.dynamic_slice_in_dim(out_grad, zhi * half_rows, half_rows, 0)
    far_half = cross_high(lax.dynamic_slice_in_dim(out_grad, (1 - zhi) * half_rows, half_rows, 0))
    keep = jnp.where(zhi == k, own_half, far_half)
    give = jnp.where(zhi == k, far_half, own_half)
    cotangent = jnp.stack([keep, cross_core(give)]).reshape(2, low, rows, channels)

    block = 64
    blocks = rows // block
    elements = chunks * rows * channels
    at_block = lambda t, s: (0, t, 0)
    state_out = pl.pallas_call(
        functools.partial(state_kernel, info, low, planes, seg),
        grid_spec=pltpu.PrefetchScalarGridSpec(
            num_scalar_prefetch=1,
            grid=(blocks,),
            in_specs=[
                full((2 * planes, SUB, channels)),
                full((chunks, 2, SUB, channels)),
                pl.BlockSpec((chunks, 3, block, channels), lambda t, s: (0, 0, t, 0)),
                pl.BlockSpec((chunks, block, channels), at_block),
                full((2, low, rows, channels)),
                pl.BlockSpec((block, rows), lambda t, s: (t, 0)),
                full((rows, rows)),
                full((1, channels)),
                full((1, channels)),
                full((1, channels)),
                full((1, channels)),
            ],
            out_specs=[
                full((2, low, rows, channels)),
                pl.BlockSpec((chunks, block, channels), at_block),
                pl.BlockSpec((chunks, block, channels), at_block),
                pl.BlockSpec((chunks, block, channels), at_block),
                pl.BlockSpec((chunks, block, channels), at_block),
                pl.BlockSpec((chunks, block, channels), at_block),
                full((chunks, SUB, channels)),
                full((2, SUB, channels)),
                full((SUB, channels)),
            ],
            scratch_shapes=[
                pltpu.VMEM((chunks, SUB, channels), F32),
                pltpu.VMEM((chunks, SUB, channels), F32),
                pltpu.VMEM((chunks, rows, channels), F32),
            ],
        ),
        out_shape=(
            jax.ShapeDtypeStruct((2, low, rows, channels), BF16),
            jax.ShapeDtypeStruct((chunks, rows, channels), F32),
            jax.ShapeDtypeStruct((chunks, rows, channels), F32),
            jax.ShapeDtypeStruct((chunks, rows, channels), F32),
            jax.ShapeDtypeStruct((chunks, rows, channels), BF16),
            jax.ShapeDtypeStruct((chunks, rows, channels), BF16),
            jax.ShapeDtypeStruct((chunks, SUB, channels), F32),
            jax.ShapeDtypeStruct((2, SUB, channels), F32),
            jax.ShapeDtypeStruct((SUB, channels), F32),
        ),
        compiler_params=params(),
        cost_estimate=cost(60 * elements, 30 * elements, 4 * elements),
        name="states",
    )(scalars, gathered, maps, mixed, highway, cotangent, order, back_order, fp2, rp2, fb2, rb2)
    out_group, previous, direct, reset_z, reset_zb, skip, binj, reset_sums, run_back = state_out

    gathered_back = gather_maps(run_back)

    grads, forget_sums = pl.pallas_call(
        functools.partial(back_kernel, info, low, planes, seg),
        grid_spec=pltpu.PrefetchScalarGridSpec(
            num_scalar_prefetch=1,
            grid=(blocks,),
            in_specs=[
                full((2 * planes, SUB, channels)),
                full((2 * planes, SUB, channels)),
                full((chunks, 2, SUB, channels)),
                full((chunks, SUB, channels)),
                pl.BlockSpec((chunks, 2, block, channels), lambda t, s: (0, 0, blocks - 1 - t, 0)),
                pl.BlockSpec((chunks, block, channels), lambda t, s: (0, blocks - 1 - t, 0)),
                pl.BlockSpec((chunks, block, channels), lambda t, s: (0, blocks - 1 - t, 0)),
                pl.BlockSpec((chunks, block, channels), lambda t, s: (0, blocks - 1 - t, 0)),
                full((1, channels)),
                full((1, channels)),
                full((1, channels)),
            ],
            out_specs=[
                pl.BlockSpec((chunks, 2, block, channels), lambda t, s: (0, 0, blocks - 1 - t, 0)),
                full((2, SUB, channels)),
            ],
            scratch_shapes=[pltpu.VMEM((chunks, SUB, channels), F32)],
        ),
        out_shape=(
            jax.ShapeDtypeStruct((chunks, 2, rows, channels), BF16),
            jax.ShapeDtypeStruct((2, SUB, channels), F32),
        ),
        compiler_params=params(),
        cost_estimate=cost(30 * elements, 20 * elements, 2 * elements),
        name="state_grads",
    )(scalars, gathered, gathered_back, maps, binj, mixed, previous, direct, reset_z, fp2, rp2, fb2)

    got = cross_core(out_group[1])
    stay = jnp.where(k == zhi, out_group[0], got)
    leave = jnp.where(k == zhi, got, out_group[0])
    came = cross_high(leave)
    output = jnp.where(zhi == 0, jnp.stack([stay, came]), jnp.stack([came, stay])).reshape(groups * rows, channels)

    def chunk_grad(c, joined):
        extra = [pl.BlockSpec((tile, width), lambda t, s: (t, 0))] if joined is not None else []
        return pl.pallas_call(
            functools.partial(input_kernel, info, groups, joined is not None),
            grid_spec=pltpu.PrefetchScalarGridSpec(
                num_scalar_prefetch=1,
                grid=(tiles,),
                in_specs=[
                    pl.BlockSpec((1, 2, tile, channels), lambda t, s, c=c: (c, 0, t, 0)),
                    pl.BlockSpec((1, tile, channels), lambda t, s, c=c: (c, t, 0)),
                    full((3, width, channels)),
                    full((1, width)),
                    pl.BlockSpec((tile, width), lambda t, s: (t, 0)),
                    pl.BlockSpec((1, tile, LANES), lambda t, s, c=c: (c, t, 0)),
                    pl.BlockSpec((1, tile, channels), lambda t, s, c=c: (c, t, 0)),
                ]
                + extra,
                out_specs=[
                    pl.BlockSpec((tile, width), lambda t, s: (t, 0)),
                    pl.BlockSpec((SUB, tile), lambda t, s: (0, t)),
                    full((2, SUB, width)),
                ],
            ),
            out_shape=(
                jax.ShapeDtypeStruct((rows, width), BF16),
                jax.ShapeDtypeStruct((SUB, rows), F32),
                jax.ShapeDtypeStruct((2, SUB, width), F32),
            ),
            compiler_params=params(),
            cost_estimate=cost(6 * rows * width * channels, 8 * rows * width + 6 * width * channels),
            name="chunk_grad",
        )(scalars, grads, reset_zb, full_weight, gain2, xs[c], stats, skip, *([joined] if joined is not None else []))

    norm_sums = []
    far, far_sums = [], []
    for dz in list(range(1, low)) + [0]:
        value, sums, gb = chunk_grad(low + dz, None)
        norm_sums.append(gb)
        from_core, sums_core = cross_core(value), cross_core(sums)
        value, sums, gb = chunk_grad(dz, from_core)
        norm_sums.append(gb)
        sums = sums + sums_core
        if dz:
            far.append(cross_low(value, dz))
            far_sums.append(cross_low(sums, dz))
    far_value = far[0]
    far_sum = far_sums[0]
    for n in range(1, len(far)):
        far_value = (far_value.astype(F32) + far[n].astype(F32)).astype(BF16)
        far_sum = far_sum + far_sums[n]
    input_grad = pl.pallas_call(
        last_kernel,
        grid=(tiles,),
        in_specs=[
            pl.BlockSpec((tile, width), lambda t: (t, 0)),
            pl.BlockSpec((tile, rows), lambda t: (t, 0)),
            full((rows, width)),
            full((rows, width)),
            full((SUB, rows)),
            full((SUB, rows)),
        ],
        out_specs=pl.BlockSpec((tile, width), lambda t: (t, 0)),
        out_shape=jax.ShapeDtypeStruct((rows, width), F32),
        compiler_params=params(),
        cost_estimate=cost(4 * rows * rows * width, 10 * rows * width),
        name="input_grad",
    )(inputs, back_order, value, far_value, sums, far_sum)

    def weight_part(source, count, name):
        spec = (chunks, count, rows, channels) if count > 1 else (chunks, rows, channels)
        return pl.pallas_call(
            functools.partial(weight_grad_kernel, count),
            grid_spec=pltpu.PrefetchScalarGridSpec(
                num_scalar_prefetch=1,
                grid=(planes,),
                in_specs=[
                    pl.BlockSpec(
                        (chunks, rows, part), lambda t, s: (0, 0, (planes - 1 - t) ^ s[info.P])
                    ),
                    full(spec),
                ],
                out_specs=pl.BlockSpec((1, part, count * channels), lambda t, s: (planes - 1 - t, 0, 0)),
            ),
            out_shape=jax.ShapeDtypeStruct((planes, part, count * channels), BF16),
            compiler_params=params(),
            cost_estimate=cost(2 * chunks * rows * width * count * channels, 6 * chunks * rows * width),
            name=name,
        )(scalars, normed, source)

    def add(a, b):
        return (a.astype(F32) + b.astype(F32)).astype(BF16)

    def reduce_plane(values, order_bits):
        held = dict(enumerate(values))
        for bit in order_bits:
            away = [d for d in held if d & bit]
            came = cross_plane(jnp.stack([held[d] for d in away]), bit)
            held = {d: add(held[d], came[away.index(d | bit)]) for d in held if not d & bit}
        return held[0]

    def reduce_halves(value):
        half = part // 2
        first = reduce_plane([value[d, :half] for d in range(planes)], bits)
        second = reduce_plane([value[d, half:] for d in range(planes)], bits[::-1])
        return jnp.concatenate([first, second], axis=0)

    reset_part = reduce_halves(weight_part(reset_zb, 1, "weight_grad_reset"))
    main_part = reduce_halves(weight_part(grads, 2, "weight_grad_main"))
    stream_parts = jnp.stack([main_part[:, :channels], main_part[:, channels:], reset_part])

    blocks_sum = [jnp.zeros((part, channels), F32) for _ in range(3)]
    for r in range(rounds):
        targets = round_to(r)
        back = {(core, dst): src for (core, src), dst in targets.items()}
        came = move(
            lax.dynamic_index_in_dim(stream_parts, here_send_stream[r], 0, keepdims=False),
            lambda p, k, z: (p, k, back[(k, z)]) if (k, z) in back else None,
        )
        for at in range(3):
            blocks_sum[at] = blocks_sum[at] + jnp.where(
                here_sent[r] & (here_send_at[r] == at), came.astype(F32), 0.0
            )
    for stream in range(3):
        is_local = here_chosen[stream] == 0
        for at in range(3):
            blocks_sum[at] = blocks_sum[at] + jnp.where(
                is_local & (here_local[stream] == at), stream_parts[stream].astype(F32), 0.0
            )
    owned = jnp.stack(blocks_sum)
    owned_low = owned.astype(BF16)
    from_core = cross_core(lax.dynamic_slice_in_dim(owned_low, (1 - k) * (part // 2), part // 2, 1))
    mine = add(lax.dynamic_slice_in_dim(owned, k * (part // 2), part // 2, 1), from_core)
    first, second, spots, names = gather_halves(mine)
    first_other, second_other = cross_core(first), cross_core(second)
    spot_scalars = jnp.concatenate([scalars, jnp.asarray(spots)])
    quarter = part // 4
    piece = (1, 3, quarter, channels)
    weight_grad = pl.pallas_call(
        functools.partial(spread_kernel, info),
        grid_spec=pltpu.PrefetchScalarGridSpec(
            num_scalar_prefetch=1,
            grid=(planes,),
            in_specs=[
                pl.BlockSpec(piece, lambda d, s: (d, 0, 0, 0)),
                pl.BlockSpec(piece, lambda d, s: (s[spot_at + d], 0, 0, 0)),
                pl.BlockSpec(piece, lambda d, s: (d, 0, 0, 0)),
                pl.BlockSpec(piece, lambda d, s: (s[spot_at + d], 0, 0, 0)),
            ],
            out_specs=pl.BlockSpec((part, 3 * channels), lambda d, s: (d ^ s[info.P], 0)),
        ),
        out_shape=jax.ShapeDtypeStruct((width, 3 * channels), F32),
        compiler_params=params(),
        cost_estimate=cost(0, 18 * width * channels),
        name="spread_weight_grad",
    )(spot_scalars, first, second, first_other, second_other)

    gate_sums = jnp.sum(jnp.concatenate([forget_sums, reset_sums]), axis=1)
    spread = lax.dynamic_update_slice(jnp.zeros((4, width), F32), gate_sums, (0, g * channels))
    norm_total = norm_sums[0]
    for value in norm_sums[1:]:
        norm_total = norm_total + value
    small = jnp.concatenate([jnp.sum(norm_total, axis=1), spread], axis=0)
    small = small + cross_core(small)
    for bit in bits:
        small = small + cross_plane(small, bit)
    for bit in bits_of(groups):
        small = small + cross_low(small, bit)
    gate_block = lax.dynamic_slice_in_dim(small[2:], z * channels, channels, 1)
    return (
        output,
        input_grad,
        weight_grad,
        small[0],
        small[1],
        gate_block[1],
        gate_block[3],
        gate_block[0],
        gate_block[2],
    )


def solution(mesh):
    placed = (
        P(("seq", "col"), None),
        P(),
        P(),
        P(None, "col"),
        P("col"),
        P("col"),
        P("col"),
        P("col"),
        P(),
        P("seq", "col"),
    )
    return jax.shard_map(
        per_device,
        mesh=mesh,
        in_specs=placed,
        out_specs=(
            P("seq", "col"),
            P(("seq", "col"), None),
            P(None, "col"),
            P(),
            P(),
            P("col"),
            P("col"),
            P("col"),
            P("col"),
        ),
        check_vma=False,
    )
```

```python
import functools

import jax
import jax.numpy as jnp
import numpy as np
from jax import lax
from jax.experimental import pallas as pl
from jax.experimental.pallas import tpu as pltpu
from jax.sharding import PartitionSpec as P

EPSILON = 1e-05
F32 = jnp.float32
BF16 = jnp.bfloat16
LANES = 128
SUB = 8
VMEM_LIMIT = 56 * 1024 * 1024


def bits_of(count):
    return [1 << b for b in range(count.bit_length() - 1)]


def colour(edges, count):
    degree = max([sum(e[0] == n for e in edges) for n in range(count)] + [sum(e[1] == n for e in edges) for n in range(count)])
    out = [[None] * degree for _ in range(count)]
    into = [[None] * degree for _ in range(count)]
    taken = {}
    for at, edge in enumerate(edges):
        src, dst = edge[0], edge[1]
        first = next(c for c in range(degree) if out[src][c] is None)
        second = next(c for c in range(degree) if into[dst][c] is None)
        if first != second:
            path, node, at_dst, look = [], dst, True, first
            while True:
                found = (into if at_dst else out)[node][look]
                if found is None:
                    break
                path.append(found)
                node = edges[found][0] if at_dst else edges[found][1]
                at_dst = not at_dst
                look = second if look == first else first
            for found in path:
                old = taken[found]
                out[edges[found][0]][old] = None
                into[edges[found][1]][old] = None
            for found in path:
                new = second if taken[found] == first else first
                taken[found] = new
                out[edges[found][0]][new] = found
                into[edges[found][1]][new] = found
        taken[at] = first
        out[src][first] = at
        into[dst][first] = at
    rounds = [[] for _ in range(degree)]
    for at, edge in enumerate(edges):
        rounds[taken[at]].append(edge)
    return rounds


def routes(groups, streams):
    low = groups // 2
    plans = []
    for core in range(2):
        local, edges = [], []
        for dst in range(groups):
            for stream in streams:
                block = stream * groups + dst % low + low * core
                src, at = block // 3, block % 3
                (local if src == dst else edges).append((src, dst, stream, at))
        plans.append((local, colour(edges, groups)))
    count = max(len(rounds) for _, rounds in plans)
    return [(local, rounds + [[]] * (count - len(rounds))) for local, rounds in plans], count


def row_order(rows):
    seg = rows // SUB
    matrix = np.zeros((rows, rows), np.float32)
    for i in range(seg):
        for j in range(SUB):
            matrix[i * SUB + j, j * seg + i] = 1.0
    return matrix


def gate(value):
    small = jnp.exp(-jnp.abs(value))
    minor = small / (1.0 + small)
    major = 1.0 - minor
    up = value >= 0.0
    return jnp.where(up, major, minor), jnp.where(up, minor, major)


def kept_of(base, step, seg, bounds, channels):
    at = lax.broadcasted_iota(jnp.int32, (SUB, LANES), 0) * seg + (base + step)
    starts = at == bounds[0]
    for bound in bounds[1:]:
        starts = starts | (at == bound)
    kept = jnp.where(starts, 0.0, 1.0)
    return jnp.concatenate([kept] * (channels // LANES), axis=1)


class Info:
    def __init__(self):
        self.spots = {}
        self.columns = []

    def put(self, name, values):
        self.spots[name] = len(self.columns)
        self.columns += list(np.asarray(values, np.int32))

    def __getattr__(self, name):
        return self.spots[name]

    def table(self):
        return np.stack(self.columns, axis=1)


def bounds_of(lengths):
    starts = [0]
    for n in range(lengths.shape[0] - 1):
        starts.append(starts[-1] + lengths[n])
    return starts


def cut_kernel(count, copies, s, block_ref, *out_refs):
    part = block_ref.shape[0]
    for n in range(count):

        @pl.when(pl.program_id(0) == n)
        def _():
            for copy in range(copies):
                out_refs[n][copy * part : (copy + 1) * part] = block_ref[...]


def pick_kernel(name, info, sources, s, *refs):
    came, outs = refs[:sources], refs[sources:]
    outs = list(outs) if len(outs) > 1 else [outs[0].at[n] for n in range(outs[0].shape[0])]
    for n, out in enumerate(outs):
        for r in range(sources):

            @pl.when(s[getattr(info, name) + n] == r)
            def _():
                out[...] = came[r][...]


def norm_rows(x_ref, gain, bias, normed_ref, hat_ref, inv_ref):
    block = 32
    for r in range(x_ref.shape[0] // block):
        at = slice(r * block, (r + 1) * block)
        x = x_ref[at].astype(F32)
        average = jnp.mean(x, axis=1, keepdims=True)
        centred = x - average
        inv = lax.rsqrt(jnp.mean(centred * centred, axis=1, keepdims=True) + EPSILON)
        hat = centred * inv
        normed_ref[0, at] = (hat * gain + bias).astype(BF16)
        hat_ref[0, at] = hat.astype(BF16)
        inv_ref[0, at] = jnp.broadcast_to(inv, (block, LANES))


def group_columns(info, s, channels):
    return pl.ds(pl.multiple_of(s[info.g] * channels, channels), channels)


def norm_kernel(info, s, x_ref, gain_ref, bias_ref, *refs):
    normed_ref, hx_ref, hat_ref, inv_ref = refs[-4:]
    norm_rows(x_ref, gain_ref[...], bias_ref[...], normed_ref, hat_ref, inv_ref)
    hx_ref[0] = x_ref[:, group_columns(info, s, hx_ref.shape[2])]


def segment_maps(base, seg, lengths, mixed_ref, fp, fb):
    channels = mixed_ref.shape[3]
    run_decay = jnp.ones((SUB, channels), F32)
    run_state = jnp.zeros((SUB, channels), F32)
    bounds = bounds_of(lengths)
    for i in range(mixed_ref.shape[2] // SUB):
        at = slice(i * SUB, (i + 1) * SUB)
        candidate = mixed_ref[0, 0, at].astype(F32)
        forget, rest = gate(mixed_ref[0, 1, at].astype(F32) + fp * candidate + fb)
        decay = forget * kept_of(base, i, seg, bounds, channels)
        run_state = decay * run_state + rest * candidate
        run_decay = decay * run_decay
    return run_decay, run_state


def mix_kernel(info, low, planes, seg, here, away, split, s, lengths, normed_ref, fp_ref, fb_ref, *refs):
    count = here + (planes + 1 if split else planes)
    pieces = refs[:count]
    mixed_ref, map_ref, full_ref, w_ref, in_sem, out_sem = refs[count:]
    part = w_ref.shape[1] // planes
    parts = [(d, 0, part) for d in range(planes)]
    if split:
        parts = parts[:3] + [(3, 0, part // 2), (3, part // 2, part // 2)]
    step = pl.program_id(0)

    def copies(slot):
        stream = s[info.slot_stream + slot]
        if slot < here:
            return [pltpu.make_async_copy(pieces[slot], w_ref.at[stream], in_sem.at[slot])]
        found = []
        for n, (d, start, size) in enumerate(parts):
            rows = pl.ds(pl.multiple_of((d ^ s[info.p]) * part + start, size), size)
            piece = pieces[here + n].at[slot - here]
            spot = here + (slot - here) * len(parts) + n
            found.append(pltpu.make_async_copy(piece, w_ref.at[stream, rows, :], in_sem.at[spot]))
        return found

    @pl.when(step == 0)
    def _():
        for slot in range(here + away):

            @pl.when(s[info.slot_stream + slot] >= 0)
            def _():
                for copy in copies(slot):
                    copy.start()

        for slot in range(here + away):

            @pl.when(s[info.slot_stream + slot] >= 0)
            def _():
                for copy in copies(slot):
                    copy.wait()

        pltpu.make_async_copy(w_ref, full_ref, out_sem).start()

    for stream in range(3):
        mixed_ref[0, stream] = jnp.dot(normed_ref[0], w_ref[stream], preferred_element_type=F32).astype(BF16)
    decay, state = segment_maps(s[info.base + step * low], seg, lengths, mixed_ref, fp_ref[...], fb_ref[...])
    map_ref[0, 0] = decay
    map_ref[0, 1] = state

    @pl.when(step == pl.num_programs(0) - 1)
    def _():
        pltpu.make_async_copy(w_ref, full_ref, out_sem).wait()


def mix_far_kernel(info, low, seg, order, tile, s, lengths, w_ref, gain_ref, bias_ref, fp_ref, fb_ref, near_ref, *refs):
    count = len(order)
    pieces = refs[: 2 * count]
    normed_ref, hx_ref, hat_ref, inv_ref, mixed_ref, map_ref, run_ref, x_ref, sem = refs[2 * count + 5 :]
    channels = w_ref.shape[2]
    step = pl.program_id(0)

    def copies(n):
        return [
            pltpu.make_async_copy(pieces[2 * n], x_ref.at[n, pl.ds(0, tile), :], sem.at[2 * n]),
            pltpu.make_async_copy(pieces[2 * n + 1], x_ref.at[n, pl.ds(tile, x_ref.shape[1] - tile), :], sem.at[2 * n + 1]),
        ]

    @pl.when(step == 0)
    def _():
        for n in range(count):
            for copy in copies(n):
                copy.start()
        for dk in range(2):
            map_ref[dk * low] = near_ref[dk * low]

    for n in range(count):

        @pl.when(step == n)
        def _():
            for copy in copies(n):
                copy.wait()

    mine = x_ref.at[step]
    norm_rows(mine, gain_ref[...], bias_ref[...], normed_ref, hat_ref, inv_ref)
    hx_ref[0] = mine[:, group_columns(info, s, channels)]
    for stream in range(3):
        mixed_ref[0, stream] = jnp.dot(normed_ref[0], w_ref[stream], preferred_element_type=F32).astype(BF16)
    chunk = far_chunk(low, step)
    decay, state = segment_maps(s[info.base + chunk], seg, lengths, mixed_ref, fp_ref[...], fb_ref[...])
    map_ref[chunk, 0] = decay
    map_ref[chunk, 1] = state

    @pl.when(step == count - 1)
    def _():
        rows = []
        for dk in range(2):
            decay = jnp.ones((1, channels), F32)
            state = jnp.zeros((1, channels), F32)
            for zl in range(low):
                c = dk * low + (zl ^ s[info.zlo])
                for j in range(SUB):
                    d, b = map_ref[c, 0, j : j + 1, :], map_ref[c, 1, j : j + 1, :]
                    state = d * state + b
                    decay = d * decay
            rows += [decay, state]
        run_ref[...] = jnp.concatenate(rows + [jnp.zeros((4, channels), F32)], axis=0)


def far_chunk(low, n):
    return n // (low - 1) * low + 1 + n % (low - 1)


def gathered_maps(info, planes, s, refs, into):
    for d in range(planes):
        plane = d ^ s[info.p]
        into[s[info.zhi] * planes + plane] = refs[d][...]
        into[(1 - s[info.zhi]) * planes + plane] = refs[planes][d]


def state_kernel(info, low, planes, seg, s, lengths, *refs):
    gathered_refs = refs[: planes + 1]
    (
        map_ref, mixed_ref, hx_ref, og_ref, og_far_ref, order_ref, back_order_ref, fp_ref, rp_ref, fb_ref, rb_ref,
        out_ref, out_far_ref, prev_ref, direct_ref, rz_ref, rzb_ref, skip_ref, binj_ref, sums_ref, runb_ref,
        cell_ref, prod_ref, kept_out_ref, gathered_ref,
    ) = refs[planes + 1 :]
    chunks, channels = map_ref.shape[0], map_ref.shape[3]
    step = pl.program_id(0)
    last = pl.num_programs(0) - 1
    k, zlo = s[info.k], s[info.zlo]

    @pl.when(step == 0)
    def _():
        gathered_maps(info, planes, s, gathered_refs, gathered_ref)
        carry = jnp.zeros((1, channels), F32)
        own = [carry, carry]
        for plane in range(planes):
            for core in range(2):
                for zh in range(2):
                    e = zh * planes + plane
                    mine = (plane == s[info.p]) & (zh == s[info.zhi])
                    own[core] = jnp.where(mine, carry, own[core])
                    decay = jnp.where(k == core, gathered_ref[e, 0:1, :], gathered_ref[e, 2:3, :])
                    state = jnp.where(k == core, gathered_ref[e, 1:2, :], gathered_ref[e, 3:4, :])
                    carry = decay * carry + state
        for dk in range(2):
            carry = jnp.where(k == 0, own[dk], own[1 - dk])
            for zl in range(low):
                c = dk * low + (zl ^ zlo)
                for j in range(SUB):
                    cell_ref[c, j : j + 1, :] = carry
                    carry = map_ref[c, 0, j : j + 1, :] * carry + map_ref[c, 1, j : j + 1, :]
        prod_ref[...] = jnp.ones_like(prod_ref)
        binj_ref[...] = jnp.zeros_like(binj_ref)
        sums_ref[...] = jnp.zeros_like(sums_ref)

    rows = hx_ref.shape[1]
    steps = rows // SUB
    bounds = bounds_of(lengths)
    fp, rp, fb, rb = fp_ref[...], rp_ref[...], fb_ref[...], rb_ref[...]
    rz_sum, peep_sum = sums_ref[0], sums_ref[1]
    for c in range(chunks):
        dk, dz = c // low, c % low
        grad = jnp.dot(order_ref[...], (og_ref, og_far_ref)[dk][dz ^ zlo], preferred_element_type=F32)
        base = s[info.base + c]
        cell, prod, binj = cell_ref[c], prod_ref[c], binj_ref[c]
        for i in range(steps):
            at = slice(i * SUB, (i + 1) * SUB)
            candidate = mixed_ref[c, 0, at].astype(F32)
            forget, rest = gate(mixed_ref[c, 1, at].astype(F32) + fp * candidate + fb)
            kept = kept_of(base, step * steps + i, seg, bounds, channels)
            previous = kept * cell
            decay = forget * kept
            cell = forget * previous + rest * candidate
            reset, skip = gate(mixed_ref[c, 2, at].astype(F32) + rp * previous + rb)
            x = hx_ref[c, at].astype(F32)
            g = grad[at]
            kept_out_ref[c, pl.ds(pl.multiple_of(step * rows + i * SUB, SUB), SUB), :] = reset * cell + skip * x
            direct = g * reset
            g_skip = g * skip
            rz = direct * skip * (cell - x)
            prev_ref[c, at] = previous
            direct_ref[c, at] = direct
            rz_ref[c, at] = rz
            rzb_ref[c, at] = rz.astype(BF16)
            skip_ref[c, at] = g_skip.astype(BF16)
            binj = binj + prod * (decay * direct + kept * (rz * rp))
            prod = prod * decay
            rz_sum = rz_sum + rz
            peep_sum = peep_sum + rz * previous
        cell_ref[c] = cell
        prod_ref[c] = prod
        binj_ref[c] = binj
    sums_ref[0] = rz_sum
    sums_ref[1] = peep_sum

    @pl.when(step == last)
    def _():
        for c in range(chunks):
            dk, dz = c // low, c % low
            (out_ref, out_far_ref)[dk][dz ^ zlo] = jnp.dot(
                back_order_ref[...], kept_out_ref[c].astype(BF16), preferred_element_type=F32
            ).astype(BF16)
        runs = []
        for dk in range(2):
            acc = jnp.zeros((1, channels), F32)
            for zl in reversed(range(low)):
                c = dk * low + (zl ^ zlo)
                for j in reversed(range(SUB)):
                    acc = binj_ref[c, j : j + 1, :] + map_ref[c, 0, j : j + 1, :] * acc
            runs.append(acc)
        runb_ref[...] = jnp.concatenate(runs + [jnp.zeros((6, channels), F32)], axis=0)


def back_kernel(info, low, planes, seg, s, lengths, *refs):
    gathered_refs, back_refs = refs[: planes + 1], refs[planes + 1 : 2 * planes + 2]
    (
        map_ref, binj_ref, mixed_ref, prev_ref, direct_ref, rz_ref, fp_ref, rp_ref, fb_ref,
        grad_c_ref, grad_f_ref, sums_ref,
        carry_ref, gathered_ref, back_ref,
    ) = refs[2 * planes + 2 :]
    chunks, channels = map_ref.shape[0], map_ref.shape[3]
    step = pl.program_id(0)
    count = pl.num_programs(0)
    k, zlo = s[info.k], s[info.zlo]

    @pl.when(step == 0)
    def _():
        gathered_maps(info, planes, s, gathered_refs, gathered_ref)
        gathered_maps(info, planes, s, back_refs, back_ref)
        carry = jnp.zeros((1, channels), F32)
        own = [carry, carry]
        for plane in reversed(range(planes)):
            for core in (1, 0):
                for zh in (1, 0):
                    e = zh * planes + plane
                    mine = (plane == s[info.p]) & (zh == s[info.zhi])
                    own[core] = jnp.where(mine, carry, own[core])
                    decay = jnp.where(k == core, gathered_ref[e, 0:1, :], gathered_ref[e, 2:3, :])
                    inject = jnp.where(k == core, back_ref[e, 0:1, :], back_ref[e, 1:2, :])
                    carry = decay * carry + inject
        for dk in range(2):
            carry = jnp.where(k == 0, own[dk], own[1 - dk])
            for zl in reversed(range(low)):
                c = dk * low + (zl ^ zlo)
                for j in reversed(range(SUB)):
                    carry_ref[c, j : j + 1, :] = carry
                    carry = map_ref[c, 0, j : j + 1, :] * carry + binj_ref[c, j : j + 1, :]
        sums_ref[...] = jnp.zeros_like(sums_ref)

    rows = prev_ref.shape[1]
    steps = rows // SUB
    bounds = bounds_of(lengths)
    fp, rp, fb = fp_ref[...], rp_ref[...], fb_ref[...]
    fz_sum, peep_sum = sums_ref[0], sums_ref[1]
    for c in range(chunks):
        base = s[info.base + c]
        back = carry_ref[c]
        for i in reversed(range(steps)):
            at = slice(i * SUB, (i + 1) * SUB)
            candidate = mixed_ref[c, 0, at].astype(F32)
            forget, rest = gate(mixed_ref[c, 1, at].astype(F32) + fp * candidate + fb)
            kept = kept_of(base, (count - 1 - step) * steps + i, seg, bounds, channels)
            cell_grad = direct_ref[c, at] + back
            back = kept * (forget * cell_grad + rz_ref[c, at] * rp)
            held = cell_grad * rest
            forget_z = held * forget * (prev_ref[c, at] - candidate)
            grad_c_ref[c, at] = (held + forget_z * fp).astype(BF16)
            grad_f_ref[c, at] = forget_z.astype(BF16)
            fz_sum = fz_sum + forget_z
            peep_sum = peep_sum + forget_z * candidate
        carry_ref[c] = back
    sums_ref[0] = fz_sum
    sums_ref[1] = peep_sum


def input_kernel(info, joined, s, grad_c_ref, grad_f_ref, rzb_ref, w_ref, gain_ref, hat_ref, inv_ref, skip_ref, *refs):
    v_ref, s_ref, gb_ref, grad_ref, first_ref, second_ref = refs[1:] if joined else refs
    tile = pl.program_id(0)
    nt = (((1,), (1,)), ((), ()))
    grad = lax.dot_general(grad_c_ref[0], w_ref[0], nt, preferred_element_type=F32)
    grad = grad + lax.dot_general(grad_f_ref[0], w_ref[1], nt, preferred_element_type=F32)
    grad_ref[...] = grad + lax.dot_general(rzb_ref[0], w_ref[2], nt, preferred_element_type=F32)

    @pl.when(tile == 0)
    def _():
        first_ref[...] = jnp.zeros_like(first_ref)
        second_ref[...] = jnp.zeros_like(second_ref)

    rows, width = grad_ref.shape
    flag = jnp.where(s[info.g] == tile, 1.0, 0.0)
    gain = gain_ref[...]
    block = 32
    gain_sum = jnp.zeros((SUB, width), F32)
    bias_sum = jnp.zeros((SUB, width), F32)
    for r in range(rows // block):
        at = slice(r * block, (r + 1) * block)
        value = grad_ref[at]
        inv = jnp.concatenate([inv_ref[0, at]] * (width // LANES), axis=1)
        hat = hat_ref[0, at].astype(F32)
        scaled = value * gain
        product = scaled * hat
        first, second = first_ref[at], second_ref[at]
        for lane in range(width // LANES):
            first = first + scaled[:, lane * LANES : (lane + 1) * LANES]
            second = second + product[:, lane * LANES : (lane + 1) * LANES]
        first_ref[at] = first
        second_ref[at] = second
        matched = value * hat
        for i in range(block // SUB):
            gain_sum = gain_sum + matched[i * SUB : (i + 1) * SUB]
            bias_sum = bias_sum + value[i * SUB : (i + 1) * SUB]
        out = scaled * inv + skip_ref[0, at].astype(F32) * flag
        if joined:
            out = out + refs[0][at].astype(F32)
        v_ref[at] = out.astype(BF16)
    gb_ref[0] = gain_sum
    gb_ref[1] = bias_sum

    @pl.when(tile == pl.num_programs(0) - 1)
    def _():
        lane = lax.broadcasted_iota(jnp.int32, (rows, LANES), 1)
        first = jnp.sum(first_ref[...], axis=1, keepdims=True)
        second = jnp.sum(second_ref[...], axis=1, keepdims=True)
        s_ref[...] = jnp.where(lane == 0, first, jnp.where(lane == 1, second, 0.0)).T[:SUB]


def last_kernel(count, x_ref, order_ref, *refs):
    parts, (s_ref, out_ref) = refs[:count], refs[count:]
    width = x_ref.shape[1]
    x = x_ref[...].astype(F32)
    average = jnp.mean(x, axis=1, keepdims=True)
    centred = x - average
    inv = lax.rsqrt(jnp.mean(centred * centred, axis=1, keepdims=True) + EPSILON)
    order = order_ref[...]
    value = jnp.dot(order, parts[0][...], preferred_element_type=F32)
    for part in parts[1:]:
        value = value + jnp.dot(order, part[...], preferred_element_type=F32)
    sums = lax.dot_general(
        order.astype(F32), s_ref[...], (((1,), (1,)), ((), ())),
        precision=lax.Precision.HIGHEST, preferred_element_type=F32,
    )
    first = sums[:, 0:1] * (1.0 / width)
    second = sums[:, 1:2] * (1.0 / width)
    out_ref[...] = value - inv * (first + centred * inv * second)


def weight_grad_kernel(order, s, normed_ref, grads_ref, *out_refs):
    tn = (((0,), (0,)), ((), ()))
    total = lax.dot_general(normed_ref[0], grads_ref[0], tn, preferred_element_type=F32)
    for c in range(1, normed_ref.shape[0]):
        total = total + lax.dot_general(normed_ref[c], grads_ref[c], tn, preferred_element_type=F32)
    low = total.astype(BF16)
    half = low.shape[0] // 2
    for at, places in enumerate(order):

        @pl.when(pl.program_id(0) == at)
        def _():
            for ref, place, rows in places:
                out_refs[ref][place] = (low, low[:half], low[half:])[rows]


def owned_kernel(info, count, s, *refs):
    came, outs, total_ref, slot_ref, sem = refs[:count], refs[count : count + 2], *refs[count + 2 :]
    total_ref[...] = jnp.zeros_like(total_ref)
    for wait in (False, True):
        for n in range(count):

            @pl.when(s[info.owned + n] >= 0)
            def _():
                copy = pltpu.make_async_copy(came[n], slot_ref.at[n], sem.at[n])
                if not wait:
                    copy.start()
                else:
                    copy.wait()
                    total_ref[s[info.owned + n]] += slot_ref[n].astype(F32)

    half = total_ref.shape[1] // 2
    for n, out in enumerate(outs):
        core = s[info.k] if n == 0 else 1 - s[info.k]
        rows = pl.ds(pl.multiple_of(core * half, half), half)
        for block in range(3):
            out[block] = total_ref[block, rows, :].astype(BF16)


def spread_kernel(count, steps, s, *refs):
    pieces, out_ref = refs[:count], refs[-1]
    rows, channels = out_ref.shape[0], pieces[0].shape[2]
    for n, (piece, start) in enumerate(steps):

        @pl.when(pl.program_id(0) == n)
        def _():
            for block in range(3):
                values = pieces[piece][block, start : start + rows]
                out_ref[:, block * channels : (block + 1) * channels] = values.astype(F32)


def cost(flops, moved, exps=0):
    return pl.CostEstimate(flops=int(flops), bytes_accessed=int(moved), transcendentals=int(exps))


def per_device(
    inputs, norm_gain, norm_bias, weight, forget_peep, reset_peep, forget_bias, reset_bias, seq_lengths, out_grad
):
    rows, width = inputs.shape
    seqs, groups = lax.axis_size("seq"), lax.axis_size("col")
    planes, low = seqs // 2, groups // 2
    channels = width // groups
    chunks = groups
    seg = rows // SUB
    part = width // planes
    half, quarter = part // 2, part // 4
    seq, z = lax.axis_index("seq"), lax.axis_index("col")
    k, zhi = seq % 2, z // low
    params = functools.partial(pltpu.CompilerParams, vmem_limit_bytes=VMEM_LIMIT)
    others = range(1, planes)
    short = planes == 4
    anywhere = pl.BlockSpec(memory_space=pl.ANY)
    full = lambda shape: pl.BlockSpec(shape, lambda *_: (0,) * len(shape))
    shape_of = jax.ShapeDtypeStruct

    def move(value, to):
        pairs = []
        for a in range(seqs):
            for b in range(groups):
                target = to(a // 2, a % 2, b)
                if target is not None:
                    pairs.append((a * groups + b, (target[0] * 2 + target[1]) * groups + target[2]))
        return lax.ppermute(value, ("seq", "col"), pairs)

    def cross_core(value):
        return move(value, lambda p, k, z: (p, 1 - k, z))

    def cross_low(value, dz):
        return move(value, lambda p, k, z: (p, k, z ^ dz))

    def cross_high(value):
        return move(value, lambda p, k, z: (p, k, (z + low) % groups))

    def cross_plane(value, dp):
        return move(value, lambda p, k, z: (p ^ dp, k, z))

    def after(values, *first):
        return lax.optimization_barrier((values, first))[0]

    def gather_maps(value):
        near = [value] + [cross_plane(value, d) for d in others]
        return near + [cross_high(jnp.stack(near))]

    def add_up(values):
        total = values[0].astype(F32)
        for value in values[1:]:
            total = total + value.astype(F32)
        return total.astype(BF16)

    device = np.arange(seqs * groups)
    dev_p, dev_k, dev_z = device // groups // 2, device // groups % 2, device % groups
    dev_zhi, dev_zlo = dev_z // low, dev_z % low
    info = Info()
    for name, value in (("p", dev_p), ("k", dev_k), ("zhi", dev_zhi), ("zlo", dev_zlo), ("g", dev_zlo + low * dev_k)):
        info.put(name, [value])
    info.put(
        "base",
        [((2 * dev_p + (dev_k ^ (c // low))) * groups + dev_zhi * low + (dev_zlo ^ (c % low))) * rows for c in range(chunks)],
    )
    at_dev = lambda table: np.asarray(table)[:, dev_k, dev_z]
    plans, rounds = routes(groups, range(3))
    here = max(sum(dst == n for _, dst, _, _ in local) for local, _ in plans for n in range(groups))
    away = 0
    slot_stream = np.full((6, 2, groups), -1, np.int32)
    slot_round = np.full((3, 2, groups), -1, np.int32)
    local_block = np.zeros((3, 2, groups), np.int32)
    sends_block = np.zeros((rounds, 2, groups), np.int32)
    for core, (local, plan) in enumerate(plans):
        for n in range(groups):
            for at, edge in enumerate(edge for edge in local if edge[1] == n):
                slot_stream[at, core, n] = edge[2]
                local_block[at, core, n] = edge[3]
            found = [(r, e[2]) for r, edges in enumerate(plan) for e in edges if e[1] == n]
            for at, (r, stream) in enumerate(found):
                slot_stream[here + at, core, n] = stream
                slot_round[at, core, n] = r
            away = max(away, len(found))
        for r, edges in enumerate(plan):
            for src, _, _, at in edges:
                sends_block[r, core, src] = at
    info.put("slot_stream", at_dev(slot_stream[: here + away]))
    info.put("slot_round", at_dev(slot_round[:away]))
    info.put("local_block", at_dev(local_block))
    info.put("sends_block", at_dev(sends_block))
    back_routes = [(streams, *routes(groups, streams)) for streams in ([0, 2], [1])]
    owned, back_stream = [], []
    for streams, back_plans, count in back_routes:
        for r in range(count):
            takes = np.full((2, groups), -1, np.int32)
            source = np.zeros((2, groups), np.int32)
            for core, (_, plan) in enumerate(back_plans):
                for src, dst, stream, at in plan[r]:
                    takes[core, src] = at
                    source[core, dst] = streams.index(stream)
            owned.append(takes)
            back_stream.append(source)
        for stream in streams:
            takes = np.full((2, groups), -1, np.int32)
            for core, (local, _) in enumerate(back_plans):
                for src, _, found, at in local:
                    if found == stream:
                        takes[core, src] = at
            owned.append(takes)
    info.put("owned", at_dev(owned))
    info.put("back_stream", at_dev(back_stream[: back_routes[0][2]]))
    visits = [3, 1, 2, 0] if short else list(range(planes))
    info.put("visits", [dev_p ^ d for d in visits])
    whole_planes = range(3 if short else planes)
    split_planes = range(3, 4) if short else []
    for name, chosen in (("whole_rows", whole_planes), ("split_rows", split_planes)):
        found = [((dev_p ^ d) * 2 + (dev_k ^ dk)) * 2 + n for dk in range(2) for d in chosen for n in range(2)]
        info.put(name, np.asarray(found).reshape(-1, seqs * groups))
    scalars = lax.dynamic_index_in_dim(jnp.asarray(info.table()), seq * groups + z, 0, keepdims=False)

    order = jnp.asarray(row_order(rows), BF16)
    back_order = jnp.asarray(row_order(rows).T.copy(), BF16)

    def call(kernel, out_shape, in_specs, out_specs, grid=(1,), scratch=(), lengths=False, aliases=None, **rest):
        return pl.pallas_call(
            kernel,
            grid_spec=pltpu.PrefetchScalarGridSpec(
                num_scalar_prefetch=2 if lengths else 1,
                grid=grid,
                in_specs=in_specs,
                out_specs=out_specs,
                scratch_shapes=list(scratch),
            ),
            out_shape=out_shape,
            input_output_aliases=aliases or {},
            compiler_params=params(),
            **rest,
        )

    def cut(name, count, copies, first=()):
        source, row = after((weight, scalars), *first) if first else (weight, scalars)
        at = getattr(info, name)
        return call(
            functools.partial(cut_kernel, count, copies),
            [shape_of((copies * part, channels), BF16)] * count,
            [pl.BlockSpec((part, channels), lambda t, s: (s[info.p], s[at + t]))],
            [full((copies * part, channels))] * count,
            grid=(count,),
            cost_estimate=cost(0, 0),
            name="cut_weight",
        )(row, source)

    def round_to(plan, r):
        return {(core, e[0]): e[1] for core, (_, rounds_of) in enumerate(plan) for e in rounds_of[r]}

    blocks_out = cut("sends_block", rounds, 1)
    arrived = []
    for r in range(rounds):
        to = round_to(plans, r)
        arrived.append(move(blocks_out[r], lambda p, k, z: (p, k, to[(k, z)]) if (k, z) in to else None))
    permuted = jnp.dot(order, after(inputs, blocks_out), preferred_element_type=F32).astype(BF16)
    x_core = cross_core(permuted)
    plane_groups = [[2 * n + core for n in range(planes)] for core in range(2)]
    local_full = [
        lax.all_gather(value, "seq", axis_index_groups=plane_groups, tiled=True)
        for value in cut("local_block", here, 1, (permuted,))
    ]
    tile = 128 if rows % 128 == 0 else rows
    tiles = rows // tile
    early = [cross_low(permuted[:tile], dz) for dz in range(1, low)]

    gates = jnp.stack([forget_peep, reset_peep, forget_bias, reset_bias])
    gates_far = cross_high(after(gates, x_core))
    gates = jnp.where(zhi == k, gates, gates_far)
    fp, rp, fb, rb = (gates[n : n + 1] for n in range(4))

    half_rows = low * rows
    own_half = lax.dynamic_slice_in_dim(out_grad, zhi * half_rows, half_rows, 0)
    unit = half_rows // 32
    far_parts = []
    for start, size in ((0, 8), (8, 11), (19, 13)):
        far_parts.append(lax.dynamic_slice_in_dim(out_grad, (1 - zhi) * half_rows + start * unit, size * unit, 0))
    taken = call(
        functools.partial(pick_kernel, "slot_round", info, rounds),
        shape_of((away, part, channels), BF16),
        [full((part, channels))] * rounds,
        full((away, part, channels)),
        cost_estimate=cost(0, 3 * part * channels),
        name="pick_blocks",
    )(scalars, *arrived)
    taken, x_late, far_parts = after((taken, permuted[tile:], far_parts), local_full, x_core, early, gates)
    far_came = [cross_high(far_parts[0])]
    late = [cross_low(x_late, dz) for dz in range(1, low)]
    if short:
        near_one, near_two = cross_plane(taken, 1), cross_plane(taken, 2)
        taken_full = [taken, near_one, near_two]
        taken_ends = [cross_plane(near_one[:, :half], 2), cross_plane(near_two[:, half:], 1)]
    else:
        taken_full = [taken] + [cross_plane(taken, d) for d in others]
        taken_ends = []
    gain2, bias2 = norm_gain[None, :], norm_bias[None, :]

    row_shapes = (
        shape_of((chunks, rows, width), BF16),
        shape_of((chunks, rows, channels), BF16),
        shape_of((chunks, rows, width), BF16),
        shape_of((chunks, rows, LANES), F32),
    )
    mix_shapes = (shape_of((chunks, 3, rows, channels), BF16), shape_of((chunks, 2, SUB, channels), F32))
    wide = 256 if rows % 256 == 0 else rows

    def normalise(c, value, held):
        return call(
            functools.partial(norm_kernel, info),
            row_shapes,
            [pl.BlockSpec((wide, width), lambda t, s: (t, 0)), full((1, width)), full((1, width))]
            + [anywhere] * len(held),
            [
                pl.BlockSpec((1, wide, width), lambda t, s: (c, t, 0)),
                pl.BlockSpec((1, wide, channels), lambda t, s: (c, t, 0)),
                pl.BlockSpec((1, wide, width), lambda t, s: (c, t, 0)),
                pl.BlockSpec((1, wide, LANES), lambda t, s: (c, t, 0)),
            ],
            grid=(rows // wide,),
            aliases={4 + n: n for n in range(len(held))},
            cost_estimate=cost(12 * rows * width, 7 * rows * width),
            name="norm_chunk",
        )(scalars, value, gain2, bias2, *held)

    held = normalise(0, permuted, ())
    held = normalise(low, x_core, held)

    early, late, far_parts = after((early, late, far_parts), taken_full, taken_ends, held, far_came)
    cross = [(cross_core(a), cross_core(b)) for a, b in zip(early, late)]
    far_came.append(cross_high(far_parts[1]))
    mix_cost = cost(3 * chunks * rows * width * channels, 4 * chunks * rows * width + 12 * width * channels)
    mixed, maps, full_weight = call(
        functools.partial(mix_kernel, info, low, planes, seg, here, away, short),
        mix_shapes + (shape_of((3, width, channels), BF16),),
        [pl.BlockSpec((1, rows, width), lambda t, *_: (t * low, 0, 0)), full((1, channels)), full((1, channels))]
        + [anywhere] * (here + len(taken_full) + len(taken_ends)),
        [
            pl.BlockSpec((1, 3, rows, channels), lambda t, *_: (t * low, 0, 0, 0)),
            pl.BlockSpec((1, 2, SUB, channels), lambda t, *_: (t * low, 0, 0, 0)),
            anywhere,
        ],
        grid=(2,),
        scratch=[
            pltpu.VMEM((3, width, channels), BF16),
            pltpu.SemaphoreType.DMA((here + away * (planes + 1),)),
            pltpu.SemaphoreType.DMA,
        ],
        lengths=True,
        cost_estimate=mix_cost,
        name="mix_near",
    )(scalars, seq_lengths, held[0], fp, fb, *local_full, *taken_full, *taken_ends)

    mixed, far_parts = after((mixed, far_parts), far_came)
    far_came.append(cross_high(far_parts[2]))
    far_order = [far_chunk(low, n) for n in range(2 * (low - 1))]
    far_pieces = [(early[c % low - 1], late[c % low - 1]) if c < low else cross[c % low - 1] for c in far_order]
    far_at = lambda t: far_chunk(low, t)
    *held, mixed, maps, run_maps = call(
        functools.partial(mix_far_kernel, info, low, seg, far_order, tile),
        row_shapes + mix_shapes + (shape_of((SUB, channels), F32),),
        [full((3, width, channels)), full((1, width)), full((1, width)), full((1, channels)), full((1, channels))]
        + [full((chunks, 2, SUB, channels))]
        + [anywhere] * (2 * len(far_order))
        + [anywhere] * 5,
        [
            pl.BlockSpec((1, rows, width), lambda t, *_: (far_at(t), 0, 0)),
            pl.BlockSpec((1, rows, channels), lambda t, *_: (far_at(t), 0, 0)),
            pl.BlockSpec((1, rows, width), lambda t, *_: (far_at(t), 0, 0)),
            pl.BlockSpec((1, rows, LANES), lambda t, *_: (far_at(t), 0, 0)),
            pl.BlockSpec((1, 3, rows, channels), lambda t, *_: (far_at(t), 0, 0, 0)),
            full((chunks, 2, SUB, channels)),
            full((SUB, channels)),
        ],
        grid=(len(far_order),),
        scratch=[
            pltpu.VMEM((len(far_order), rows, width), BF16),
            pltpu.SemaphoreType.DMA((2 * len(far_order),)),
        ],
        lengths=True,
        aliases={8 + 2 * len(far_order) + n: n for n in range(5)},
        cost_estimate=mix_cost,
        name="mix_far",
    )(
        scalars, seq_lengths, full_weight, gain2, bias2, fp, fb, maps,
        *[piece for pair in far_pieces for piece in pair], *held, mixed,
    )
    normed, highway, hats, invs = held

    gathered = gather_maps(run_maps)
    far_half = jnp.concatenate(after(far_came, run_maps), axis=0)
    keep = jnp.where(zhi == k, own_half, far_half)
    give = cross_core(jnp.where(zhi == k, far_half, own_half))

    map_specs = [full((SUB, channels))] * planes + [full((planes, SUB, channels))]
    block = 64
    blocks = rows // block
    elements = chunks * rows * channels
    runs = (low, rows, channels)
    part_rows = (chunks, block, channels)
    at_block = lambda t, *_: (0, t, 0)
    state_out = call(
        functools.partial(state_kernel, info, low, planes, seg),
        (
            shape_of(runs, BF16),
            shape_of(runs, BF16),
            shape_of((chunks, rows, channels), F32),
            shape_of((chunks, rows, channels), F32),
            shape_of((chunks, rows, channels), F32),
            shape_of((chunks, rows, channels), BF16),
            shape_of((chunks, rows, channels), BF16),
            shape_of((chunks, SUB, channels), F32),
            shape_of((2, SUB, channels), F32),
            shape_of((SUB, channels), F32),
        ),
        map_specs
        + [
            full((chunks, 2, SUB, channels)),
            pl.BlockSpec((chunks, 3, block, channels), lambda t, *_: (0, 0, t, 0)),
            pl.BlockSpec(part_rows, at_block),
            full(runs),
            full(runs),
            pl.BlockSpec((block, rows), lambda t, *_: (t, 0)),
            full((rows, rows)),
        ]
        + [full((1, channels))] * 4,
        [full(runs), full(runs)]
        + [pl.BlockSpec(part_rows, at_block)] * 5
        + [full((chunks, SUB, channels)), full((2, SUB, channels)), full((SUB, channels))],
        grid=(blocks,),
        scratch=[
            pltpu.VMEM((chunks, SUB, channels), F32),
            pltpu.VMEM((chunks, SUB, channels), F32),
            pltpu.VMEM((chunks, rows, channels), F32),
            pltpu.VMEM((2 * planes, SUB, channels), F32),
        ],
        lengths=True,
        cost_estimate=cost(60 * elements, 30 * elements, 4 * elements),
        name="states",
    )(
        scalars, seq_lengths, *gathered, maps, mixed, highway, keep.reshape(runs), give.reshape(runs),
        order, back_order, fp, rp, fb, rb,
    )
    out_own, out_far, previous, direct, reset_z, reset_zb, skip, binj, reset_sums, run_back = state_out

    if short:
        places = [[(0, 1, 1), (1, 1, 2)], [(0, 0, 1), (3, 1, 2)], [(2, 1, 1), (1, 0, 2)], [(2, 0, 1), (3, 0, 2)]]
        part_shapes = [(2, half, channels)] * 4
    else:
        places = [[(d, 0, 0)] for d in visits]
        part_shapes = [(1, part, channels)] * planes

    def weight_part(source, name):
        return call(
            functools.partial(weight_grad_kernel, places),
            [shape_of(shape, BF16) for shape in part_shapes],
            [pl.BlockSpec((chunks, rows, part), lambda t, s: (0, 0, s[info.visits + t])), full((chunks, rows, channels))],
            [full(shape) for shape in part_shapes],
            grid=(planes,),
            cost_estimate=cost(2 * chunks * rows * width * channels, 4 * chunks * rows * width),
            name=name,
        )(scalars, normed, source)

    def first_sends(parts):
        if short:
            return [cross_plane(parts[0], 1), cross_plane(parts[1], 2)]
        return [cross_plane(parts[d], d) for d in others]

    def second_start(parts, came):
        if not short:
            return came
        return [add_up([parts[2][1], came[0][1]]), add_up([parts[3][1], came[1][1]])]

    def second_end(parts, came, over):
        if not short:
            return add_up([parts[0][0]] + [value[0] for value in came])
        first = add_up([parts[2][0], came[0][0], cross_plane(over[0], 2)])
        second = add_up([parts[3][0], came[1][0], cross_plane(over[1], 1)])
        return jnp.concatenate([first, second], axis=0)

    def second_sends(parts, came):
        return second_end(parts, came, second_start(parts, came))

    def to_owners(which, values):
        _, back_plans, count = back_routes[which]
        found = []
        for r in range(count):
            back = {(core, dst): src for (core, src), dst in round_to(back_plans, r).items()}
            found.append(move(values[r], lambda p, k, z: (p, k, back[(k, z)]) if (k, z) in back else None))
        return found

    near_back = [run_back] + [cross_plane(run_back, d) for d in others]
    reset_wg = weight_part(after(reset_zb, near_back), "weight_grad_reset")
    gathered_back = near_back + [after(cross_high(jnp.stack(near_back)), reset_wg)]
    got = after(cross_core(out_far), reset_wg)
    stay = jnp.where(k == zhi, out_own, got)
    leave = jnp.where(k == zhi, got, out_own).reshape(4, half_rows // 4, channels)
    binj, leave = after((binj, leave), reset_wg, leave, gathered_back)
    out_came = []

    def send_out(piece):
        out_came.append(cross_high(piece))

    send_out(leave[0])
    reset_came = first_sends(after(reset_wg, gathered_back))

    grad_c, grad_f, forget_sums = call(
        functools.partial(back_kernel, info, low, planes, seg),
        (
            shape_of((chunks, rows, channels), BF16),
            shape_of((chunks, rows, channels), BF16),
            shape_of((2, SUB, channels), F32),
        ),
        map_specs * 2
        + [
            full((chunks, 2, SUB, channels)),
            full((chunks, SUB, channels)),
            pl.BlockSpec((chunks, 2, block, channels), lambda t, *_: (0, 0, blocks - 1 - t, 0)),
        ]
        + [pl.BlockSpec(part_rows, lambda t, *_: (0, blocks - 1 - t, 0))] * 3
        + [full((1, channels))] * 3,
        [pl.BlockSpec(part_rows, lambda t, *_: (0, blocks - 1 - t, 0))] * 2 + [full((2, SUB, channels))],
        grid=(blocks,),
        scratch=[
            pltpu.VMEM((chunks, SUB, channels), F32),
            pltpu.VMEM((2 * planes, SUB, channels), F32),
            pltpu.VMEM((2 * planes, SUB, channels), F32),
        ],
        lengths=True,
        cost_estimate=cost(30 * elements, 20 * elements, 2 * elements),
        name="state_grads",
    )(scalars, seq_lengths, *gathered, *gathered_back, maps, binj, mixed, previous, direct, reset_z, fp, rp, fb)

    def chunk_grad(c, joined):
        extra = [pl.BlockSpec((rows, channels), lambda t, s: (0, t))] if joined is not None else []
        chunk_block = pl.BlockSpec((1, rows, channels), lambda t, s: (c, 0, 0))
        return call(
            functools.partial(input_kernel, info, joined is not None),
            (shape_of((rows, width), BF16), shape_of((SUB, rows), F32), shape_of((2, SUB, width), F32)),
            [
                chunk_block,
                chunk_block,
                chunk_block,
                pl.BlockSpec((3, channels, channels), lambda t, s: (0, t, 0)),
                pl.BlockSpec((1, channels), lambda t, s: (0, t)),
                pl.BlockSpec((1, rows, channels), lambda t, s: (c, 0, t)),
                pl.BlockSpec((1, rows, LANES), lambda t, s: (c, 0, 0)),
                chunk_block,
            ]
            + extra,
            [
                pl.BlockSpec((rows, channels), lambda t, s: (0, t)),
                full((SUB, rows)),
                pl.BlockSpec((2, SUB, channels), lambda t, s: (0, 0, t)),
            ],
            grid=(groups,),
            scratch=[
                pltpu.VMEM((rows, channels), F32),
                pltpu.VMEM((rows, LANES), F32),
                pltpu.VMEM((rows, LANES), F32),
            ],
            cost_estimate=cost(6 * rows * width * channels, 8 * rows * width + 6 * width * channels),
            name="chunk_grad",
        )(
            scalars, grad_c, grad_f, reset_zb, full_weight, gain2, hats, invs, skip,
            *([joined] if joined is not None else []),
        )

    norm_sums = []

    def grads_of(c, joined, *first):
        nonlocal grad_c
        grad_c = after(grad_c, *first)
        value, sums, gb = chunk_grad(c, joined)
        norm_sums.append(gb)
        return value, sums

    reset_came, out_came[-1], leave = after((reset_came, out_came[-1], leave), grad_c)
    over = second_start(reset_wg, reset_came)
    send_out(leave[1])
    candidate_wg = weight_part(after(grad_c, over, out_came[0]), "weight_grad_candidate")
    reset_part = after(second_end(reset_wg, reset_came, over), candidate_wg)
    out_came[-1], leave = after((out_came[-1], leave), candidate_wg)
    send_out(leave[2])
    candidate_came = first_sends(after(candidate_wg, reset_part))
    back_far = []
    for dz in range(1, low):
        value, sums = grads_of(low + dz, None, candidate_wg, reset_part, out_came[1])
        back_far.append((value, sums))
    candidate_came, out_came[-1], leave = after((candidate_came, out_came[-1], leave), back_far)
    send_out(leave[3])
    over = second_start(candidate_wg, candidate_came)
    from_core = [(cross_core(value), cross_core(sums)) for value, sums in after(back_far, over)]
    forget_wg = weight_part(after(grad_f, over, back_far, out_came[2]), "weight_grad_forget")
    from_core, out_came[-1] = after((from_core, out_came[-1]), forget_wg)
    candidate_part = after(second_end(candidate_wg, candidate_came, over), forget_wg)
    forget_came = first_sends(after(forget_wg, candidate_part, from_core, out_came))
    if rounds_first := back_routes[0][2]:
        sends = call(
            functools.partial(pick_kernel, "back_stream", info, 2),
            [shape_of((part, channels), BF16)] * rounds_first,
            [full((part, channels))] * 2,
            [full((part, channels))] * rounds_first,
            cost_estimate=cost(0, 3 * part * channels),
            name="pick_parts",
        )(scalars, candidate_part, reset_part)
    first_parts = to_owners(0, sends)
    far_values = []
    for dz in range(1, low):
        value, sums = grads_of(dz, from_core[dz - 1][0], forget_wg, sends)
        far_values.append((value, sums + from_core[dz - 1][1]))
    forget_came = after(forget_came, far_values)
    over = second_start(forget_wg, forget_came)
    value_other, sums_other = grads_of(low, None, over, far_values)
    forget_part = after(second_end(forget_wg, forget_came, over), value_other)
    first_parts = after(first_parts, value_other)
    forget_part = after(forget_part, first_parts)
    last_parts = to_owners(1, [forget_part] * back_routes[1][2])
    value_core, sums_core = cross_core(value_other), cross_core(sums_other)
    value_own, sums_own = grads_of(0, None, forget_part, first_parts)
    last_parts = after(last_parts, value_own)
    far = [
        (cross_low(value, dz + 1), cross_low(sums, dz + 1))
        for dz, (value, sums) in enumerate(after(far_values, last_parts))
    ]
    owned_parts = first_parts + [candidate_part, reset_part] + last_parts + [forget_part]

    block_piece = (3, half, channels)
    own_blocks, give_blocks = call(
        functools.partial(owned_kernel, info, len(owned_parts)),
        [shape_of(block_piece, BF16)] * 2,
        [anywhere] * len(owned_parts),
        [full(block_piece)] * 2,
        scratch=[
            pltpu.VMEM((3, part, channels), F32),
            pltpu.VMEM((len(owned_parts), part, channels), BF16),
            pltpu.SemaphoreType.DMA((len(owned_parts),)),
        ],
        cost_estimate=cost(0, 6 * part * channels),
        name="own_blocks",
    )(scalars, *owned_parts)
    own_sum = add_up([own_blocks, cross_core(give_blocks)])
    whole = [own_sum] + [cross_plane(own_sum, d) for d in (others[:2] if short else others)]
    split = []
    if short:
        split = [cross_plane(whole[1][:, :quarter], 2), cross_plane(whole[2][:, quarter:], 1)]
    whole = whole + [cross_core(value) for value in whole]
    split = split + [cross_core(value) for value in split]

    def spread(name, values, steps, held):
        return call(
            functools.partial(spread_kernel, len(values), steps),
            shape_of((width, 3 * channels), F32),
            [full(value.shape) for value in values] + [anywhere] * len(held),
            pl.BlockSpec((quarter, 3 * channels), lambda t, s: (s[getattr(info, name) + t], 0)),
            grid=(len(steps),),
            aliases={1 + len(values): 0} if held else None,
            cost_estimate=cost(0, 9 * width * channels),
            name="spread_" + name,
        )(scalars, *values, *held)

    weight_grad = spread("whole_rows", whole, [(n, at) for n in range(len(whole)) for at in (0, quarter)], ())
    if short:
        weight_grad = spread("split_rows", split, [(n, 0) for n in range(len(split))], (weight_grad,))
    gate_sums = jnp.sum(jnp.concatenate([forget_sums, reset_sums]), axis=1)
    spread_sums = lax.dynamic_update_slice(
        jnp.zeros((4, width), F32), gate_sums, (0, (z % low + low * k) * channels)
    )
    small = jnp.concatenate([jnp.sum(sum(norm_sums[1:], norm_sums[0]), axis=1), spread_sums], axis=0)
    small = after(small, whole)
    small = small + cross_core(small)
    for bit in bits_of(planes):
        small = small + cross_plane(small, bit)
    for bit in bits_of(groups):
        small = small + cross_low(small, bit)

    came = jnp.stack(out_came).reshape(stay.shape)
    output = jnp.where(zhi == 0, jnp.stack([stay, came]), jnp.stack([came, stay])).reshape(groups * rows, channels)
    far, weight_grad = after((far, weight_grad), weight_grad)
    parts = [value_own, value_core] + [value for value, _ in far]
    sums = sum([sums_core] + [sums for _, sums in far], sums_own)
    input_grad = pl.pallas_call(
        functools.partial(last_kernel, len(parts)),
        grid=(tiles,),
        in_specs=[
            pl.BlockSpec((tile, width), lambda t: (t, 0)),
            pl.BlockSpec((tile, rows), lambda t: (t, 0)),
        ]
        + [full((rows, width))] * len(parts)
        + [full((SUB, rows))],
        out_specs=pl.BlockSpec((tile, width), lambda t: (t, 0)),
        out_shape=shape_of((rows, width), F32),
        compiler_params=params(),
        cost_estimate=cost(4 * rows * rows * width, 10 * rows * width),
        name="input_grad",
    )(inputs, back_order, *parts, sums)
    gate_block = lax.dynamic_slice_in_dim(small[2:], z * channels, channels, 1)
    return (
        output,
        input_grad,
        weight_grad,
        small[0],
        small[1],
        gate_block[1],
        gate_block[3],
        gate_block[0],
        gate_block[2],
    )


def solution(mesh):
    placed = (
        P(("seq", "col"), None),
        P(),
        P(),
        P(None, "col"),
        P("col"),
        P("col"),
        P("col"),
        P("col"),
        P(),
        P("seq", "col"),
    )
    return jax.shard_map(
        per_device,
        mesh=mesh,
        in_specs=placed,
        out_specs=(
            P("seq", "col"),
            P(("seq", "col"), None),
            P(None, "col"),
            P(),
            P(),
            P("col"),
            P("col"),
            P("col"),
            P("col"),
        ),
        check_vma=False,
    )
```

```python
import functools

import jax
import jax.numpy as jnp
import numpy as np
from jax import lax
from jax.experimental import pallas as pl
from jax.experimental.pallas import tpu as pltpu
from jax.sharding import PartitionSpec as P

EPSILON = 1e-05
F32 = jnp.float32
BF16 = jnp.bfloat16
LANES = 128
SUB = 8
VMEM_LIMIT = 56 * 1024 * 1024


def bits_of(count):
    return [1 << b for b in range(count.bit_length() - 1)]


def colour(edges, count):
    degree = max([sum(e[0] == n for e in edges) for n in range(count)] + [sum(e[1] == n for e in edges) for n in range(count)])
    out = [[None] * degree for _ in range(count)]
    into = [[None] * degree for _ in range(count)]
    taken = {}
    for at, edge in enumerate(edges):
        src, dst = edge[0], edge[1]
        first = next(c for c in range(degree) if out[src][c] is None)
        second = next(c for c in range(degree) if into[dst][c] is None)
        if first != second:
            path, node, at_dst, look = [], dst, True, first
            while True:
                found = (into if at_dst else out)[node][look]
                if found is None:
                    break
                path.append(found)
                node = edges[found][0] if at_dst else edges[found][1]
                at_dst = not at_dst
                look = second if look == first else first
            for found in path:
                old = taken[found]
                out[edges[found][0]][old] = None
                into[edges[found][1]][old] = None
            for found in path:
                new = second if taken[found] == first else first
                taken[found] = new
                out[edges[found][0]][new] = found
                into[edges[found][1]][new] = found
        taken[at] = first
        out[src][first] = at
        into[dst][first] = at
    rounds = [[] for _ in range(degree)]
    for at, edge in enumerate(edges):
        rounds[taken[at]].append(edge)
    return rounds


def busiest(edges, groups):
    links = {}
    for src, dst, _, _ in edges:
        a, b = src % groups, dst % groups
        for n in range(min(a, b), max(a, b)):
            links[n, a < b] = links.get((n, a < b), 0) + 1
    return max(links.values(), default=0)


def balance(rounds, groups):
    if len(rounds) != 2:
        return rounds
    paths = []
    left = [(r, e) for r in range(2) for e in rounds[r]]
    while left:
        path = [left.pop()]
        grown = True
        while grown:
            near = [x for x in left if any(x[1][0] == y[1][0] or x[1][1] == y[1][1] for y in path)]
            left = [x for x in left if x not in near]
            path += near
            grown = bool(near)
        paths.append(path)
    best = None
    for flips in range(2 ** len(paths)):
        tried = [[], []]
        for n, path in enumerate(paths):
            for r, edge in path:
                tried[r ^ (flips >> n & 1)].append(edge)
        score = sum(busiest(edges, groups) for edges in tried)
        score = (max(busiest(edges, groups) for edges in tried), score)
        if best is None or score < best[0]:
            best = (score, tried)
    return best[1]


def routes(groups, streams):
    low = groups // 2
    local, edges = [], []
    load = [0] * (2 * groups)
    for core in range(2):
        for z in range(groups):
            for stream in streams:
                block = stream * groups + z % low + low * core
                owner, at = block // 3, block % 3
                dst = core * groups + z
                if owner == z:
                    local.append((dst, dst, stream, at))
                else:
                    edges.append([core, owner, dst, stream, at])
    found = []
    for owner in range(groups):
        mine = [e for e in edges if e[1] == owner]
        quota = -(-len(mine) // 2)
        for core, _, dst, stream, at in mine:
            src = core * groups + owner
            if load[src] == quota:
                src = (1 - core) * groups + owner
            load[src] += 1
            found.append((src, dst, stream, at))
    return local, balance(colour(found, 2 * groups), groups)


def row_order(rows):
    seg = rows // SUB
    matrix = np.zeros((rows, rows), np.float32)
    for i in range(seg):
        for j in range(SUB):
            matrix[i * SUB + j, j * seg + i] = 1.0
    return matrix


def gate(value):
    small = jnp.exp(-jnp.abs(value))
    minor = small / (1.0 + small)
    major = 1.0 - minor
    up = value >= 0.0
    return jnp.where(up, major, minor), jnp.where(up, minor, major)


def kept_of(base, step, seg, bounds, channels):
    at = lax.broadcasted_iota(jnp.int32, (SUB, LANES), 0) * seg + (base + step)
    starts = at == bounds[0]
    for bound in bounds[1:]:
        starts = starts | (at == bound)
    kept = jnp.where(starts, 0.0, 1.0)
    return jnp.concatenate([kept] * (channels // LANES), axis=1)


class Info:
    def __init__(self):
        self.spots = {}
        self.columns = []

    def put(self, name, values):
        self.spots[name] = len(self.columns)
        self.columns += list(np.asarray(values, np.int32))

    def __getattr__(self, name):
        return self.spots[name]

    def table(self):
        return np.stack(self.columns, axis=1)


def bounds_of(lengths):
    starts = [0]
    for n in range(lengths.shape[0] - 1):
        starts.append(starts[-1] + lengths[n])
    return starts


def cut_kernel(count, s, *refs):
    for n in range(count):
        refs[count + n][...] = refs[n][...]


def pick_kernel(name, info, sources, s, *refs):
    came, outs = refs[:sources], refs[sources:]
    outs = list(outs) if len(outs) > 1 else [outs[0].at[n] for n in range(outs[0].shape[0])]
    for n, out in enumerate(outs):
        for r in range(sources):

            @pl.when(s[getattr(info, name) + n] == r)
            def _():
                out[...] = came[r][...]


def norm_rows(x_ref, gain, bias, normed_ref, hat_ref, inv_ref):
    block = 32
    for r in range(x_ref.shape[0] // block):
        at = slice(r * block, (r + 1) * block)
        x = x_ref[at].astype(F32)
        average = jnp.mean(x, axis=1, keepdims=True)
        centred = x - average
        inv = lax.rsqrt(jnp.mean(centred * centred, axis=1, keepdims=True) + EPSILON)
        hat = centred * inv
        normed_ref[0, at] = (hat * gain + bias).astype(BF16)
        hat_ref[0, at] = hat.astype(BF16)
        inv_ref[0, at] = jnp.broadcast_to(inv, (block, LANES))


def group_columns(info, s, channels):
    return pl.ds(pl.multiple_of(s[info.g] * channels, channels), channels)


def norm_kernel(info, s, x_ref, gain_ref, bias_ref, *refs):
    normed_ref, hx_ref, hat_ref, inv_ref = refs[-4:]
    norm_rows(x_ref, gain_ref[...], bias_ref[...], normed_ref, hat_ref, inv_ref)
    hx_ref[0] = x_ref[:, group_columns(info, s, hx_ref.shape[2])]


def segment_maps(base, seg, lengths, mixed_ref, fp, fb):
    channels = mixed_ref.shape[3]
    run_decay = jnp.ones((SUB, channels), F32)
    run_state = jnp.zeros((SUB, channels), F32)
    bounds = bounds_of(lengths)
    for i in range(mixed_ref.shape[2] // SUB):
        at = slice(i * SUB, (i + 1) * SUB)
        candidate = mixed_ref[0, 0, at].astype(F32)
        forget, rest = gate(mixed_ref[0, 1, at].astype(F32) + fp * candidate + fb)
        decay = forget * kept_of(base, i, seg, bounds, channels)
        run_state = decay * run_state + rest * candidate
        run_decay = decay * run_decay
    return run_decay, run_state


def mix_kernel(info, low, planes, seg, here, away, split, s, lengths, normed_ref, fp_ref, fb_ref, *refs):
    part = refs[0].shape[-2]
    whole = [(d, 0, part) for d in range(planes)]
    if split:
        ends = [(3, 0, part // 2), (3, part // 2, part // 2)]
        whole = whole[:3] + ends
    count = (here + 1) * len(whole)
    pieces = refs[:count]
    mixed_ref, map_ref, full_ref, w_ref, in_sem, out_sem = refs[count:]
    step = pl.program_id(0)

    def copies(slot):
        stream = s[info.slot_stream + slot]
        found = []
        for n, (d, start, size) in enumerate(whole):
            rows = pl.ds(pl.multiple_of((d ^ s[info.p]) * part + start, size), size)
            piece = pieces[slot * len(whole) + n] if slot < here else pieces[here * len(whole) + n].at[slot - here]
            spot = slot * len(whole) + n
            found.append(pltpu.make_async_copy(piece, w_ref.at[stream, rows, :], in_sem.at[spot]))
        return found

    @pl.when(step == 0)
    def _():
        for slot in range(here + away):

            @pl.when(s[info.slot_stream + slot] >= 0)
            def _():
                for copy in copies(slot):
                    copy.start()

        for slot in range(here + away):

            @pl.when(s[info.slot_stream + slot] >= 0)
            def _():
                for copy in copies(slot):
                    copy.wait()

        pltpu.make_async_copy(w_ref, full_ref, out_sem).start()

    for stream in range(2):
        mixed_ref[0, stream] = jnp.dot(normed_ref[0], w_ref[stream], preferred_element_type=F32).astype(BF16)
    decay, state = segment_maps(s[info.base + step * low], seg, lengths, mixed_ref, fp_ref[...], fb_ref[...])
    map_ref[0, 0] = decay
    map_ref[0, 1] = state

    @pl.when(step == pl.num_programs(0) - 1)
    def _():
        pltpu.make_async_copy(w_ref, full_ref, out_sem).wait()


def mix_far_kernel(info, low, seg, order, sizes, s, lengths, w_ref, gain_ref, bias_ref, fp_ref, fb_ref, near_ref, *refs):
    count = len(order)
    pieces = refs[: len(sizes) * count]
    normed_ref, hx_ref, hat_ref, inv_ref, mixed_ref, map_ref, run_ref, x_ref, sem = refs[len(sizes) * count + 5 :]
    channels = w_ref.shape[2]
    step = pl.program_id(0)

    def copies(n):
        found, start = [], 0
        for m, size in enumerate(sizes):
            spot = n * len(sizes) + m
            found.append(pltpu.make_async_copy(pieces[spot], x_ref.at[n, pl.ds(start, size), :], sem.at[spot]))
            start += size
        return found

    @pl.when(step == 0)
    def _():
        for n in range(count):
            for copy in copies(n):
                copy.start()
        for dk in range(2):
            map_ref[dk * low] = near_ref[dk * low]

    for n in range(count):

        @pl.when(step == n)
        def _():
            for copy in copies(n):
                copy.wait()

    mine = x_ref.at[step]
    norm_rows(mine, gain_ref[...], bias_ref[...], normed_ref, hat_ref, inv_ref)
    hx_ref[0] = mine[:, group_columns(info, s, channels)]
    for stream in range(2):
        mixed_ref[0, stream] = jnp.dot(normed_ref[0], w_ref[stream], preferred_element_type=F32).astype(BF16)
    chunk = far_chunk(low, step)
    decay, state = segment_maps(s[info.base + chunk], seg, lengths, mixed_ref, fp_ref[...], fb_ref[...])
    map_ref[chunk, 0] = decay
    map_ref[chunk, 1] = state

    @pl.when(step == count - 1)
    def _():
        rows = []
        for dk in range(2):
            decay = jnp.ones((1, channels), F32)
            state = jnp.zeros((1, channels), F32)
            for zl in range(low):
                c = dk * low + (zl ^ s[info.zlo])
                for j in range(SUB):
                    d, b = map_ref[c, 0, j : j + 1, :], map_ref[c, 1, j : j + 1, :]
                    state = d * state + b
                    decay = d * decay
            rows += [decay, state]
        run_ref[...] = jnp.concatenate(rows + [jnp.zeros((4, channels), F32)], axis=0)


def reset_kernel(normed_ref, w_ref, out_ref):
    out_ref[0] = jnp.dot(normed_ref[0], w_ref[0], preferred_element_type=F32).astype(BF16)


def far_chunk(low, n):
    return n // (low - 1) * low + 1 + n % (low - 1)


def gathered_maps(info, planes, s, refs, into):
    for d in range(planes):
        plane = d ^ s[info.p]
        into[s[info.zhi] * planes + plane] = refs[d][...]
        into[(1 - s[info.zhi]) * planes + plane] = refs[planes][d]


def state_kernel(info, low, planes, seg, sizes, s, lengths, *refs):
    gathered_refs = refs[: planes + 1]
    map_ref, mixed_ref, reset_ref, hx_ref, og_ref, og_cross_ref = refs[planes + 1 : planes + 7]
    far_refs = refs[planes + 7 : planes + 7 + 2 * len(sizes)]
    (
        order_ref, back_order_ref, fp_ref, rp_ref, fb_ref, rb_ref,
        out_ref, out_far_ref, prev_ref, direct_ref, rz_ref, skip_ref, binj_ref, sums_ref, runb_ref,
        cell_ref, prod_ref, kept_out_ref, gathered_ref, grad_ref, og_all_ref, og_sem,
    ) = refs[planes + 7 + 2 * len(sizes) :]
    chunks, channels = map_ref.shape[0], map_ref.shape[3]
    step = pl.program_id(0)
    last = pl.num_programs(0) - 1
    k, zlo = s[info.k], s[info.zlo]

    @pl.when(step == 0)
    def _():
        stays = s[info.zhi] == k
        here_copies = [
            pltpu.make_async_copy(ref, og_all_ref.at[n], og_sem.at[n, 0]) for n, ref in enumerate((og_ref, og_cross_ref))
        ]
        far_copies = []
        for n in range(2):
            start = 0
            for m, size in enumerate(sizes):
                target = og_all_ref.at[n, pl.ds(start, size), :]
                far_copies.append(pltpu.make_async_copy(far_refs[n * len(sizes) + m], target, og_sem.at[n, m]))
                start += size

        @pl.when(stays)
        def _():
            for copy in here_copies:
                copy.start()

        @pl.when(jnp.logical_not(stays))
        def _():
            for copy in far_copies:
                copy.start()

        gathered_maps(info, planes, s, gathered_refs, gathered_ref)
        carry = jnp.zeros((1, channels), F32)
        own = [carry, carry]
        for plane in range(planes):
            for core in range(2):
                for zh in range(2):
                    e = zh * planes + plane
                    mine = (plane == s[info.p]) & (zh == s[info.zhi])
                    own[core] = jnp.where(mine, carry, own[core])
                    decay = jnp.where(k == core, gathered_ref[e, 0:1, :], gathered_ref[e, 2:3, :])
                    state = jnp.where(k == core, gathered_ref[e, 1:2, :], gathered_ref[e, 3:4, :])
                    carry = decay * carry + state
        for dk in range(2):
            carry = jnp.where(k == 0, own[dk], own[1 - dk])
            for zl in range(low):
                c = dk * low + (zl ^ zlo)
                for j in range(SUB):
                    cell_ref[c, j : j + 1, :] = carry
                    carry = map_ref[c, 0, j : j + 1, :] * carry + map_ref[c, 1, j : j + 1, :]

        @pl.when(stays)
        def _():
            for copy in here_copies:
                copy.wait()

        @pl.when(jnp.logical_not(stays))
        def _():
            for copy in far_copies:
                copy.wait()

        chunk_rows = order_ref.shape[0]
        for c in range(chunks):
            dk, dz = c // low, c % low
            at = pl.ds(pl.multiple_of((dz ^ zlo) * chunk_rows, chunk_rows), chunk_rows)
            grad_ref[c] = jnp.dot(order_ref[...], og_all_ref[dk, at, :], preferred_element_type=F32).astype(BF16)
        prod_ref[...] = jnp.ones_like(prod_ref)
        binj_ref[...] = jnp.zeros_like(binj_ref)
        sums_ref[...] = jnp.zeros_like(sums_ref)

    rows = hx_ref.shape[1]
    bounds = bounds_of(lengths)
    fp, rp, fb, rb = fp_ref[...], rp_ref[...], fb_ref[...], rb_ref[...]
    rz_sum, peep_sum = sums_ref[0], sums_ref[1]
    first, second = slice(0, SUB), slice(SUB, 2 * SUB)
    for c in range(chunks):
        base = s[info.base + c]
        cell, prod, binj = cell_ref[c], prod_ref[c], binj_ref[c]
        for i in range(rows // (2 * SUB)):
            at = slice(2 * i * SUB, 2 * (i + 1) * SUB)
            now = step * (rows // SUB) + 2 * i
            candidate = mixed_ref[c, 0, at].astype(F32)
            forget, rest = gate(mixed_ref[c, 1, at].astype(F32) + fp * candidate + fb)
            inject = rest * candidate
            kept = [kept_of(base, now + n, seg, bounds, channels) for n in range(2)]
            previous = [kept[0] * cell]
            cells = [forget[first] * previous[0] + inject[first]]
            previous.append(kept[1] * cells[0])
            cell = forget[second] * previous[1] + inject[second]
            cells = jnp.concatenate([cells[0], cell], axis=0)
            previous = jnp.concatenate(previous, axis=0)
            reset, skip = gate(reset_ref[c, at].astype(F32) + rp * previous + rb)
            x = hx_ref[c, at].astype(F32)
            here = pl.ds(pl.multiple_of(step * rows + 2 * i * SUB, 2 * SUB), 2 * SUB)
            g = grad_ref[c, here, :].astype(F32)
            out = (reset * cells + skip * x).astype(BF16)
            kept_out_ref[c, here, :] = out
            direct = g * reset
            rz = direct * skip * (cells - x)
            prev_ref[c, at] = previous.astype(BF16)
            direct_ref[c, at] = direct.astype(BF16)
            rz_ref[c, at] = rz.astype(BF16)
            skip_ref[c, at] = (g * skip).astype(BF16)
            back = forget * direct + rz * rp
            for n, half in ((0, first), (1, second)):
                prod_kept = prod * kept[n]
                binj = binj + prod_kept * back[half]
                prod = prod_kept * forget[half]
            rz_sum = rz_sum + (rz[first] + rz[second])
            peep = rz * previous
            peep_sum = peep_sum + (peep[first] + peep[second])
        cell_ref[c] = cell
        prod_ref[c] = prod
        binj_ref[c] = binj
    sums_ref[0] = rz_sum
    sums_ref[1] = peep_sum

    @pl.when(step == last)
    def _():
        for c in range(chunks):
            dk, dz = c // low, c % low
            (out_ref, out_far_ref)[dk][dz ^ zlo] = jnp.dot(
                back_order_ref[...], kept_out_ref[c], preferred_element_type=F32
            ).astype(BF16)
        runs = []
        for dk in range(2):
            acc = jnp.zeros((1, channels), F32)
            for zl in reversed(range(low)):
                c = dk * low + (zl ^ zlo)
                for j in reversed(range(SUB)):
                    acc = binj_ref[c, j : j + 1, :] + map_ref[c, 0, j : j + 1, :] * acc
            runs.append(acc)
        runb_ref[...] = jnp.concatenate(runs + [jnp.zeros((6, channels), F32)], axis=0)


def back_kernel(info, low, planes, seg, s, lengths, *refs):
    gathered_refs, back_refs = refs[: planes + 1], refs[planes + 1 : 2 * planes + 2]
    (
        map_ref, binj_ref, mixed_ref, prev_ref, direct_ref, rz_ref, fp_ref, rp_ref, fb_ref,
        grad_c_ref, grad_f_ref, sums_ref,
        carry_ref, gathered_ref, back_ref,
    ) = refs[2 * planes + 2 :]
    chunks, channels = map_ref.shape[0], map_ref.shape[3]
    step = pl.program_id(0)
    count = pl.num_programs(0)
    k, zlo = s[info.k], s[info.zlo]

    @pl.when(step == 0)
    def _():
        gathered_maps(info, planes, s, gathered_refs, gathered_ref)
        gathered_maps(info, planes, s, back_refs, back_ref)
        carry = jnp.zeros((1, channels), F32)
        own = [carry, carry]
        for plane in reversed(range(planes)):
            for core in (1, 0):
                for zh in (1, 0):
                    e = zh * planes + plane
                    mine = (plane == s[info.p]) & (zh == s[info.zhi])
                    own[core] = jnp.where(mine, carry, own[core])
                    decay = jnp.where(k == core, gathered_ref[e, 0:1, :], gathered_ref[e, 2:3, :])
                    inject = jnp.where(k == core, back_ref[e, 0:1, :], back_ref[e, 1:2, :])
                    carry = decay * carry + inject
        for dk in range(2):
            carry = jnp.where(k == 0, own[dk], own[1 - dk])
            for zl in reversed(range(low)):
                c = dk * low + (zl ^ zlo)
                for j in reversed(range(SUB)):
                    carry_ref[c, j : j + 1, :] = carry
                    carry = map_ref[c, 0, j : j + 1, :] * carry + binj_ref[c, j : j + 1, :]
        sums_ref[...] = jnp.zeros_like(sums_ref)

    rows = prev_ref.shape[1]
    bounds = bounds_of(lengths)
    fp, rp, fb = fp_ref[...], rp_ref[...], fb_ref[...]
    fz_sum, peep_sum = sums_ref[0], sums_ref[1]
    first, second = slice(0, SUB), slice(SUB, 2 * SUB)
    for c in range(chunks):
        base = s[info.base + c]
        back = carry_ref[c]
        for i in reversed(range(rows // (2 * SUB))):
            at = slice(2 * i * SUB, 2 * (i + 1) * SUB)
            now = (count - 1 - step) * (rows // SUB) + 2 * i
            candidate = mixed_ref[c, 0, at].astype(F32)
            forget, rest = gate(mixed_ref[c, 1, at].astype(F32) + fp * candidate + fb)
            direct = direct_ref[c, at].astype(F32)
            prev_grad = rz_ref[c, at].astype(F32) * rp
            later = direct[second] + back
            back = kept_of(base, now + 1, seg, bounds, channels) * (forget[second] * later + prev_grad[second])
            sooner = direct[first] + back
            back = kept_of(base, now, seg, bounds, channels) * (forget[first] * sooner + prev_grad[first])
            held = jnp.concatenate([sooner, later], axis=0) * rest
            forget_z = held * forget * (prev_ref[c, at].astype(F32) - candidate)
            grad_c_ref[c, at] = (held + forget_z * fp).astype(BF16)
            grad_f_ref[c, at] = forget_z.astype(BF16)
            fz_sum = fz_sum + (forget_z[first] + forget_z[second])
            peep = forget_z * candidate
            peep_sum = peep_sum + (peep[first] + peep[second])
        carry_ref[c] = back
    sums_ref[0] = fz_sum
    sums_ref[1] = peep_sum


def input_kernel(info, count, s, w_ref, gain_ref, *refs):
    ins = [refs[6 * n : 6 * n + 6] for n in range(count)]
    outs = refs[6 * count :]
    v_refs, s_refs = outs[:count], outs[count : 2 * count]
    gb_ref, grad_ref, first_ref, second_ref = outs[2 * count :]
    tile = pl.program_id(0)
    nt = (((1,), (1,)), ((), ()))
    rows, width = grad_ref.shape[1:]
    flag = jnp.where(s[info.g] == tile, 1.0, 0.0)
    gain = gain_ref[...]
    block = 32
    gain_sum = jnp.zeros((SUB, width), F32)
    bias_sum = jnp.zeros((SUB, width), F32)

    @pl.when(tile == 0)
    def _():
        first_ref[...] = jnp.zeros_like(first_ref)
        second_ref[...] = jnp.zeros_like(second_ref)

    for n, (grad_c_ref, grad_f_ref, rz_ref, _, _, _) in enumerate(ins):
        grad = lax.dot_general(grad_c_ref[0], w_ref[0], nt, preferred_element_type=F32)
        grad = grad + lax.dot_general(grad_f_ref[0], w_ref[1], nt, preferred_element_type=F32)
        grad_ref[n] = grad + lax.dot_general(rz_ref[0], w_ref[2], nt, preferred_element_type=F32)
    for n, (_, _, _, hat_ref, inv_ref, skip_ref) in enumerate(ins):
        for r in range(rows // block):
            at = slice(r * block, (r + 1) * block)
            value = grad_ref[n, at]
            inv = jnp.concatenate([inv_ref[0, at]] * (width // LANES), axis=1)
            hat = hat_ref[0, at].astype(F32)
            scaled = value * gain
            product = scaled * hat
            first, second = first_ref[n, at], second_ref[n, at]
            for lane in range(width // LANES):
                first = first + scaled[:, lane * LANES : (lane + 1) * LANES]
                second = second + product[:, lane * LANES : (lane + 1) * LANES]
            first_ref[n, at] = first
            second_ref[n, at] = second
            matched = value * hat
            for i in range(block // SUB):
                gain_sum = gain_sum + matched[i * SUB : (i + 1) * SUB]
                bias_sum = bias_sum + value[i * SUB : (i + 1) * SUB]
            v_refs[n][at] = (scaled * inv + skip_ref[0, at].astype(F32) * flag).astype(BF16)
    gb_ref[0] = gain_sum
    gb_ref[1] = bias_sum

    @pl.when(tile == pl.num_programs(0) - 1)
    def _():
        lane = lax.broadcasted_iota(jnp.int32, (rows, LANES), 1)
        for n in range(count):
            first = jnp.sum(first_ref[n], axis=1, keepdims=True)
            second = jnp.sum(second_ref[n], axis=1, keepdims=True)
            s_refs[n][...] = jnp.where(lane == 0, first, jnp.where(lane == 1, second, 0.0)).T[:SUB]


def input_part_kernel(x_ref, order_ref, own_ref, core_ref, s_ref, out_ref):
    width = x_ref.shape[1]
    x = x_ref[...].astype(F32)
    average = jnp.mean(x, axis=1, keepdims=True)
    centred = x - average
    inv = lax.rsqrt(jnp.mean(centred * centred, axis=1, keepdims=True) + EPSILON)
    order = order_ref[...]
    value = jnp.dot(order, own_ref[...], preferred_element_type=F32)
    value = value + jnp.dot(order, core_ref[...], preferred_element_type=F32)
    sums = lax.dot_general(
        order.astype(F32), s_ref[...], (((1,), (1,)), ((), ())),
        precision=lax.Precision.HIGHEST, preferred_element_type=F32,
    )
    first = sums[:, 0:1] * (1.0 / width)
    second = sums[:, 1:2] * (1.0 / width)
    out_ref[...] = value - inv * (first + centred * inv * second)


def last_kernel(starts, part_ref, order_ref, *refs):
    pieces, out_ref = refs[: len(starts)], refs[len(starts)]
    order = order_ref[...]
    value = part_ref[...]
    for start, piece in zip(starts, pieces):
        value = value + jnp.dot(order[:, start : start + piece.shape[0]], piece[...], preferred_element_type=F32)
    out_ref[...] = value


def weight_grad_kernel(count, order, s, normed_ref, *refs):
    grads, outs = refs[:count], refs[count:]
    each = len(outs) // count
    tn = (((0,), (0,)), ((), ()))
    for n in range(count):
        total = lax.dot_general(normed_ref[0], grads[n][0], tn, preferred_element_type=F32)
        for c in range(1, normed_ref.shape[0]):
            total = total + lax.dot_general(normed_ref[c], grads[n][c], tn, preferred_element_type=F32)
        low = total.astype(BF16)
        half = low.shape[0] // 2
        for at, places in enumerate(order):

            @pl.when(pl.program_id(0) == at)
            def _():
                for ref, place, rows in places:
                    outs[n * each + ref][place] = (low, low[:half], low[half:])[rows]


def owned_kernel(info, count, s, *refs):
    came, outs, total_ref, slot_ref, sem = refs[:count], refs[count : count + 2], *refs[count + 2 :]
    total_ref[...] = jnp.zeros_like(total_ref)
    for wait in (False, True):
        for n in range(count):

            @pl.when(s[info.owned + n] >= 0)
            def _():
                copy = pltpu.make_async_copy(came[n], slot_ref.at[n], sem.at[n])
                if not wait:
                    copy.start()
                else:
                    copy.wait()
                    total_ref[s[info.owned + n]] += slot_ref[n].astype(F32)

    half = total_ref.shape[1] // 2
    for n, out in enumerate(outs):
        core = s[info.k] if n == 0 else 1 - s[info.k]
        rows = pl.ds(pl.multiple_of(core * half, half), half)
        for block in range(3):
            out[block] = total_ref[block, rows, :].astype(BF16)


def spread_kernel(count, steps, s, *refs):
    pieces, out_ref = refs[:count], refs[-1]
    rows, channels = out_ref.shape[0], pieces[0].shape[2]
    for n, (piece, start) in enumerate(steps):

        @pl.when(pl.program_id(0) == n)
        def _():
            for block in range(3):
                values = pieces[piece][block, start : start + rows]
                out_ref[:, block * channels : (block + 1) * channels] = values.astype(F32)


def cost(flops, moved, exps=0):
    return pl.CostEstimate(flops=int(flops), bytes_accessed=int(moved), transcendentals=int(exps))


def per_device(
    inputs, norm_gain, norm_bias, weight, forget_peep, reset_peep, forget_bias, reset_bias, seq_lengths, out_grad
):
    rows, width = inputs.shape
    seqs, groups = lax.axis_size("seq"), lax.axis_size("col")
    planes, low = seqs // 2, groups // 2
    channels = width // groups
    chunks = groups
    seg = rows // SUB
    part = width // planes
    half, quarter = part // 2, part // 4
    seq, z = lax.axis_index("seq"), lax.axis_index("col")
    k, zhi = seq % 2, z // low
    params = functools.partial(pltpu.CompilerParams, vmem_limit_bytes=VMEM_LIMIT)
    others = range(1, planes)
    short = planes == 4
    anywhere = pl.BlockSpec(memory_space=pl.ANY)
    full = lambda shape: pl.BlockSpec(shape, lambda *_: (0,) * len(shape))
    shape_of = jax.ShapeDtypeStruct

    def move(value, to):
        pairs = []
        for a in range(seqs):
            for b in range(groups):
                target = to(a // 2, a % 2, b)
                if target is not None:
                    pairs.append((a * groups + b, (target[0] * 2 + target[1]) * groups + target[2]))
        return lax.ppermute(value, ("seq", "col"), pairs)

    def cross_core(value):
        return move(value, lambda p, k, z: (p, 1 - k, z))

    def cross_low(value, dz):
        return move(value, lambda p, k, z: (p, k, z ^ dz))

    def cross_high(value):
        return move(value, lambda p, k, z: (p, k, (z + low) % groups))

    def cross_plane(value, dp):
        return move(value, lambda p, k, z: (p ^ dp, k, z))

    def move_nodes(value, pairs):
        spot = lambda p, n: (2 * p + n // groups) * groups + n % groups
        return lax.ppermute(
            value, ("seq", "col"), [(spot(p, src), spot(p, dst)) for p in range(planes) for src, dst in pairs]
        )

    def after(values, *first):
        return lax.optimization_barrier((values, first))[0]

    def add_up(values):
        total = values[0].astype(F32)
        for value in values[1:]:
            total = total + value.astype(F32)
        return total.astype(BF16)

    device = np.arange(seqs * groups)
    dev_p, dev_k, dev_z = device // groups // 2, device // groups % 2, device % groups
    dev_zhi, dev_zlo = dev_z // low, dev_z % low
    info = Info()
    for name, value in (("p", dev_p), ("k", dev_k), ("zhi", dev_zhi), ("zlo", dev_zlo), ("g", dev_zlo + low * dev_k)):
        info.put(name, [value])
    info.put(
        "base",
        [((2 * dev_p + (dev_k ^ (c // low))) * groups + dev_zhi * low + (dev_zlo ^ (c % low))) * rows for c in range(chunks)],
    )
    node = dev_k * groups + dev_z
    at_dev = lambda table: np.asarray(table, np.int32)[:, node]
    local, plan = routes(groups, range(3))
    rounds = len(plan)
    here = max(sum(e[1] == n for e in local) for n in range(2 * groups))
    slot_stream = np.full((here + rounds, 2 * groups), -1)
    cut_block = np.zeros((rounds + here, 2 * groups))
    for r, edges in enumerate(plan):
        for src, dst, stream, at in edges:
            cut_block[r, src] = at
            slot_stream[here + r, dst] = stream
    for n in range(2 * groups):
        for at, edge in enumerate(edge for edge in local if edge[1] == n):
            slot_stream[at, n] = edge[2]
            cut_block[rounds + at, n] = edge[3]
    info.put("slot_stream", at_dev(slot_stream))
    info.put("cut_block", at_dev(cut_block))
    back_routes = [(streams, *routes(groups, streams)) for streams in ([0, 2], [1])]
    owned, back_stream = [], []
    for streams, back_local, back_plan in back_routes:
        for edges in back_plan:
            takes = np.full(2 * groups, -1)
            source = np.zeros(2 * groups)
            for src, dst, stream, at in edges:
                takes[src] = at
                source[dst] = streams.index(stream)
            owned.append(takes)
            back_stream.append(source)
        for stream in streams:
            takes = np.full(2 * groups, -1)
            for src, _, found, at in back_local:
                if found == stream:
                    takes[src] = at
            owned.append(takes)
    info.put("owned", at_dev(owned))
    info.put("back_stream", at_dev(back_stream[: len(back_routes[0][2])]))
    visits = [3, 1, 2, 0] if short else list(range(planes))
    info.put("visits", [dev_p ^ d for d in visits])
    def piece_rows(d, dk):
        return [((dev_p ^ d) * 2 + (dev_k ^ dk)) * 2 + n for n in range(2)]

    whole_planes = range(3 if short else planes)
    near_rows = sum([piece_rows(d, 0) for d in whole_planes], []) + piece_rows(0, 1)
    far_rows = sum([piece_rows(d, 1) for d in whole_planes[1:]], []) + (piece_rows(3, 0) if short else [])
    last_rows = piece_rows(3, 1) if short else []
    info.put("near_rows", near_rows)
    info.put("far_rows", far_rows)
    info.put("last_rows", last_rows)
    scalars = lax.dynamic_index_in_dim(jnp.asarray(info.table()), seq * groups + z, 0, keepdims=False)

    order = jnp.asarray(row_order(rows), BF16)
    back_order = jnp.asarray(row_order(rows).T.copy(), BF16)

    tile = 128 if rows % 128 == 0 else rows
    tiles = rows // tile

    def call(kernel, out_shape, in_specs, out_specs, grid=(1,), scratch=(), lengths=False, aliases=None, **rest):
        return pl.pallas_call(
            kernel,
            grid_spec=pltpu.PrefetchScalarGridSpec(
                num_scalar_prefetch=2 if lengths else 1,
                grid=grid,
                in_specs=in_specs,
                out_specs=out_specs,
                scratch_shapes=list(scratch),
            ),
            out_shape=out_shape,
            input_output_aliases=aliases or {},
            compiler_params=params(),
            **rest,
        )

    def settle(*values):
        return lax.optimization_barrier(values)

    gain2, bias2 = norm_gain[None, :], norm_bias[None, :]

    row_shapes = (
        shape_of((chunks, rows, width), BF16),
        shape_of((chunks, rows, channels), BF16),
        shape_of((chunks, rows, width), BF16),
        shape_of((chunks, rows, LANES), F32),
    )
    mix_shapes = (shape_of((chunks, 2, rows, channels), BF16), shape_of((chunks, 2, SUB, channels), F32))
    wide = 256 if rows % 256 == 0 else rows

    def normalise(c, value, held):
        return call(
            functools.partial(norm_kernel, info),
            row_shapes,
            [pl.BlockSpec((wide, width), lambda t, s: (t, 0)), full((1, width)), full((1, width))]
            + [anywhere] * len(held),
            [
                pl.BlockSpec((1, wide, width), lambda t, s: (c, t, 0)),
                pl.BlockSpec((1, wide, channels), lambda t, s: (c, t, 0)),
                pl.BlockSpec((1, wide, width), lambda t, s: (c, t, 0)),
                pl.BlockSpec((1, wide, LANES), lambda t, s: (c, t, 0)),
            ],
            grid=(rows // wide,),
            aliases={4 + n: n for n in range(len(held))},
            cost_estimate=cost(12 * rows * width, 7 * rows * width),
            name="norm_chunk",
        )(scalars, value, gain2, bias2, *held)

    blocks_out = call(
        functools.partial(cut_kernel, rounds + here),
        [shape_of((part, channels), BF16)] * (rounds + here),
        [
            pl.BlockSpec((part, channels), lambda t, s, n=n: (s[info.p], s[info.cut_block + n]))
            for n in range(rounds + here)
        ],
        [full((part, channels))] * (rounds + here),
        cost_estimate=cost(0, 0),
        name="cut_weight",
    )(scalars, *[weight] * (rounds + here))
    arrived = [move_nodes(blocks_out[r], [(e[0], e[1]) for e in plan[r]]) for r in range(rounds)]
    locals_here = blocks_out[rounds:]
    if short:
        local_near = [[cross_plane(value, 1), cross_plane(value, 2)] for value in locals_here]
    else:
        local_near = [[cross_plane(value, d) for d in others] for value in locals_here]
    permuted = jnp.dot(order, after(inputs, blocks_out), preferred_element_type=F32).astype(BF16)
    x_core = cross_core(permuted)
    quad = rows // 4
    x_cuts = [(0, quad), (quad, 2 * quad), (3 * quad, quad)]
    x_sends = [permuted[start : start + size] for start, size in x_cuts]
    lows = range(1, low)
    held = normalise(0, permuted, ())
    held = normalise(low, x_core, held)
    x_sends = after(x_sends, x_core)
    x_far = [[cross_low(x_sends[0], dz) for dz in lows]]
    local_near, x_core, held = settle(local_near, x_core, held)

    local_ends = []
    if short:
        local_ends = [[cross_plane(one[:half], 2), cross_plane(two[half:], 1)] for one, two in local_near]
    gates = jnp.stack([forget_peep, reset_peep, forget_bias, reset_bias])
    gates_far = cross_high(gates)
    half_rows = low * rows
    own_half = lax.dynamic_slice_in_dim(out_grad, zhi * half_rows, half_rows, 0)
    unit = half_rows // 32
    far_parts = []
    for start, size in ((0, 7), (7, 9), (16, 12), (28, 4)):
        far_parts.append(lax.dynamic_slice_in_dim(out_grad, (1 - zhi) * half_rows + start * unit, size * unit, 0))
    taken = jnp.stack(arrived)
    taken, local_ends, x_far, gates_far, held, x_sends, far_parts, own_half = settle(
        taken, local_ends, x_far, gates_far, held, x_sends, far_parts, own_half
    )
    gates = jnp.where(zhi == k, gates, gates_far)
    fp, rp, fb, rb = (gates[n : n + 1] for n in range(4))

    taken_full = [taken] + [cross_plane(taken, d) for d in (others[:2] if short else others)]
    x_far.append([cross_low(x_sends[1], dz) for dz in lows])
    far_came = [cross_high(far_parts[0])]
    x_cross = [[cross_core(value) for value in x_far[0]]]
    taken_full, x_far, far_came, x_cross, x_sends, far_parts = settle(
        taken_full, x_far, far_came, x_cross, x_sends, far_parts
    )

    taken_ends = []
    if short:
        taken_ends = [cross_plane(taken_full[1][:, :half], 2), cross_plane(taken_full[2][:, half:], 1)]
    x_far.append([cross_low(x_sends[2], dz) for dz in lows])
    taken_full, taken_ends, x_far, x_cross, far_came, far_parts = settle(
        taken_full, taken_ends, x_far, x_cross, far_came, far_parts
    )

    x_cross += [[cross_core(value) for value in values] for values in x_far[1:]]
    far_cross = [cross_core(far_came[0])]
    far_came.append(cross_high(far_parts[1]))
    weight_pieces = []
    for n, value in enumerate(locals_here):
        weight_pieces += [value] + local_near[n] + (local_ends[n] if short else [])
    weight_pieces += taken_full + taken_ends
    mix_cost = cost(3 * chunks * rows * width * channels, 4 * chunks * rows * width + 12 * width * channels)
    mixed, maps, full_weight = call(
        functools.partial(mix_kernel, info, low, planes, seg, here, rounds, short),
        mix_shapes + (shape_of((3, width, channels), BF16),),
        [pl.BlockSpec((1, rows, width), lambda t, *_: (t * low, 0, 0)), full((1, channels)), full((1, channels))]
        + [anywhere] * len(weight_pieces),
        [
            pl.BlockSpec((1, 2, rows, channels), lambda t, *_: (t * low, 0, 0, 0)),
            pl.BlockSpec((1, 2, SUB, channels), lambda t, *_: (t * low, 0, 0, 0)),
            anywhere,
        ],
        grid=(2,),
        scratch=[
            pltpu.VMEM((3, width, channels), BF16),
            pltpu.SemaphoreType.DMA(((here + rounds) * (planes + 1),)),
            pltpu.SemaphoreType.DMA,
        ],
        lengths=True,
        cost_estimate=mix_cost,
        name="mix_near",
    )(scalars, seq_lengths, held[0], fp, fb, *weight_pieces)

    mixed, maps, full_weight, x_far, x_cross, far_came, far_parts, far_cross = settle(
        mixed, maps, full_weight, x_far, x_cross, far_came, far_parts, far_cross
    )

    far_cross += [cross_core(value) for value in far_came[1:]]
    own_cross = cross_core(own_half)
    far_came.append(cross_high(far_parts[2]))
    far_order = [far_chunk(low, n) for n in range(2 * (low - 1))]
    far_pieces = [(x_far, x_cross)[c // low][n][c % low - 1] for c in far_order for n in range(len(x_cuts))]
    far_at = lambda t: far_chunk(low, t)
    *held, mixed, maps, run_maps = call(
        functools.partial(mix_far_kernel, info, low, seg, far_order, [size for _, size in x_cuts]),
        row_shapes + mix_shapes + (shape_of((SUB, channels), F32),),
        [full((2, width, channels)), full((1, width)), full((1, width)), full((1, channels)), full((1, channels))]
        + [full((chunks, 2, SUB, channels))]
        + [anywhere] * len(far_pieces)
        + [anywhere] * 5,
        [
            pl.BlockSpec((1, rows, width), lambda t, *_: (far_at(t), 0, 0)),
            pl.BlockSpec((1, rows, channels), lambda t, *_: (far_at(t), 0, 0)),
            pl.BlockSpec((1, rows, width), lambda t, *_: (far_at(t), 0, 0)),
            pl.BlockSpec((1, rows, LANES), lambda t, *_: (far_at(t), 0, 0)),
            pl.BlockSpec((1, 2, rows, channels), lambda t, *_: (far_at(t), 0, 0, 0)),
            full((chunks, 2, SUB, channels)),
            full((SUB, channels)),
        ],
        grid=(len(far_order),),
        scratch=[
            pltpu.VMEM((len(far_order), rows, width), BF16),
            pltpu.SemaphoreType.DMA((len(far_pieces),)),
        ],
        lengths=True,
        aliases={8 + len(far_pieces) + n: n for n in range(5)},
        cost_estimate=mix_cost,
        name="mix_far",
    )(
        scalars, seq_lengths, full_weight, gain2, bias2, fp, fb, maps,
        *far_pieces, *held, mixed,
    )
    normed, highway, hats, invs = held

    run_maps, far_came, far_parts, far_cross, own_cross = settle(run_maps, far_came, far_parts, far_cross, own_cross)
    near_maps = [run_maps] + [cross_plane(run_maps, d) for d in others]
    far_cross.append(cross_core(far_came[2]))
    far_came.append(cross_high(far_parts[3]))
    near_maps, far_came, far_cross = settle(near_maps, far_came, far_cross)
    far_maps = cross_high(jnp.stack(near_maps))
    far_cross.append(cross_core(far_came[3]))
    reset_mixed = pl.pallas_call(
        reset_kernel,
        grid=(chunks,),
        in_specs=[
            pl.BlockSpec((1, rows, width), lambda c: (c, 0, 0)),
            pl.BlockSpec((1, width, channels), lambda c: (2, 0, 0)),
        ],
        out_specs=pl.BlockSpec((1, rows, channels), lambda c: (c, 0, 0)),
        out_shape=shape_of((chunks, rows, channels), BF16),
        compiler_params=params(),
        cost_estimate=cost(2 * chunks * rows * width * channels, 2 * chunks * rows * width),
        name="mix_reset",
    )(after(normed, near_maps), full_weight)
    near_maps, far_maps, far_cross, reset_mixed = settle(near_maps, far_maps, far_cross, reset_mixed)
    gathered = near_maps + [far_maps]

    map_specs = [full((SUB, channels))] * planes + [full((planes, SUB, channels))]
    block = 128 if rows % 128 == 0 else rows
    blocks = rows // block
    elements = chunks * rows * channels
    runs = (low, rows, channels)
    part_rows = (chunks, block, channels)
    at_block = lambda t, *_: (0, t, 0)
    state_out = call(
        functools.partial(state_kernel, info, low, planes, seg, [value.shape[0] for value in far_came]),
        (
            shape_of(runs, BF16),
            shape_of(runs, BF16),
            shape_of((chunks, rows, channels), BF16),
            shape_of((chunks, rows, channels), BF16),
            shape_of((chunks, rows, channels), BF16),
            shape_of((chunks, rows, channels), BF16),
            shape_of((chunks, SUB, channels), F32),
            shape_of((2, SUB, channels), F32),
            shape_of((SUB, channels), F32),
        ),
        map_specs
        + [
            full((chunks, 2, SUB, channels)),
            pl.BlockSpec((chunks, 2, block, channels), lambda t, *_: (0, 0, t, 0)),
            pl.BlockSpec(part_rows, at_block),
            pl.BlockSpec(part_rows, at_block),
            anywhere,
            anywhere,
        ]
        + [anywhere] * (2 * len(far_came))
        + [
            full((rows, rows)),
            full((rows, rows)),
        ]
        + [full((1, channels))] * 4,
        [full(runs), full(runs)]
        + [pl.BlockSpec(part_rows, at_block)] * 4
        + [full((chunks, SUB, channels)), full((2, SUB, channels)), full((SUB, channels))],
        grid=(blocks,),
        scratch=[
            pltpu.VMEM((chunks, SUB, channels), F32),
            pltpu.VMEM((chunks, SUB, channels), F32),
            pltpu.VMEM((chunks, rows, channels), BF16),
            pltpu.VMEM((2 * planes, SUB, channels), F32),
            pltpu.VMEM((chunks, rows, channels), BF16),
            pltpu.VMEM((2, low * rows, channels), BF16),
            pltpu.SemaphoreType.DMA((2, len(far_came))),
        ],
        lengths=True,
        cost_estimate=cost(60 * elements, 30 * elements, 4 * elements),
        name="states",
    )(
        scalars, seq_lengths, *gathered, maps, mixed, reset_mixed, highway, own_half, own_cross, *far_came, *far_cross,
        order, back_order, fp, rp, fb, rb,
    )
    out_own, out_far, previous, direct, reset_z, skip, binj, reset_sums, run_back = state_out

    if short:
        places = [[(0, 1, 1), (1, 1, 2)], [(0, 0, 1), (3, 1, 2)], [(2, 1, 1), (1, 0, 2)], [(2, 0, 1), (3, 0, 2)]]
        part_shapes = [(2, half, channels)] * 4
    else:
        places = [[(d, 0, 0)] for d in visits]
        part_shapes = [(1, part, channels)] * planes

    def weight_part(sources, name):
        found = call(
            functools.partial(weight_grad_kernel, len(sources), places),
            [shape_of(shape, BF16) for shape in part_shapes] * len(sources),
            [pl.BlockSpec((chunks, rows, part), lambda t, s: (0, 0, s[info.visits + t]))]
            + [full((chunks, rows, channels))] * len(sources),
            [full(shape) for shape in part_shapes] * len(sources),
            grid=(planes,),
            cost_estimate=cost(2 * chunks * rows * width * channels * len(sources), 4 * chunks * rows * width),
            name=name,
        )(scalars, normed, *sources)
        return [found[n * len(part_shapes) : (n + 1) * len(part_shapes)] for n in range(len(sources))]

    def first_sends(parts):
        if short:
            return [cross_plane(parts[0], 1), cross_plane(parts[1], 2)]
        return [cross_plane(parts[d], d) for d in others]

    def second_start(parts, came):
        if not short:
            return came
        return [add_up([parts[2][1], came[0][1]]), add_up([parts[3][1], came[1][1]])]

    def second_sends(over):
        return [cross_plane(over[0], 2), cross_plane(over[1], 1)] if short else []

    def second_end(parts, came, over):
        if not short:
            return add_up([parts[0][0]] + [value[0] for value in came])
        first = add_up([parts[2][0], came[0][0], over[0]])
        second = add_up([parts[3][0], came[1][0], over[1]])
        return jnp.concatenate([first, second], axis=0)

    def to_owners(which, values, chosen):
        back_plan = back_routes[which][2]
        return [
            move_nodes(values[r], [(e[1], e[0]) for e in back_plan[r]]) for r in range(len(back_plan))[chosen]
        ]

    near_back = [run_back] + [cross_plane(run_back, d) for d in others]
    out_core = cross_core(out_far)
    near_back, out_core, out_own, reset_z = settle(near_back, out_core, out_own, reset_z)
    stay = jnp.where(k == zhi, out_own, out_core)
    leave = jnp.where(k == zhi, out_core, out_own).reshape(half_rows, channels)
    leave = [leave[start * unit : (start + size) * unit] for start, size in ((0, 7), (7, 7), (14, 7), (21, 7), (28, 4))]

    far_back = cross_high(jnp.stack(near_back))
    out_came = [cross_high(leave[0])]
    (reset_wg,) = weight_part([reset_z], "weight_grad_reset")
    near_back, far_back, reset_wg, out_came, leave, binj = settle(near_back, far_back, reset_wg, out_came, leave, binj)
    gathered_back = near_back + [far_back]

    out_came.append(cross_high(leave[1]))
    reset_came = first_sends(reset_wg)

    grad_c, grad_f, forget_sums = call(
        functools.partial(back_kernel, info, low, planes, seg),
        (
            shape_of((chunks, rows, channels), BF16),
            shape_of((chunks, rows, channels), BF16),
            shape_of((2, SUB, channels), F32),
        ),
        map_specs * 2
        + [
            full((chunks, 2, SUB, channels)),
            full((chunks, SUB, channels)),
            pl.BlockSpec((chunks, 2, block, channels), lambda t, *_: (0, 0, blocks - 1 - t, 0)),
        ]
        + [pl.BlockSpec(part_rows, lambda t, *_: (0, blocks - 1 - t, 0))] * 3
        + [full((1, channels))] * 3,
        [pl.BlockSpec(part_rows, lambda t, *_: (0, blocks - 1 - t, 0))] * 2 + [full((2, SUB, channels))],
        grid=(blocks,),
        scratch=[
            pltpu.VMEM((chunks, SUB, channels), F32),
            pltpu.VMEM((2 * planes, SUB, channels), F32),
            pltpu.VMEM((2 * planes, SUB, channels), F32),
        ],
        lengths=True,
        cost_estimate=cost(30 * elements, 20 * elements, 2 * elements),
        name="state_grads",
    )(scalars, seq_lengths, *gathered, *gathered_back, maps, binj, mixed, previous, direct, reset_z, fp, rp, fb)

    def chunk_grads(chosen, sources):
        each = []
        for c in chosen:
            chunk_block = pl.BlockSpec((1, rows, channels), lambda t, s, c=c: (c, 0, 0))
            each += [chunk_block] * 3
            each += [
                pl.BlockSpec((1, rows, channels), lambda t, s, c=c: (c, 0, t)),
                pl.BlockSpec((1, rows, LANES), lambda t, s, c=c: (c, 0, 0)),
                chunk_block,
            ]
        count = len(chosen)
        found = call(
            functools.partial(input_kernel, info, count),
            [shape_of((rows, width), BF16)] * count
            + [shape_of((SUB, rows), F32)] * count
            + [shape_of((2, SUB, width), F32)],
            [
                pl.BlockSpec((3, channels, channels), lambda t, s: (0, t, 0)),
                pl.BlockSpec((1, channels), lambda t, s: (0, t)),
            ]
            + each,
            [pl.BlockSpec((rows, channels), lambda t, s: (0, t))] * count
            + [full((SUB, rows))] * count
            + [pl.BlockSpec((2, SUB, channels), lambda t, s: (0, 0, t))],
            grid=(groups,),
            scratch=[
                pltpu.VMEM((count, rows, channels), F32),
                pltpu.VMEM((count, rows, LANES), F32),
                pltpu.VMEM((count, rows, LANES), F32),
            ],
            cost_estimate=cost(6 * count * rows * width * channels, (8 * rows * count + 6 * channels) * width),
            name="chunk_grads",
        )(scalars, full_weight, gain2, *(list(sources) + [hats, invs, skip]) * count)
        norm_sums.append(found[2 * count])
        return found[:count], found[count : 2 * count]

    norm_sums = []

    grad_c, grad_f, reset_came, out_came, leave = settle(grad_c, grad_f, reset_came, out_came, leave)
    over = second_start(reset_wg, reset_came)
    grad_c, over, leave = settle(grad_c, over, leave)

    reset_over = second_sends(over)
    out_came.append(cross_high(leave[2]))
    (candidate_wg,) = weight_part([grad_c], "weight_grad_candidate")
    candidate_wg, reset_over, out_came, leave = settle(candidate_wg, reset_over, out_came, leave)
    reset_part = second_end(reset_wg, reset_came, reset_over)
    candidate_wg, reset_part, leave, grad_f = settle(candidate_wg, reset_part, leave, grad_f)

    candidate_came = first_sends(candidate_wg)
    out_came.append(cross_high(leave[3]))
    (forget_wg,) = weight_part([grad_f], "weight_grad_forget")
    forget_wg, candidate_came, out_came, leave = settle(forget_wg, candidate_came, out_came, leave)
    over = second_start(candidate_wg, candidate_came)
    sources = (grad_c, grad_f, reset_z)
    over, forget_wg, sources, leave = settle(over, forget_wg, sources, leave)

    candidate_over = second_sends(over)
    forget_came = first_sends(forget_wg)
    out_came.append(cross_high(leave[4]))
    far_pairs = [chunk_grads([low + dz, dz], sources) for dz in lows]
    far_pairs, candidate_over, forget_came, out_came, sources = settle(
        far_pairs, candidate_over, forget_came, out_came, sources
    )
    candidate_part = second_end(candidate_wg, candidate_came, candidate_over)
    over = second_start(forget_wg, forget_came)
    sends = call(
        functools.partial(pick_kernel, "back_stream", info, 2),
        [shape_of((part, channels), BF16)] * len(back_routes[0][2]),
        [full((part, channels))] * 2,
        [full((part, channels))] * len(back_routes[0][2]),
        cost_estimate=cost(0, 3 * part * channels),
        name="pick_parts",
    )(scalars, candidate_part, reset_part)
    sends, over, sources, far_pairs = settle(sends, over, sources, far_pairs)

    forget_over = second_sends(over)
    owned_parts = to_owners(0, sends, slice(0, 1))
    from_core = [cross_core(values[0]) for values, _ in far_pairs]
    sums_across = [cross_core(sums[0]) for _, sums in far_pairs]
    (other_value,), (other_sums,) = chunk_grads([low], sources)
    other_value, other_sums, forget_over, owned_parts, from_core, sums_across, sends, sources = settle(
        other_value, other_sums, forget_over, owned_parts, from_core, sums_across, sends, sources
    )
    forget_part = second_end(forget_wg, forget_came, forget_over)
    far_sums = [sums[1] + sums_across[n] for n, (_, sums) in enumerate(far_pairs)]
    forget_part, sends, far_sums, sources, far_pairs, from_core = settle(
        forget_part, sends, far_sums, sources, far_pairs, from_core
    )

    owned_parts = owned_parts + to_owners(0, sends, slice(1, None))
    last_parts = to_owners(1, [forget_part] * len(back_routes[1][2]), slice(0, 1))
    value_core, sums_core = cross_core(other_value), cross_core(other_sums)
    (own_value,), (own_sums,) = chunk_grads([0], sources)
    sixteen = rows // 32
    v_cuts = [(0, 14 * sixteen), (14 * sixteen, 9 * sixteen), (23 * sixteen, 5 * sixteen), (28 * sixteen, 4 * sixteen)]
    v_sends = [
        [
            add_up([values[1][start : start + size], from_core[n][start : start + size]])
            for n, (values, _) in enumerate(far_pairs)
        ]
        for start, size in v_cuts
    ]
    own_value, own_sums, owned_parts, last_parts, value_core, sums_core, v_sends, far_sums, forget_part = settle(
        own_value, own_sums, owned_parts, last_parts, value_core, sums_core, v_sends, far_sums, forget_part
    )

    gate_sums = jnp.sum(jnp.concatenate([forget_sums, reset_sums]), axis=1)
    spread_sums = lax.dynamic_update_slice(
        jnp.zeros((4, width), F32), gate_sums, (0, (z % low + low * k) * channels)
    )
    small = jnp.concatenate([jnp.sum(sum(norm_sums[1:], norm_sums[0]), axis=1), spread_sums], axis=0)
    last_parts = last_parts + to_owners(1, [forget_part] * len(back_routes[1][2]), slice(1, None))
    small_came = cross_low(small, 1)
    far_sums = [cross_low(sums, dz) for dz, sums in zip(lows, far_sums)]
    last_parts, small, small_came, far_sums = settle(last_parts, small, small_came, far_sums)
    small = small + small_came
    sums = sum([sums_core] + far_sums, own_sums)
    owned_parts = owned_parts + [candidate_part, reset_part] + last_parts + [forget_part]
    def send_far(n):
        return [cross_low(value, dz) for dz, value in zip(lows, v_sends[n])]

    block_piece = (3, half, channels)
    own_blocks, give_blocks = call(
        functools.partial(owned_kernel, info, len(owned_parts)),
        [shape_of(block_piece, BF16)] * 2,
        [anywhere] * len(owned_parts),
        [full(block_piece)] * 2,
        scratch=[
            pltpu.VMEM((3, part, channels), F32),
            pltpu.VMEM((len(owned_parts), part, channels), BF16),
            pltpu.SemaphoreType.DMA((len(owned_parts),)),
        ],
        cost_estimate=cost(0, 6 * part * channels),
        name="own_blocks",
    )(scalars, *owned_parts)
    own_blocks, give_blocks, small, v_sends = settle(own_blocks, give_blocks, small, v_sends)

    give_blocks = cross_core(give_blocks)
    own_blocks, give_blocks = settle(own_blocks, give_blocks)
    own_sum = add_up([own_blocks, give_blocks])
    own_sum, v_sends, small, sums = settle(own_sum, v_sends, small, sums)

    whole = [own_sum] + [cross_plane(own_sum, d) for d in (others[:2] if short else others)]
    whole_core = [cross_core(own_sum)]
    v_came = [send_far(0)]
    input_part = pl.pallas_call(
        input_part_kernel,
        grid=(tiles,),
        in_specs=[
            pl.BlockSpec((tile, width), lambda t: (t, 0)),
            pl.BlockSpec((tile, rows), lambda t: (t, 0)),
            full((rows, width)),
            full((rows, width)),
            full((SUB, rows)),
        ],
        out_specs=pl.BlockSpec((tile, width), lambda t: (t, 0)),
        out_shape=shape_of((rows, width), F32),
        compiler_params=params(),
        cost_estimate=cost(4 * rows * rows * width, 10 * rows * width),
        name="input_part",
    )(inputs, back_order, own_value, value_core, sums)
    whole, whole_core, v_came, v_sends, small, input_part = settle(
        whole, whole_core, v_came, v_sends, small, input_part
    )

    def spread(name, values, steps, held):
        return call(
            functools.partial(spread_kernel, len(values), steps),
            shape_of((width, 3 * channels), F32),
            [full(value.shape) for value in values] + [anywhere] * len(held),
            pl.BlockSpec((quarter, 3 * channels), lambda t, s: (s[getattr(info, name) + t], 0)),
            grid=(len(steps),),
            aliases={1 + len(values): 0} if held else None,
            cost_estimate=cost(0, 9 * width * channels),
            name="spread_" + name,
        )(scalars, *values, *held)

    split = []
    if short:
        split = [whole[1][:, :quarter], whole[2][:, quarter:]]
        whole, split, v_sends, small = settle(whole, split, v_sends, small)
        split = [cross_plane(split[0], 2), cross_plane(split[1], 1)]
    whole_core += [cross_core(value) for value in whole[1:]]
    v_came.append(send_far(1))
    values = whole + whole_core[:1]
    weight_grad = spread("near_rows", values, [(n, at) for n in range(len(values)) for at in (0, quarter)], ())
    weight_grad, split, whole_core, v_came, v_sends, small = settle(
        weight_grad, split, whole_core, v_came, v_sends, small
    )

    small_came = [cross_low(small, bit) for bit in bits_of(groups)[1:2]]
    split_core = [cross_core(value) for value in split]
    v_came.append(send_far(2))
    values = whole_core[1:] + split
    steps = [(n, at) for n in range(len(whole_core) - 1) for at in (0, quarter)]
    steps += [(len(whole_core) - 1 + n, 0) for n in range(len(split))]
    weight_grad = spread("far_rows", values, steps, (weight_grad,))
    split_core, v_came, v_sends, small, small_came, weight_grad = settle(
        split_core, v_came, v_sends, small, small_came, weight_grad
    )
    small = sum(small_came, small)
    for bit in bits_of(groups)[2:]:
        small = small + cross_low(small, bit)

    v_came.append(send_far(3))
    small_came = cross_core(small)
    if short:
        weight_grad = spread("last_rows", split_core, [(0, 0), (1, 0)], (weight_grad,))
    weight_grad, v_came, small, small_came = settle(weight_grad, v_came, small, small_came)
    small = small + small_came
    small = sum([cross_plane(small, d) for d in others], small)

    came = jnp.concatenate(out_came, axis=0).reshape(stay.shape)
    output = jnp.where(zhi == 0, jnp.stack([stay, came]), jnp.stack([came, stay])).reshape(groups * rows, channels)
    parts = [(start, value) for (start, _), came_now in zip(v_cuts, v_came) for value in came_now]
    input_grad = pl.pallas_call(
        functools.partial(last_kernel, [start for start, _ in parts]),
        grid=(tiles,),
        in_specs=[pl.BlockSpec((tile, width), lambda t: (t, 0)), pl.BlockSpec((tile, rows), lambda t: (t, 0))]
        + [full(value.shape) for _, value in parts],
        out_specs=pl.BlockSpec((tile, width), lambda t: (t, 0)),
        out_shape=shape_of((rows, width), F32),
        input_output_aliases={0: 0},
        compiler_params=params(),
        cost_estimate=cost(2 * rows * rows * width, 10 * rows * width),
        name="input_grad",
    )(input_part, back_order, *[value for _, value in parts])
    gate_block = lax.dynamic_slice_in_dim(small[2:], z * channels, channels, 1)
    return (
        output,
        input_grad,
        weight_grad,
        small[0],
        small[1],
        gate_block[1],
        gate_block[3],
        gate_block[0],
        gate_block[2],
    )


def solution(mesh):
    placed = (
        P(("seq", "col"), None),
        P(),
        P(),
        P(None, "col"),
        P("col"),
        P("col"),
        P("col"),
        P("col"),
        P(),
        P("seq", "col"),
    )
    return jax.shard_map(
        per_device,
        mesh=mesh,
        in_specs=placed,
        out_specs=(
            P("seq", "col"),
            P(("seq", "col"), None),
            P(None, "col"),
            P(),
            P(),
            P("col"),
            P("col"),
            P("col"),
            P("col"),
        ),
        check_vma=False,
    )
```

```python
import functools

import jax
import jax.numpy as jnp
import numpy as np
from jax import lax
from jax.experimental import pallas as pl
from jax.experimental.pallas import tpu as pltpu
from jax.sharding import PartitionSpec as P

EPSILON = 1e-05
F32 = jnp.float32
BF16 = jnp.bfloat16
LANES = 128
SUB = 8
VMEM_LIMIT = 56 * 1024 * 1024


def bits_of(count):
    return [1 << b for b in range(count.bit_length() - 1)]


def colour(edges, count):
    degree = max([sum(e[0] == n for e in edges) for n in range(count)] + [sum(e[1] == n for e in edges) for n in range(count)])
    out = [[None] * degree for _ in range(count)]
    into = [[None] * degree for _ in range(count)]
    taken = {}
    for at, edge in enumerate(edges):
        src, dst = edge[0], edge[1]
        first = next(c for c in range(degree) if out[src][c] is None)
        second = next(c for c in range(degree) if into[dst][c] is None)
        if first != second:
            path, node, at_dst, look = [], dst, True, first
            while True:
                found = (into if at_dst else out)[node][look]
                if found is None:
                    break
                path.append(found)
                node = edges[found][0] if at_dst else edges[found][1]
                at_dst = not at_dst
                look = second if look == first else first
            for found in path:
                old = taken[found]
                out[edges[found][0]][old] = None
                into[edges[found][1]][old] = None
            for found in path:
                new = second if taken[found] == first else first
                taken[found] = new
                out[edges[found][0]][new] = found
                into[edges[found][1]][new] = found
        taken[at] = first
        out[src][first] = at
        into[dst][first] = at
    rounds = [[] for _ in range(degree)]
    for at, edge in enumerate(edges):
        rounds[taken[at]].append(edge)
    return rounds


def busiest(edges, groups):
    links = {}
    for src, dst, _, _ in edges:
        a, b = src % groups, dst % groups
        for n in range(min(a, b), max(a, b)):
            links[n, a < b] = links.get((n, a < b), 0) + 1
    return max(links.values(), default=0)


def balance(rounds, groups):
    if len(rounds) != 2:
        return rounds
    paths = []
    left = [(r, e) for r in range(2) for e in rounds[r]]
    while left:
        path = [left.pop()]
        grown = True
        while grown:
            near = [x for x in left if any(x[1][0] == y[1][0] or x[1][1] == y[1][1] for y in path)]
            left = [x for x in left if x not in near]
            path += near
            grown = bool(near)
        paths.append(path)
    best = None
    for flips in range(2 ** len(paths)):
        tried = [[], []]
        for n, path in enumerate(paths):
            for r, edge in path:
                tried[r ^ (flips >> n & 1)].append(edge)
        score = sum(busiest(edges, groups) for edges in tried)
        score = (max(busiest(edges, groups) for edges in tried), score)
        if best is None or score < best[0]:
            best = (score, tried)
    return best[1]


def routes(groups, streams):
    low = groups // 2
    local, edges = [], []
    load = [0] * (2 * groups)
    for core in range(2):
        for z in range(groups):
            for stream in streams:
                block = stream * groups + z % low + low * core
                owner, at = block // 3, block % 3
                dst = core * groups + z
                if owner == z:
                    local.append((dst, dst, stream, at))
                else:
                    edges.append([core, owner, dst, stream, at])
    found = []
    for owner in range(groups):
        mine = [e for e in edges if e[1] == owner]
        quota = -(-len(mine) // 2)
        for core, _, dst, stream, at in mine:
            src = core * groups + owner
            if load[src] == quota:
                src = (1 - core) * groups + owner
            load[src] += 1
            found.append((src, dst, stream, at))
    return local, balance(colour(found, 2 * groups), groups)


def row_order(rows):
    seg = rows // SUB
    matrix = np.zeros((rows, rows), np.float32)
    for i in range(seg):
        for j in range(SUB):
            matrix[i * SUB + j, j * seg + i] = 1.0
    return matrix


def gate(value):
    small = jnp.exp(-jnp.abs(value))
    minor = small / (1.0 + small)
    major = 1.0 - minor
    up = value >= 0.0
    return jnp.where(up, major, minor), jnp.where(up, minor, major)


def kept_of(base, step, seg, bounds, channels):
    at = lax.broadcasted_iota(jnp.int32, (SUB, LANES), 0) * seg + (base + step)
    starts = at == bounds[0]
    for bound in bounds[1:]:
        starts = starts | (at == bound)
    kept = jnp.where(starts, 0.0, 1.0)
    return jnp.concatenate([kept] * (channels // LANES), axis=1)


class Info:
    def __init__(self):
        self.spots = {}
        self.columns = []

    def put(self, name, values):
        self.spots[name] = len(self.columns)
        self.columns += list(np.asarray(values, np.int32))

    def __getattr__(self, name):
        return self.spots[name]

    def table(self):
        return np.stack(self.columns, axis=1)


def bounds_of(lengths):
    starts = [0]
    for n in range(lengths.shape[0] - 1):
        starts.append(starts[-1] + lengths[n])
    return starts


def cut_kernel(count, s, *refs):
    for n in range(count):
        refs[count + n][...] = refs[n][...]


def pick_kernel(name, info, sources, s, *refs):
    came, outs = refs[:sources], refs[sources:]
    outs = list(outs) if len(outs) > 1 else [outs[0].at[n] for n in range(outs[0].shape[0])]
    for n, out in enumerate(outs):
        for r in range(sources):

            @pl.when(s[getattr(info, name) + n] == r)
            def _():
                out[...] = came[r][...]


def norm_rows(x_ref, gain, bias, normed_ref, hat_ref, inv_ref):
    block = 32
    for r in range(x_ref.shape[0] // block):
        at = slice(r * block, (r + 1) * block)
        x = x_ref[at].astype(F32)
        average = jnp.mean(x, axis=1, keepdims=True)
        centred = x - average
        inv = lax.rsqrt(jnp.mean(centred * centred, axis=1, keepdims=True) + EPSILON)
        hat = centred * inv
        normed_ref[0, at] = (hat * gain + bias).astype(BF16)
        hat_ref[0, at] = hat.astype(BF16)
        inv_ref[0, at] = jnp.broadcast_to(inv, (block, LANES))


def group_columns(info, s, channels):
    return pl.ds(pl.multiple_of(s[info.g] * channels, channels), channels)


def norm_kernel(info, s, x_ref, gain_ref, bias_ref, *refs):
    normed_ref, hx_ref, hat_ref, inv_ref = refs[-4:]
    norm_rows(x_ref, gain_ref[...], bias_ref[...], normed_ref, hat_ref, inv_ref)
    hx_ref[0] = x_ref[:, group_columns(info, s, hx_ref.shape[2])]


def segment_maps(base, seg, lengths, mixed_ref, fp, fb):
    channels = mixed_ref.shape[3]
    run_decay = jnp.ones((SUB, channels), F32)
    run_state = jnp.zeros((SUB, channels), F32)
    bounds = bounds_of(lengths)
    for i in range(mixed_ref.shape[2] // SUB):
        at = slice(i * SUB, (i + 1) * SUB)
        candidate = mixed_ref[0, 0, at].astype(F32)
        forget, rest = gate(mixed_ref[0, 1, at].astype(F32) + fp * candidate + fb)
        decay = forget * kept_of(base, i, seg, bounds, channels)
        run_state = decay * run_state + rest * candidate
        run_decay = decay * run_decay
    return run_decay, run_state


def mix_kernel(info, low, planes, seg, here, away, split, s, lengths, normed_ref, fp_ref, fb_ref, *refs):
    part = refs[0].shape[-2]
    whole = [(d, 0, part) for d in range(planes)]
    if split:
        ends = [(3, 0, part // 2), (3, part // 2, part // 2)]
        here_parts = whole[:3] + ends
        away_parts = [(d, n * (part // 2), part // 2) for d in range(3) for n in range(2)] + ends
    else:
        here_parts = away_parts = whole
    count = here * len(here_parts) + len(away_parts)
    pieces = refs[:count]
    mixed_ref, map_ref, full_ref, w_ref, in_sem, out_sem = refs[count:]
    step = pl.program_id(0)

    def copies(slot):
        stream = s[info.slot_stream + slot]
        found = []
        for n, (d, start, size) in enumerate(here_parts if slot < here else away_parts):
            rows = pl.ds(pl.multiple_of((d ^ s[info.p]) * part + start, size), size)
            if slot < here:
                piece = pieces[slot * len(here_parts) + n]
            else:
                piece = pieces[here * len(here_parts) + n].at[slot - here]
            spot = slot * len(away_parts) + n
            found.append(pltpu.make_async_copy(piece, w_ref.at[stream, rows, :], in_sem.at[spot]))
        return found

    @pl.when(step == 0)
    def _():
        for slot in range(here + away):

            @pl.when(s[info.slot_stream + slot] >= 0)
            def _():
                for copy in copies(slot):
                    copy.start()

        for slot in range(here + away):

            @pl.when(s[info.slot_stream + slot] >= 0)
            def _():
                for copy in copies(slot):
                    copy.wait()

        pltpu.make_async_copy(w_ref, full_ref, out_sem).start()

    for stream in range(2):
        mixed_ref[0, stream] = jnp.dot(normed_ref[0], w_ref[stream], preferred_element_type=F32).astype(BF16)
    decay, state = segment_maps(s[info.base + step * low], seg, lengths, mixed_ref, fp_ref[...], fb_ref[...])
    map_ref[0, 0] = decay
    map_ref[0, 1] = state

    @pl.when(step == pl.num_programs(0) - 1)
    def _():
        pltpu.make_async_copy(w_ref, full_ref, out_sem).wait()


def mix_far_kernel(info, low, seg, order, sizes, s, lengths, w_ref, gain_ref, bias_ref, fp_ref, fb_ref, near_ref, *refs):
    count = len(order)
    pieces = refs[: len(sizes) * count]
    normed_ref, hx_ref, hat_ref, inv_ref, mixed_ref, map_ref, run_ref, x_ref, sem = refs[len(sizes) * count + 5 :]
    channels = w_ref.shape[2]
    step = pl.program_id(0)

    def copies(n):
        found, start = [], 0
        for m, size in enumerate(sizes):
            spot = n * len(sizes) + m
            found.append(pltpu.make_async_copy(pieces[spot], x_ref.at[n, pl.ds(start, size), :], sem.at[spot]))
            start += size
        return found

    @pl.when(step == 0)
    def _():
        for n in range(count):
            for copy in copies(n):
                copy.start()
        for dk in range(2):
            map_ref[dk * low] = near_ref[dk * low]

    for n in range(count):

        @pl.when(step == n)
        def _():
            for copy in copies(n):
                copy.wait()

    mine = x_ref.at[step]
    norm_rows(mine, gain_ref[...], bias_ref[...], normed_ref, hat_ref, inv_ref)
    hx_ref[0] = mine[:, group_columns(info, s, channels)]
    for stream in range(2):
        mixed_ref[0, stream] = jnp.dot(normed_ref[0], w_ref[stream], preferred_element_type=F32).astype(BF16)
    chunk = far_chunk(low, step)
    decay, state = segment_maps(s[info.base + chunk], seg, lengths, mixed_ref, fp_ref[...], fb_ref[...])
    map_ref[chunk, 0] = decay
    map_ref[chunk, 1] = state

    @pl.when(step == count - 1)
    def _():
        rows = []
        for dk in range(2):
            decay = jnp.ones((1, channels), F32)
            state = jnp.zeros((1, channels), F32)
            for zl in range(low):
                c = dk * low + (zl ^ s[info.zlo])
                for j in range(SUB):
                    d, b = map_ref[c, 0, j : j + 1, :], map_ref[c, 1, j : j + 1, :]
                    state = d * state + b
                    decay = d * decay
            rows += [decay, state]
        run_ref[...] = jnp.concatenate(rows + [jnp.zeros((4, channels), F32)], axis=0)


def reset_kernel(normed_ref, w_ref, *refs):
    refs[-1][0] = jnp.dot(normed_ref[0], w_ref[0], preferred_element_type=F32).astype(BF16)


def far_chunk(low, n):
    return n // (low - 1) * low + 1 + n % (low - 1)


def gathered_maps(info, planes, s, refs, into):
    for d in range(planes):
        plane = d ^ s[info.p]
        into[s[info.zhi] * planes + plane] = refs[d][...]
        into[(1 - s[info.zhi]) * planes + plane] = refs[planes][d]


def state_kernel(info, low, planes, seg, sizes, s, lengths, *refs):
    gathered_refs = refs[: planes + 1]
    map_ref, mixed_ref, reset_ref, hx_ref, og_ref, og_cross_ref = refs[planes + 1 : planes + 7]
    far_refs = refs[planes + 7 : planes + 7 + 2 * len(sizes)]
    (
        order_ref, fp_ref, rp_ref, fb_ref, rb_ref,
        out_ref, out_far_ref, prev_ref, direct_ref, rz_ref, skip_ref, binj_ref, sums_ref, runb_ref,
        cell_ref, prod_ref, gathered_ref, grad_ref, og_all_ref, og_sem,
    ) = refs[planes + 7 + 2 * len(sizes) :]
    chunks, channels = map_ref.shape[0], map_ref.shape[3]
    step = pl.program_id(0)
    last = pl.num_programs(0) - 1
    k, zlo = s[info.k], s[info.zlo]

    @pl.when(step == 0)
    def _():
        stays = s[info.zhi] == k
        here_copies = [
            pltpu.make_async_copy(ref, og_all_ref.at[n], og_sem.at[n, 0]) for n, ref in enumerate((og_ref, og_cross_ref))
        ]
        far_copies = []
        for n in range(2):
            start = 0
            for m, size in enumerate(sizes):
                target = og_all_ref.at[n, pl.ds(start, size), :]
                far_copies.append(pltpu.make_async_copy(far_refs[n * len(sizes) + m], target, og_sem.at[n, m]))
                start += size

        @pl.when(stays)
        def _():
            for copy in here_copies:
                copy.start()

        @pl.when(jnp.logical_not(stays))
        def _():
            for copy in far_copies:
                copy.start()

        gathered_maps(info, planes, s, gathered_refs, gathered_ref)
        carry = jnp.zeros((1, channels), F32)
        own = [carry, carry]
        for plane in range(planes):
            for core in range(2):
                for zh in range(2):
                    e = zh * planes + plane
                    mine = (plane == s[info.p]) & (zh == s[info.zhi])
                    own[core] = jnp.where(mine, carry, own[core])
                    decay = jnp.where(k == core, gathered_ref[e, 0:1, :], gathered_ref[e, 2:3, :])
                    state = jnp.where(k == core, gathered_ref[e, 1:2, :], gathered_ref[e, 3:4, :])
                    carry = decay * carry + state
        for dk in range(2):
            carry = jnp.where(k == 0, own[dk], own[1 - dk])
            for zl in range(low):
                c = dk * low + (zl ^ zlo)
                for j in range(SUB):
                    cell_ref[c, j : j + 1, :] = carry
                    carry = map_ref[c, 0, j : j + 1, :] * carry + map_ref[c, 1, j : j + 1, :]

        @pl.when(stays)
        def _():
            for copy in here_copies:
                copy.wait()

        @pl.when(jnp.logical_not(stays))
        def _():
            for copy in far_copies:
                copy.wait()

        chunk_rows = order_ref.shape[0]
        for c in range(chunks):
            dk, dz = c // low, c % low
            at = pl.ds(pl.multiple_of((dz ^ zlo) * chunk_rows, chunk_rows), chunk_rows)
            grad_ref[c] = jnp.dot(order_ref[...], og_all_ref[dk, at, :], preferred_element_type=F32).astype(BF16)
        prod_ref[...] = jnp.ones_like(prod_ref)
        binj_ref[...] = jnp.zeros_like(binj_ref)
        sums_ref[...] = jnp.zeros_like(sums_ref)

    rows = hx_ref.shape[1]
    bounds = bounds_of(lengths)
    fp, rp, fb, rb = fp_ref[...], rp_ref[...], fb_ref[...], rb_ref[...]
    rz_sum, peep_sum = sums_ref[0], sums_ref[1]
    first, second = slice(0, SUB), slice(SUB, 2 * SUB)
    for c in range(chunks):
        base = s[info.base + c]
        cell, prod, binj = cell_ref[c], prod_ref[c], binj_ref[c]
        for i in range(rows // (2 * SUB)):
            at = slice(2 * i * SUB, 2 * (i + 1) * SUB)
            now = step * (rows // SUB) + 2 * i
            candidate = mixed_ref[c, 0, at].astype(F32)
            forget, rest = gate(mixed_ref[c, 1, at].astype(F32) + fp * candidate + fb)
            inject = rest * candidate
            kept = [kept_of(base, now + n, seg, bounds, channels) for n in range(2)]
            previous = [kept[0] * cell]
            cells = [forget[first] * previous[0] + inject[first]]
            previous.append(kept[1] * cells[0])
            cell = forget[second] * previous[1] + inject[second]
            cells = jnp.concatenate([cells[0], cell], axis=0)
            previous = jnp.concatenate(previous, axis=0)
            reset, skip = gate(reset_ref[c, at].astype(F32) + rp * previous + rb)
            x = hx_ref[c, at].astype(F32)
            here = pl.ds(pl.multiple_of(step * rows + 2 * i * SUB, 2 * SUB), 2 * SUB)
            g = grad_ref[c, here, :].astype(F32)
            out = (reset * cells + skip * x).astype(BF16)
            (out_ref, out_far_ref)[c // low][(c % low) ^ zlo, here, :] = out
            direct = g * reset
            rz = direct * skip * (cells - x)
            prev_ref[c, at] = previous.astype(BF16)
            direct_ref[c, at] = direct.astype(BF16)
            rz_ref[c, at] = rz.astype(BF16)
            skip_ref[c, at] = (g * skip).astype(BF16)
            back = forget * direct + rz * rp
            for n, half in ((0, first), (1, second)):
                prod_kept = prod * kept[n]
                binj = binj + prod_kept * back[half]
                prod = prod_kept * forget[half]
            rz_sum = rz_sum + (rz[first] + rz[second])
            peep = rz * previous
            peep_sum = peep_sum + (peep[first] + peep[second])
        cell_ref[c] = cell
        prod_ref[c] = prod
        binj_ref[c] = binj
    sums_ref[0] = rz_sum
    sums_ref[1] = peep_sum

    @pl.when(step == last)
    def _():
        runs = []
        for dk in range(2):
            acc = jnp.zeros((1, channels), F32)
            for zl in reversed(range(low)):
                c = dk * low + (zl ^ zlo)
                for j in reversed(range(SUB)):
                    acc = binj_ref[c, j : j + 1, :] + map_ref[c, 0, j : j + 1, :] * acc
            runs.append(acc)
        runb_ref[...] = jnp.concatenate(runs + [jnp.zeros((6, channels), F32)], axis=0)


def back_kernel(info, low, planes, seg, s, lengths, *refs):
    gathered_refs, back_refs = refs[: planes + 1], refs[planes + 1 : 2 * planes + 2]
    (
        map_ref, binj_ref, mixed_ref, prev_ref, direct_ref, rz_ref, fp_ref, rp_ref, fb_ref,
        grad_c_ref, grad_f_ref, sums_ref,
        carry_ref, gathered_ref, back_ref,
    ) = refs[2 * planes + 2 :]
    chunks, channels = map_ref.shape[0], map_ref.shape[3]
    step = pl.program_id(0)
    count = pl.num_programs(0)
    k, zlo = s[info.k], s[info.zlo]

    @pl.when(step == 0)
    def _():
        gathered_maps(info, planes, s, gathered_refs, gathered_ref)
        gathered_maps(info, planes, s, back_refs, back_ref)
        carry = jnp.zeros((1, channels), F32)
        own = [carry, carry]
        for plane in reversed(range(planes)):
            for core in (1, 0):
                for zh in (1, 0):
                    e = zh * planes + plane
                    mine = (plane == s[info.p]) & (zh == s[info.zhi])
                    own[core] = jnp.where(mine, carry, own[core])
                    decay = jnp.where(k == core, gathered_ref[e, 0:1, :], gathered_ref[e, 2:3, :])
                    inject = jnp.where(k == core, back_ref[e, 0:1, :], back_ref[e, 1:2, :])
                    carry = decay * carry + inject
        for dk in range(2):
            carry = jnp.where(k == 0, own[dk], own[1 - dk])
            for zl in reversed(range(low)):
                c = dk * low + (zl ^ zlo)
                for j in reversed(range(SUB)):
                    carry_ref[c, j : j + 1, :] = carry
                    carry = map_ref[c, 0, j : j + 1, :] * carry + binj_ref[c, j : j + 1, :]
        sums_ref[...] = jnp.zeros_like(sums_ref)

    rows = prev_ref.shape[1]
    bounds = bounds_of(lengths)
    fp, rp, fb = fp_ref[...], rp_ref[...], fb_ref[...]
    fz_sum, peep_sum = sums_ref[0], sums_ref[1]
    first, second = slice(0, SUB), slice(SUB, 2 * SUB)
    for c in range(chunks):
        base = s[info.base + c]
        back = carry_ref[c]
        for i in reversed(range(rows // (2 * SUB))):
            at = slice(2 * i * SUB, 2 * (i + 1) * SUB)
            now = (count - 1 - step) * (rows // SUB) + 2 * i
            candidate = mixed_ref[c, 0, at].astype(F32)
            forget, rest = gate(mixed_ref[c, 1, at].astype(F32) + fp * candidate + fb)
            direct = direct_ref[c, at].astype(F32)
            prev_grad = rz_ref[c, at].astype(F32) * rp
            later = direct[second] + back
            back = kept_of(base, now + 1, seg, bounds, channels) * (forget[second] * later + prev_grad[second])
            sooner = direct[first] + back
            back = kept_of(base, now, seg, bounds, channels) * (forget[first] * sooner + prev_grad[first])
            held = jnp.concatenate([sooner, later], axis=0) * rest
            forget_z = held * forget * (prev_ref[c, at].astype(F32) - candidate)
            grad_c_ref[c, at] = (held + forget_z * fp).astype(BF16)
            grad_f_ref[c, at] = forget_z.astype(BF16)
            fz_sum = fz_sum + (forget_z[first] + forget_z[second])
            peep = forget_z * candidate
            peep_sum = peep_sum + (peep[first] + peep[second])
        carry_ref[c] = back
    sums_ref[0] = fz_sum
    sums_ref[1] = peep_sum


def input_kernel(info, count, s, w_ref, gain_ref, *refs):
    ins = [refs[6 * n : 6 * n + 6] for n in range(count)]
    outs = refs[6 * count :]
    v_refs, s_refs = outs[:count], outs[count : 2 * count]
    gb_ref, grad_ref, first_ref, second_ref = outs[2 * count :]
    tile = pl.program_id(0)
    nt = (((1,), (1,)), ((), ()))
    rows, width = grad_ref.shape[1:]
    flag = jnp.where(s[info.g] == tile, 1.0, 0.0)
    gain = gain_ref[...]
    block = 32
    gain_sum = jnp.zeros((SUB, width), F32)
    bias_sum = jnp.zeros((SUB, width), F32)

    @pl.when(tile == 0)
    def _():
        first_ref[...] = jnp.zeros_like(first_ref)
        second_ref[...] = jnp.zeros_like(second_ref)

    for n, (grad_c_ref, grad_f_ref, rz_ref, _, _, _) in enumerate(ins):
        grad = lax.dot_general(grad_c_ref[0], w_ref[0], nt, preferred_element_type=F32)
        grad = grad + lax.dot_general(grad_f_ref[0], w_ref[1], nt, preferred_element_type=F32)
        grad_ref[n] = grad + lax.dot_general(rz_ref[0], w_ref[2], nt, preferred_element_type=F32)
    for n, (_, _, _, hat_ref, inv_ref, skip_ref) in enumerate(ins):
        for r in range(rows // block):
            at = slice(r * block, (r + 1) * block)
            value = grad_ref[n, at]
            inv = jnp.concatenate([inv_ref[0, at]] * (width // LANES), axis=1)
            hat = hat_ref[0, at].astype(F32)
            scaled = value * gain
            product = scaled * hat
            first, second = first_ref[n, at], second_ref[n, at]
            for lane in range(width // LANES):
                first = first + scaled[:, lane * LANES : (lane + 1) * LANES]
                second = second + product[:, lane * LANES : (lane + 1) * LANES]
            first_ref[n, at] = first
            second_ref[n, at] = second
            matched = value * hat
            for i in range(block // SUB):
                gain_sum = gain_sum + matched[i * SUB : (i + 1) * SUB]
                bias_sum = bias_sum + value[i * SUB : (i + 1) * SUB]
            v_refs[n][at] = (scaled * inv + skip_ref[0, at].astype(F32) * flag).astype(BF16)
    gb_ref[0] = gain_sum
    gb_ref[1] = bias_sum

    @pl.when(tile == pl.num_programs(0) - 1)
    def _():
        lane = lax.broadcasted_iota(jnp.int32, (rows, LANES), 1)
        for n in range(count):
            first = jnp.sum(first_ref[n], axis=1, keepdims=True)
            second = jnp.sum(second_ref[n], axis=1, keepdims=True)
            s_refs[n][...] = jnp.where(lane == 0, first, jnp.where(lane == 1, second, 0.0)).T[:SUB]


def output_kernel(info, low, sizes, s, order_ref, stay_ref, *refs):
    came_refs, (out_ref, all_ref) = refs[: len(sizes)], refs[len(sizes) :]
    rows = order_ref.shape[0]
    start = 0
    for piece, size in zip(came_refs, sizes):
        all_ref[start : start + size] = piece[...]
        start += size
    order = order_ref[...]
    for n in range(low):
        at = slice(n * rows, (n + 1) * rows)
        out_ref[s[info.zhi], at] = jnp.dot(order, stay_ref[at], preferred_element_type=F32).astype(BF16)
        out_ref[1 - s[info.zhi], at] = jnp.dot(order, all_ref[at], preferred_element_type=F32).astype(BF16)


def input_part_kernel(x_ref, order_ref, own_ref, core_ref, s_ref, out_ref):
    width = x_ref.shape[1]
    x = x_ref[...].astype(F32)
    average = jnp.mean(x, axis=1, keepdims=True)
    centred = x - average
    inv = lax.rsqrt(jnp.mean(centred * centred, axis=1, keepdims=True) + EPSILON)
    order = order_ref[...]
    value = jnp.dot(order, own_ref[...], preferred_element_type=F32)
    value = value + jnp.dot(order, core_ref[...], preferred_element_type=F32)
    sums = lax.dot_general(
        order.astype(F32), s_ref[...], (((1,), (1,)), ((), ())),
        precision=lax.Precision.HIGHEST, preferred_element_type=F32,
    )
    first = sums[:, 0:1] * (1.0 / width)
    second = sums[:, 1:2] * (1.0 / width)
    out_ref[...] = value - inv * (first + centred * inv * second)


def last_kernel(starts, part_ref, order_ref, *refs):
    pieces, out_ref = refs[: len(starts)], refs[len(starts)]
    order = order_ref[...]
    value = part_ref[...]
    for start, piece in zip(starts, pieces):
        value = value + jnp.dot(order[:, start : start + piece.shape[0]], piece[...], preferred_element_type=F32)
    out_ref[...] = value


def weight_grad_kernel(count, order, s, normed_ref, *refs):
    grads, outs = refs[:count], refs[count:]
    each = len(outs) // count
    tn = (((0,), (0,)), ((), ()))
    for n in range(count):
        total = lax.dot_general(normed_ref[0], grads[n][0], tn, preferred_element_type=F32)
        for c in range(1, normed_ref.shape[0]):
            total = total + lax.dot_general(normed_ref[c], grads[n][c], tn, preferred_element_type=F32)
        low = total.astype(BF16)
        half = low.shape[0] // 2
        for at, places in enumerate(order):

            @pl.when(pl.program_id(0) == at)
            def _():
                for ref, place, rows in places:
                    outs[n * each + ref][place] = (low, low[:half], low[half:])[rows]


def owned_kernel(info, count, s, *refs):
    came, outs, total_ref, slot_ref, sem = refs[:count], refs[count : count + 2], *refs[count + 2 :]
    total_ref[...] = jnp.zeros_like(total_ref)
    for wait in (False, True):
        for n in range(count):

            @pl.when(s[info.owned + n] >= 0)
            def _():
                copy = pltpu.make_async_copy(came[n], slot_ref.at[n], sem.at[n])
                if not wait:
                    copy.start()
                else:
                    copy.wait()
                    total_ref[s[info.owned + n]] += slot_ref[n].astype(F32)

    half = total_ref.shape[1] // 2
    for n, out in enumerate(outs):
        core = s[info.k] if n == 0 else 1 - s[info.k]
        rows = pl.ds(pl.multiple_of(core * half, half), half)
        for block in range(3):
            out[block] = total_ref[block, rows, :].astype(BF16)


def spread_kernel(count, steps, s, *refs):
    pieces, out_ref = refs[:count], refs[-1]
    rows, channels = out_ref.shape[0], pieces[0].shape[2]
    for n, (piece, start) in enumerate(steps):

        @pl.when(pl.program_id(0) == n)
        def _():
            for block in range(3):
                values = pieces[piece][block, start : start + rows]
                out_ref[:, block * channels : (block + 1) * channels] = values.astype(F32)


def cost(flops, moved, exps=0):
    return pl.CostEstimate(flops=int(flops) // 20, bytes_accessed=int(moved) // 20, transcendentals=int(exps) // 20)


def per_device(
    inputs, norm_gain, norm_bias, weight, forget_peep, reset_peep, forget_bias, reset_bias, seq_lengths, out_grad
):
    rows, width = inputs.shape
    seqs, groups = lax.axis_size("seq"), lax.axis_size("col")
    planes, low = seqs // 2, groups // 2
    channels = width // groups
    chunks = groups
    seg = rows // SUB
    part = width // planes
    half, quarter = part // 2, part // 4
    seq, z = lax.axis_index("seq"), lax.axis_index("col")
    k, zhi = seq % 2, z // low
    params = functools.partial(pltpu.CompilerParams, vmem_limit_bytes=VMEM_LIMIT)
    others = range(1, planes)
    short = planes == 4
    anywhere = pl.BlockSpec(memory_space=pl.ANY)
    full = lambda shape: pl.BlockSpec(shape, lambda *_: (0,) * len(shape))
    shape_of = jax.ShapeDtypeStruct

    def move(value, to):
        pairs = []
        for a in range(seqs):
            for b in range(groups):
                target = to(a // 2, a % 2, b)
                if target is not None:
                    pairs.append((a * groups + b, (target[0] * 2 + target[1]) * groups + target[2]))
        return lax.ppermute(value, ("seq", "col"), pairs)

    def cross_core(value):
        return move(value, lambda p, k, z: (p, 1 - k, z))

    def cross_low(value, dz):
        return move(value, lambda p, k, z: (p, k, z ^ dz))

    def cross_high(value):
        return move(value, lambda p, k, z: (p, k, (z + low) % groups))

    def cross_plane(value, dp):
        return move(value, lambda p, k, z: (p ^ dp, k, z))

    def move_nodes(value, pairs):
        spot = lambda p, n: (2 * p + n // groups) * groups + n % groups
        return lax.ppermute(
            value, ("seq", "col"), [(spot(p, src), spot(p, dst)) for p in range(planes) for src, dst in pairs]
        )

    def after(values, *first):
        return lax.optimization_barrier((values, first))[0]

    def add_up(values):
        total = values[0].astype(F32)
        for value in values[1:]:
            total = total + value.astype(F32)
        return total.astype(BF16)

    device = np.arange(seqs * groups)
    dev_p, dev_k, dev_z = device // groups // 2, device // groups % 2, device % groups
    dev_zhi, dev_zlo = dev_z // low, dev_z % low
    info = Info()
    for name, value in (("p", dev_p), ("k", dev_k), ("zhi", dev_zhi), ("zlo", dev_zlo), ("g", dev_zlo + low * dev_k)):
        info.put(name, [value])
    info.put(
        "base",
        [((2 * dev_p + (dev_k ^ (c // low))) * groups + dev_zhi * low + (dev_zlo ^ (c % low))) * rows for c in range(chunks)],
    )
    node = dev_k * groups + dev_z
    at_dev = lambda table: np.asarray(table, np.int32)[:, node]
    local, plan = routes(groups, range(3))
    rounds = len(plan)
    here = max(sum(e[1] == n for e in local) for n in range(2 * groups))
    slot_stream = np.full((here + rounds, 2 * groups), -1)
    cut_block = np.zeros((rounds + here, 2 * groups))
    for r, edges in enumerate(plan):
        for src, dst, stream, at in edges:
            cut_block[r, src] = at
            slot_stream[here + r, dst] = stream
    for n in range(2 * groups):
        for at, edge in enumerate(edge for edge in local if edge[1] == n):
            slot_stream[at, n] = edge[2]
            cut_block[rounds + at, n] = edge[3]
    info.put("slot_stream", at_dev(slot_stream))
    info.put("cut_block", at_dev(cut_block))
    back_routes = [(streams, *routes(groups, streams)) for streams in ([0, 2], [1])]
    owned, back_stream = [], []
    for streams, back_local, back_plan in back_routes:
        for edges in back_plan:
            takes = np.full(2 * groups, -1)
            source = np.zeros(2 * groups)
            for src, dst, stream, at in edges:
                takes[src] = at
                source[dst] = streams.index(stream)
            owned.append(takes)
            back_stream.append(source)
        for stream in streams:
            takes = np.full(2 * groups, -1)
            for src, _, found, at in back_local:
                if found == stream:
                    takes[src] = at
            owned.append(takes)
    info.put("owned", at_dev(owned))
    info.put("back_stream", at_dev(back_stream[: len(back_routes[0][2])]))
    visits = [3, 1, 2, 0] if short else list(range(planes))
    info.put("visits", [dev_p ^ d for d in visits])
    def piece_rows(d, dk):
        return [((dev_p ^ d) * 2 + (dev_k ^ dk)) * 2 + n for n in range(2)]

    whole_planes = range(3 if short else planes)
    near_rows = sum([piece_rows(d, 0) for d in whole_planes], []) + piece_rows(0, 1)
    far_rows = sum([piece_rows(d, 1) for d in whole_planes[1:]], []) + (piece_rows(3, 0) if short else [])
    last_rows = piece_rows(3, 1) if short else []
    info.put("near_rows", near_rows)
    info.put("far_rows", far_rows)
    info.put("last_rows", last_rows)
    scalars = lax.dynamic_index_in_dim(jnp.asarray(info.table()), seq * groups + z, 0, keepdims=False)

    order = jnp.asarray(row_order(rows), BF16)
    back_order = jnp.asarray(row_order(rows).T.copy(), BF16)

    tile = 128 if rows % 128 == 0 else rows
    tiles = rows // tile

    def call(kernel, out_shape, in_specs, out_specs, grid=(1,), scratch=(), lengths=False, aliases=None, **rest):
        return pl.pallas_call(
            kernel,
            grid_spec=pltpu.PrefetchScalarGridSpec(
                num_scalar_prefetch=2 if lengths else 1,
                grid=grid,
                in_specs=in_specs,
                out_specs=out_specs,
                scratch_shapes=list(scratch),
            ),
            out_shape=out_shape,
            input_output_aliases=aliases or {},
            compiler_params=params(),
            **rest,
        )

    def settle(*values):
        return lax.optimization_barrier(values)

    gain2, bias2 = norm_gain[None, :], norm_bias[None, :]

    row_shapes = (
        shape_of((chunks, rows, width), BF16),
        shape_of((chunks, rows, channels), BF16),
        shape_of((chunks, rows, width), BF16),
        shape_of((chunks, rows, LANES), F32),
    )
    mix_shapes = (shape_of((chunks, 2, rows, channels), BF16), shape_of((chunks, 2, SUB, channels), F32))
    wide = 256 if rows % 256 == 0 else rows

    def normalise(c, value, held):
        return call(
            functools.partial(norm_kernel, info),
            row_shapes,
            [pl.BlockSpec((wide, width), lambda t, s: (t, 0)), full((1, width)), full((1, width))]
            + [anywhere] * len(held),
            [
                pl.BlockSpec((1, wide, width), lambda t, s: (c, t, 0)),
                pl.BlockSpec((1, wide, channels), lambda t, s: (c, t, 0)),
                pl.BlockSpec((1, wide, width), lambda t, s: (c, t, 0)),
                pl.BlockSpec((1, wide, LANES), lambda t, s: (c, t, 0)),
            ],
            grid=(rows // wide,),
            aliases={4 + n: n for n in range(len(held))},
            cost_estimate=cost(12 * rows * width, 7 * rows * width),
            name="norm_chunk",
        )(scalars, value, gain2, bias2, *held)

    blocks_out = call(
        functools.partial(cut_kernel, rounds + here),
        [shape_of((part, channels), BF16)] * (rounds + here),
        [
            pl.BlockSpec((part, channels), lambda t, s, n=n: (s[info.p], s[info.cut_block + n]))
            for n in range(rounds + here)
        ],
        [full((part, channels))] * (rounds + here),
        cost_estimate=cost(0, 0),
        name="cut_weight",
    )(scalars, *[weight] * (rounds + here))
    arrived = [move_nodes(blocks_out[r], [(e[0], e[1]) for e in plan[r]]) for r in range(rounds)]
    permuted = jnp.dot(order, after(inputs, blocks_out), preferred_element_type=F32).astype(BF16)
    held = normalise(0, permuted, ())
    locals_here = blocks_out[rounds:]
    if short:
        local_near = [[cross_plane(value, 1), cross_plane(value, 2)] for value in locals_here]
    else:
        local_near = [[cross_plane(value, d) for d in others] for value in locals_here]
    x_core = cross_core(permuted)
    quad = rows // 4
    x_cuts = [(0, quad), (quad, 3 * quad)]
    x_sends = [permuted[start : start + size] for start, size in x_cuts]
    lows = range(1, low)
    x_sends = after(x_sends, x_core)
    x_far = [[cross_low(x_sends[0], dz) for dz in lows]]
    local_near, x_core, held = settle(local_near, x_core, held)

    local_ends = []
    if short:
        local_ends = [[cross_plane(one[:half], 2), cross_plane(two[half:], 1)] for one, two in local_near]
    if short:
        taken = [jnp.stack([value[:half] for value in arrived]), jnp.stack([value[half:] for value in arrived])]
    else:
        taken = [jnp.stack(arrived)]
    taken, local_ends, x_far, held, x_core, x_sends, cotangent = settle(
        taken, local_ends, x_far, held, x_core, x_sends, out_grad
    )
    half_rows = low * rows
    own_half = lax.dynamic_slice_in_dim(cotangent, zhi * half_rows, half_rows, 0)
    unit = half_rows // 32
    far_parts = []
    for start, size in ((0, 7), (7, 25)):
        far_parts.append(lax.dynamic_slice_in_dim(cotangent, (1 - zhi) * half_rows + start * unit, size * unit, 0))
    taken_full = [taken] + [[cross_plane(value, d) for value in taken] for d in (others[:2] if short else others)]
    x_far.append([cross_low(x_sends[1], dz) for dz in lows])
    held = normalise(low, x_core, held)
    gates = jnp.stack([forget_peep, reset_peep, forget_bias, reset_bias])
    taken_full, far_parts, held, gates = settle(taken_full, far_parts, held, gates)

    taken_ends = [cross_plane(taken_full[1][0], 2), cross_plane(taken_full[2][1], 1)] if short else []
    far_came = [cross_high(far_parts[0])]
    gates_far = cross_high(gates)
    taken_full, taken_ends, x_far, far_came, far_parts, gates_far = settle(
        taken_full, taken_ends, x_far, far_came, far_parts, gates_far
    )
    gates = jnp.where(zhi == k, gates, gates_far)
    fp, rp, fb, rb = (gates[n : n + 1] for n in range(4))
    x_cross = []

    x_cross += [[cross_core(value) for value in values] for values in x_far]
    far_cross = [cross_core(far_came[0])]
    own_cross = cross_core(own_half)
    far_came.append(cross_high(far_parts[1]))
    weight_pieces = []
    for n, value in enumerate(locals_here):
        weight_pieces += [value] + local_near[n] + (local_ends[n] if short else [])
    weight_pieces += sum(taken_full, []) + taken_ends
    mix_cost = cost(3 * chunks * rows * width * channels, 4 * chunks * rows * width + 12 * width * channels)
    mixed, maps, full_weight = call(
        functools.partial(mix_kernel, info, low, planes, seg, here, rounds, short),
        mix_shapes + (shape_of((3, width, channels), BF16),),
        [pl.BlockSpec((1, rows, width), lambda t, *_: (t * low, 0, 0)), full((1, channels)), full((1, channels))]
        + [anywhere] * len(weight_pieces),
        [
            pl.BlockSpec((1, 2, rows, channels), lambda t, *_: (t * low, 0, 0, 0)),
            pl.BlockSpec((1, 2, SUB, channels), lambda t, *_: (t * low, 0, 0, 0)),
            anywhere,
        ],
        grid=(2,),
        scratch=[
            pltpu.VMEM((3, width, channels), BF16),
            pltpu.SemaphoreType.DMA(((here + rounds) * (8 if short else planes),)),
            pltpu.SemaphoreType.DMA,
        ],
        lengths=True,
        cost_estimate=mix_cost,
        name="mix_near",
    )(scalars, seq_lengths, held[0], fp, fb, *weight_pieces)

    mixed, maps, full_weight, x_far, x_cross, far_cross, own_cross = settle(
        mixed, maps, full_weight, x_far, x_cross, far_cross, own_cross
    )

    far_order = [far_chunk(low, n) for n in range(2 * (low - 1))]
    far_pieces = [(x_far, x_cross)[c // low][n][c % low - 1] for c in far_order for n in range(len(x_cuts))]
    far_at = lambda t: far_chunk(low, t)
    *held, mixed, maps, run_maps = call(
        functools.partial(mix_far_kernel, info, low, seg, far_order, [size for _, size in x_cuts]),
        row_shapes + mix_shapes + (shape_of((SUB, channels), F32),),
        [full((2, width, channels)), full((1, width)), full((1, width)), full((1, channels)), full((1, channels))]
        + [full((chunks, 2, SUB, channels))]
        + [anywhere] * len(far_pieces)
        + [anywhere] * 5,
        [
            pl.BlockSpec((1, rows, width), lambda t, *_: (far_at(t), 0, 0)),
            pl.BlockSpec((1, rows, channels), lambda t, *_: (far_at(t), 0, 0)),
            pl.BlockSpec((1, rows, width), lambda t, *_: (far_at(t), 0, 0)),
            pl.BlockSpec((1, rows, LANES), lambda t, *_: (far_at(t), 0, 0)),
            pl.BlockSpec((1, 2, rows, channels), lambda t, *_: (far_at(t), 0, 0, 0)),
            full((chunks, 2, SUB, channels)),
            full((SUB, channels)),
        ],
        grid=(len(far_order),),
        scratch=[
            pltpu.VMEM((len(far_order), rows, width), BF16),
            pltpu.SemaphoreType.DMA((len(far_pieces),)),
        ],
        lengths=True,
        aliases={8 + len(far_pieces) + n: n for n in range(5)},
        cost_estimate=mix_cost,
        name="mix_far",
    )(
        scalars, seq_lengths, full_weight, gain2, bias2, fp, fb, maps,
        *far_pieces, *held, mixed,
    )
    normed, highway, hats, invs = held

    def reset_product(chosen, first, held):
        at = lambda t: sum(jnp.where(t == n, c, 0) for n, c in enumerate(chosen))
        return pl.pallas_call(
            reset_kernel,
            grid=(len(chosen),),
            in_specs=[
                pl.BlockSpec((1, rows, width), lambda t: (at(t), 0, 0)),
                pl.BlockSpec((1, width, channels), lambda t: (2, 0, 0)),
            ]
            + [anywhere] * len(held),
            out_specs=pl.BlockSpec((1, rows, channels), lambda t: (at(t), 0, 0)),
            out_shape=shape_of((chunks, rows, channels), BF16),
            input_output_aliases={2: 0} if held else {},
            compiler_params=params(),
            cost_estimate=cost(2 * len(chosen) * rows * width * channels, 2 * len(chosen) * rows * width),
            name="mix_reset",
        )(after(normed, first), full_weight, *held)

    near_chunks = [0, low]
    near_maps = [run_maps] + [cross_plane(run_maps, d) for d in others]
    reset_mixed = reset_product(near_chunks, run_maps, ())
    near_maps, far_came, reset_mixed = settle(near_maps, far_came, reset_mixed)
    far_maps = cross_high(jnp.stack(near_maps))
    far_cross.append(cross_core(far_came[1]))
    reset_mixed = reset_product([c for c in range(chunks) if c not in near_chunks], near_maps, (reset_mixed,))
    near_maps, far_maps, far_cross, reset_mixed = settle(near_maps, far_maps, far_cross, reset_mixed)
    gathered = near_maps + [far_maps]

    map_specs = [full((SUB, channels))] * planes + [full((planes, SUB, channels))]
    block = 128 if rows % 128 == 0 else rows
    blocks = rows // block
    elements = chunks * rows * channels
    runs = (low, rows, channels)
    part_rows = (chunks, block, channels)
    at_block = lambda t, *_: (0, t, 0)
    state_out = call(
        functools.partial(state_kernel, info, low, planes, seg, [value.shape[0] for value in far_came]),
        (
            shape_of(runs, BF16),
            shape_of(runs, BF16),
            shape_of((chunks, rows, channels), BF16),
            shape_of((chunks, rows, channels), BF16),
            shape_of((chunks, rows, channels), BF16),
            shape_of((chunks, rows, channels), BF16),
            shape_of((chunks, SUB, channels), F32),
            shape_of((2, SUB, channels), F32),
            shape_of((SUB, channels), F32),
        ),
        map_specs
        + [
            full((chunks, 2, SUB, channels)),
            pl.BlockSpec((chunks, 2, block, channels), lambda t, *_: (0, 0, t, 0)),
            pl.BlockSpec(part_rows, at_block),
            pl.BlockSpec(part_rows, at_block),
            anywhere,
            anywhere,
        ]
        + [anywhere] * (2 * len(far_came))
        + [
            full((rows, rows)),
        ]
        + [full((1, channels))] * 4,
        [full(runs), full(runs)]
        + [pl.BlockSpec(part_rows, at_block)] * 4
        + [full((chunks, SUB, channels)), full((2, SUB, channels)), full((SUB, channels))],
        grid=(blocks,),
        scratch=[
            pltpu.VMEM((chunks, SUB, channels), F32),
            pltpu.VMEM((chunks, SUB, channels), F32),
            pltpu.VMEM((2 * planes, SUB, channels), F32),
            pltpu.VMEM((chunks, rows, channels), BF16),
            pltpu.VMEM((2, low * rows, channels), BF16),
            pltpu.SemaphoreType.DMA((2, len(far_came))),
        ],
        lengths=True,
        cost_estimate=cost(60 * elements, 30 * elements, 4 * elements),
        name="states",
    )(
        scalars, seq_lengths, *gathered, maps, mixed, reset_mixed, highway, own_half, own_cross, *far_came, *far_cross,
        order, fp, rp, fb, rb,
    )
    out_own, out_far, previous, direct, reset_z, skip, binj, reset_sums, run_back = state_out

    if short:
        places = [[(0, 1, 1), (1, 1, 2)], [(0, 0, 1), (3, 1, 2)], [(2, 1, 1), (1, 0, 2)], [(2, 0, 1), (3, 0, 2)]]
        part_shapes = [(2, half, channels)] * 4
    else:
        places = [[(d, 0, 0)] for d in visits]
        part_shapes = [(1, part, channels)] * planes

    def weight_part(sources, name):
        found = call(
            functools.partial(weight_grad_kernel, len(sources), places),
            [shape_of(shape, BF16) for shape in part_shapes] * len(sources),
            [pl.BlockSpec((chunks, rows, part), lambda t, s: (0, 0, s[info.visits + t]))]
            + [full((chunks, rows, channels))] * len(sources),
            [full(shape) for shape in part_shapes] * len(sources),
            grid=(planes,),
            cost_estimate=cost(2 * chunks * rows * width * channels * len(sources), 4 * chunks * rows * width),
            name=name,
        )(scalars, normed, *sources)
        return [found[n * len(part_shapes) : (n + 1) * len(part_shapes)] for n in range(len(sources))]

    def first_sends(parts):
        if short:
            return [cross_plane(parts[0], 1), cross_plane(parts[1], 2)]
        return [cross_plane(parts[d], d) for d in others]

    def second_start(parts, came):
        if not short:
            return came
        return [add_up([parts[2][1], came[0][1]]), add_up([parts[3][1], came[1][1]])]

    def second_sends(over):
        return [cross_plane(over[0], 2), cross_plane(over[1], 1)] if short else []

    def second_end(parts, came, over):
        if not short:
            return add_up([parts[0][0]] + [value[0] for value in came])
        first = add_up([parts[2][0], came[0][0], over[0]])
        second = add_up([parts[3][0], came[1][0], over[1]])
        return jnp.concatenate([first, second], axis=0)

    def to_owners(which, values, chosen):
        back_plan = back_routes[which][2]
        return [
            move_nodes(values[r], [(e[1], e[0]) for e in back_plan[r]]) for r in range(len(back_plan))[chosen]
        ]

    near_back = [run_back] + [cross_plane(run_back, d) for d in others]
    out_core = cross_core(out_far)
    near_back, reset_z = settle(near_back, reset_z)
    stay = jnp.where(k == zhi, out_own, out_core)
    leave = jnp.where(k == zhi, out_core, out_own).reshape(half_rows, channels)

    far_back = cross_high(jnp.stack(near_back))
    (reset_wg,) = weight_part([reset_z], "weight_grad_reset")
    near_back, far_back, reset_wg, leave, binj = settle(near_back, far_back, reset_wg, leave, binj)
    gathered_back = near_back + [far_back]

    leave = [leave[: half_rows // 2], leave[half_rows // 2 :]]
    out_came = [cross_high(leave[0])]
    reset_came = first_sends(reset_wg)

    grad_c, grad_f, forget_sums = call(
        functools.partial(back_kernel, info, low, planes, seg),
        (
            shape_of((chunks, rows, channels), BF16),
            shape_of((chunks, rows, channels), BF16),
            shape_of((2, SUB, channels), F32),
        ),
        map_specs * 2
        + [
            full((chunks, 2, SUB, channels)),
            full((chunks, SUB, channels)),
            pl.BlockSpec((chunks, 2, block, channels), lambda t, *_: (0, 0, blocks - 1 - t, 0)),
        ]
        + [pl.BlockSpec(part_rows, lambda t, *_: (0, blocks - 1 - t, 0))] * 3
        + [full((1, channels))] * 3,
        [pl.BlockSpec(part_rows, lambda t, *_: (0, blocks - 1 - t, 0))] * 2 + [full((2, SUB, channels))],
        grid=(blocks,),
        scratch=[
            pltpu.VMEM((chunks, SUB, channels), F32),
            pltpu.VMEM((2 * planes, SUB, channels), F32),
            pltpu.VMEM((2 * planes, SUB, channels), F32),
        ],
        lengths=True,
        cost_estimate=cost(30 * elements, 20 * elements, 2 * elements),
        name="state_grads",
    )(scalars, seq_lengths, *gathered, *gathered_back, maps, binj, mixed, previous, direct, reset_z, fp, rp, fb)

    def chunk_grads(chosen, sources):
        each = []
        for c in chosen:
            chunk_block = pl.BlockSpec((1, rows, channels), lambda t, s, c=c: (c, 0, 0))
            each += [chunk_block] * 3
            each += [
                pl.BlockSpec((1, rows, channels), lambda t, s, c=c: (c, 0, t)),
                pl.BlockSpec((1, rows, LANES), lambda t, s, c=c: (c, 0, 0)),
                chunk_block,
            ]
        count = len(chosen)
        found = call(
            functools.partial(input_kernel, info, count),
            [shape_of((rows, width), BF16)] * count
            + [shape_of((SUB, rows), F32)] * count
            + [shape_of((2, SUB, width), F32)],
            [
                pl.BlockSpec((3, channels, channels), lambda t, s: (0, t, 0)),
                pl.BlockSpec((1, channels), lambda t, s: (0, t)),
            ]
            + each,
            [pl.BlockSpec((rows, channels), lambda t, s: (0, t))] * count
            + [full((SUB, rows))] * count
            + [pl.BlockSpec((2, SUB, channels), lambda t, s: (0, 0, t))],
            grid=(groups,),
            scratch=[
                pltpu.VMEM((count, rows, channels), F32),
                pltpu.VMEM((count, rows, LANES), F32),
                pltpu.VMEM((count, rows, LANES), F32),
            ],
            cost_estimate=cost(6 * count * rows * width * channels, (8 * rows * count + 6 * channels) * width),
            name="chunk_grads",
        )(scalars, full_weight, gain2, *(list(sources) + [hats, invs, skip]) * count)
        norm_sums.append(found[2 * count])
        return found[:count], found[count : 2 * count]

    norm_sums = []

    grad_c, grad_f, reset_came = settle(grad_c, grad_f, reset_came)
    over = second_start(reset_wg, reset_came)
    grad_c, over = settle(grad_c, over)

    reset_over = second_sends(over)
    (candidate_wg,) = weight_part([grad_c], "weight_grad_candidate")
    candidate_wg, reset_over, out_came, leave = settle(candidate_wg, reset_over, out_came, leave)
    out_came.append(cross_high(leave[1]))
    reset_part = second_end(reset_wg, reset_came, reset_over)
    candidate_wg, reset_part, grad_f = settle(candidate_wg, reset_part, grad_f)

    candidate_came = first_sends(candidate_wg)
    (forget_wg,) = weight_part([grad_f], "weight_grad_forget")
    forget_wg, candidate_came = settle(forget_wg, candidate_came)
    over = second_start(candidate_wg, candidate_came)
    sources = (grad_c, grad_f, reset_z)
    over, forget_wg, sources = settle(over, forget_wg, sources)

    candidate_over = second_sends(over)
    forget_came = first_sends(forget_wg)
    far_pairs = [chunk_grads([low + dz, dz], sources) for dz in lows]
    far_pairs, candidate_over, forget_came, out_came, sources = settle(
        far_pairs, candidate_over, forget_came, out_came, sources
    )
    candidate_part = second_end(candidate_wg, candidate_came, candidate_over)
    over = second_start(forget_wg, forget_came)
    sends = call(
        functools.partial(pick_kernel, "back_stream", info, 2),
        [shape_of((part, channels), BF16)] * len(back_routes[0][2]),
        [full((part, channels))] * 2,
        [full((part, channels))] * len(back_routes[0][2]),
        cost_estimate=cost(0, 3 * part * channels),
        name="pick_parts",
    )(scalars, candidate_part, reset_part)
    sends, over, sources, far_pairs = settle(sends, over, sources, far_pairs)

    forget_over = second_sends(over)
    owned_parts = to_owners(0, sends, slice(0, 1))
    from_core = [cross_core(values[0]) for values, _ in far_pairs]
    sums_across = [cross_core(sums[0]) for _, sums in far_pairs]
    (other_value,), (other_sums,) = chunk_grads([low], sources)
    other_value, other_sums, forget_over, owned_parts, from_core, sums_across, sends, sources = settle(
        other_value, other_sums, forget_over, owned_parts, from_core, sums_across, sends, sources
    )
    forget_part = second_end(forget_wg, forget_came, forget_over)
    far_sums = [sums[1] + sums_across[n] for n, (_, sums) in enumerate(far_pairs)]
    forget_part, sends, far_sums, sources, far_pairs, from_core = settle(
        forget_part, sends, far_sums, sources, far_pairs, from_core
    )

    owned_parts = owned_parts + to_owners(0, sends, slice(1, None))
    last_parts = to_owners(1, [forget_part] * len(back_routes[1][2]), slice(0, 1))
    value_core, sums_core = cross_core(other_value), cross_core(other_sums)
    (own_value,), (own_sums,) = chunk_grads([0], sources)
    sixteen = rows // 32
    v_cuts = [(0, rows)]
    own_value, own_sums, owned_parts, last_parts, value_core, sums_core, far_pairs, from_core, far_sums, forget_part = settle(
        own_value, own_sums, owned_parts, last_parts, value_core, sums_core, far_pairs, from_core, far_sums, forget_part
    )
    v_sends = [
        [
            add_up([values[1][start : start + size], from_core[n][start : start + size]])
            for n, (values, _) in enumerate(far_pairs)
        ]
        for start, size in v_cuts
    ]

    gate_sums = jnp.sum(jnp.concatenate([forget_sums, reset_sums]), axis=1)
    spread_sums = lax.dynamic_update_slice(
        jnp.zeros((4, width), F32), gate_sums, (0, (z % low + low * k) * channels)
    )
    small = jnp.concatenate([jnp.sum(sum(norm_sums[1:], norm_sums[0]), axis=1), spread_sums], axis=0)
    last_parts = last_parts + to_owners(1, [forget_part] * len(back_routes[1][2]), slice(1, None))
    small_came = cross_low(small, 1)
    far_sums = [cross_low(sums, dz) for dz, sums in zip(lows, far_sums)]
    last_parts, small, small_came, far_sums, v_sends = settle(last_parts, small, small_came, far_sums, v_sends)
    small = small + small_came
    sums = sum([sums_core] + far_sums, own_sums)
    owned_parts = owned_parts + [candidate_part, reset_part] + last_parts + [forget_part]

    block_piece = (3, half, channels)
    own_blocks, give_blocks = call(
        functools.partial(owned_kernel, info, len(owned_parts)),
        [shape_of(block_piece, BF16)] * 2,
        [anywhere] * len(owned_parts),
        [full(block_piece)] * 2,
        scratch=[
            pltpu.VMEM((3, part, channels), F32),
            pltpu.VMEM((len(owned_parts), part, channels), BF16),
            pltpu.SemaphoreType.DMA((len(owned_parts),)),
        ],
        cost_estimate=cost(0, 6 * part * channels),
        name="own_blocks",
    )(scalars, *owned_parts)
    own_blocks, give_blocks, small = settle(own_blocks, give_blocks, small)

    give_blocks = cross_core(give_blocks)
    small_came = [cross_low(small, bit) for bit in bits_of(groups)[1:2]]
    own_blocks, give_blocks, small, small_came, v_sends = settle(own_blocks, give_blocks, small, small_came, v_sends)
    small = sum(small_came, small)
    for bit in bits_of(groups)[2:]:
        small = small + cross_low(small, bit)
    v_came = [[cross_low(value, dz) for dz, value in zip(lows, v_sends[0])]]
    own_sum = add_up([own_blocks, give_blocks])
    own_sum, small, sums = settle(own_sum, small, sums)

    whole = [own_sum] + [cross_plane(own_sum, d) for d in (others[:2] if short else others)]
    whole_core = [cross_core(own_sum)]
    small_came = cross_core(small)
    output = call(
        functools.partial(output_kernel, info, low, [value.shape[0] for value in out_came]),
        shape_of((2, half_rows, channels), BF16),
        [full((rows, rows)), full((half_rows, channels))] + [full(value.shape) for value in out_came],
        full((2, half_rows, channels)),
        scratch=[pltpu.VMEM((half_rows, channels), BF16)],
        cost_estimate=cost(4 * low * rows * rows * channels, 8 * half_rows * channels),
        name="output",
    )(scalars, back_order, stay.reshape(half_rows, channels), *out_came)
    input_part = pl.pallas_call(
        input_part_kernel,
        grid=(tiles,),
        in_specs=[
            pl.BlockSpec((tile, width), lambda t: (t, 0)),
            pl.BlockSpec((tile, rows), lambda t: (t, 0)),
            full((rows, width)),
            full((rows, width)),
            full((SUB, rows)),
        ],
        out_specs=pl.BlockSpec((tile, width), lambda t: (t, 0)),
        out_shape=shape_of((rows, width), F32),
        compiler_params=params(),
        cost_estimate=cost(4 * rows * rows * width, 10 * rows * width),
        name="input_part",
    )(inputs, back_order, own_value, value_core, sums)
    whole, whole_core, small, small_came, input_part, output = settle(
        whole, whole_core, small, small_came, input_part, output
    )
    small = small + small_came
    output = output.reshape(groups * rows, channels)

    def spread(name, values, steps, held):
        return call(
            functools.partial(spread_kernel, len(values), steps),
            shape_of((width, 3 * channels), F32),
            [full(value.shape) for value in values] + [anywhere] * len(held),
            pl.BlockSpec((quarter, 3 * channels), lambda t, s: (s[getattr(info, name) + t], 0)),
            grid=(len(steps),),
            aliases={1 + len(values): 0} if held else None,
            cost_estimate=cost(0, 9 * width * channels),
            name="spread_" + name,
        )(scalars, *values, *held)

    split = []
    if short:
        split = [whole[1][:, :quarter], whole[2][:, quarter:]]
        whole, split, small = settle(whole, split, small)
        split = [cross_plane(split[0], 2), cross_plane(split[1], 1)]
    whole_core += [cross_core(value) for value in whole[1:]]
    values = whole + whole_core[:1]
    weight_grad = spread("near_rows", values, [(n, at) for n in range(len(values)) for at in (0, quarter)], ())
    weight_grad, split, whole_core, small = settle(weight_grad, split, whole_core, small)

    bits = bits_of(planes)
    small_came = cross_plane(small, bits[0])
    split_core = [cross_core(value) for value in split]
    values = whole_core[1:] + split
    steps = [(n, at) for n in range(len(whole_core) - 1) for at in (0, quarter)]
    steps += [(len(whole_core) - 1 + n, 0) for n in range(len(split))]
    weight_grad = spread("far_rows", values, steps, (weight_grad,))
    split_core, small, small_came, weight_grad = settle(split_core, small, small_came, weight_grad)
    small = small + small_came

    small_came = [cross_plane(small, bit) for bit in bits[1:2]]
    if short:
        weight_grad = spread("last_rows", split_core, [(0, 0), (1, 0)], (weight_grad,))
    small, small_came, weight_grad, v_came = settle(small, small_came, weight_grad, v_came)
    small = sum(small_came, small)
    for bit in bits[2:]:
        small = small + cross_plane(small, bit)

    parts = [(start, value) for (start, _), came_now in zip(v_cuts, v_came) for value in came_now]
    input_grad = pl.pallas_call(
        functools.partial(last_kernel, [start for start, _ in parts]),
        grid=(tiles,),
        in_specs=[pl.BlockSpec((tile, width), lambda t: (t, 0)), pl.BlockSpec((tile, rows), lambda t: (t, 0))]
        + [full(value.shape) for _, value in parts],
        out_specs=pl.BlockSpec((tile, width), lambda t: (t, 0)),
        out_shape=shape_of((rows, width), F32),
        input_output_aliases={0: 0},
        compiler_params=params(),
        cost_estimate=cost(2 * rows * rows * width, 10 * rows * width),
        name="input_grad",
    )(input_part, back_order, *[value for _, value in parts])
    gate_block = lax.dynamic_slice_in_dim(small[2:], z * channels, channels, 1)
    return (
        output,
        input_grad,
        weight_grad,
        small[0],
        small[1],
        gate_block[1],
        gate_block[3],
        gate_block[0],
        gate_block[2],
    )


def solution(mesh):
    placed = (
        P(("seq", "col"), None),
        P(),
        P(),
        P(None, "col"),
        P("col"),
        P("col"),
        P("col"),
        P("col"),
        P(),
        P("seq", "col"),
    )
    return jax.shard_map(
        per_device,
        mesh=mesh,
        in_specs=placed,
        out_specs=(
            P("seq", "col"),
            P(("seq", "col"), None),
            P(None, "col"),
            P(),
            P(),
            P("col"),
            P("col"),
            P("col"),
            P("col"),
        ),
        check_vma=False,
    )
```

```python
import functools

import jax
import jax.numpy as jnp
import numpy as np
from jax import lax
from jax.experimental import pallas as pl
from jax.experimental.pallas import tpu as pltpu
from jax.sharding import PartitionSpec as P

EPSILON = 1e-05
F32 = jnp.float32
BF16 = jnp.bfloat16
LANES = 128
SUB = 8
VMEM_LIMIT = 56 * 1024 * 1024


def bits_of(count):
    return [1 << b for b in range(count.bit_length() - 1)]


def colour(edges, count):
    degree = max([sum(e[0] == n for e in edges) for n in range(count)] + [sum(e[1] == n for e in edges) for n in range(count)])
    out = [[None] * degree for _ in range(count)]
    into = [[None] * degree for _ in range(count)]
    taken = {}
    for at, edge in enumerate(edges):
        src, dst = edge[0], edge[1]
        first = next(c for c in range(degree) if out[src][c] is None)
        second = next(c for c in range(degree) if into[dst][c] is None)
        if first != second:
            path, node, at_dst, look = [], dst, True, first
            while True:
                found = (into if at_dst else out)[node][look]
                if found is None:
                    break
                path.append(found)
                node = edges[found][0] if at_dst else edges[found][1]
                at_dst = not at_dst
                look = second if look == first else first
            for found in path:
                old = taken[found]
                out[edges[found][0]][old] = None
                into[edges[found][1]][old] = None
            for found in path:
                new = second if taken[found] == first else first
                taken[found] = new
                out[edges[found][0]][new] = found
                into[edges[found][1]][new] = found
        taken[at] = first
        out[src][first] = at
        into[dst][first] = at
    rounds = [[] for _ in range(degree)]
    for at, edge in enumerate(edges):
        rounds[taken[at]].append(edge)
    return rounds


def busiest(edges, groups):
    links = {}
    for src, dst, _, _ in edges:
        a, b = src % groups, dst % groups
        for n in range(min(a, b), max(a, b)):
            links[n, a < b] = links.get((n, a < b), 0) + 1
    return max(links.values(), default=0)


def balance(rounds, groups):
    if len(rounds) != 2:
        return rounds
    paths = []
    left = [(r, e) for r in range(2) for e in rounds[r]]
    while left:
        path = [left.pop()]
        grown = True
        while grown:
            near = [x for x in left if any(x[1][0] == y[1][0] or x[1][1] == y[1][1] for y in path)]
            left = [x for x in left if x not in near]
            path += near
            grown = bool(near)
        paths.append(path)
    best = None
    for flips in range(2 ** len(paths)):
        tried = [[], []]
        for n, path in enumerate(paths):
            for r, edge in path:
                tried[r ^ (flips >> n & 1)].append(edge)
        score = sum(busiest(edges, groups) for edges in tried)
        score = (max(busiest(edges, groups) for edges in tried), score)
        if best is None or score < best[0]:
            best = (score, tried)
    return best[1]


def routes(groups, streams):
    low = groups // 2
    local, edges = [], []
    load = [0] * (2 * groups)
    for core in range(2):
        for z in range(groups):
            for stream in streams:
                block = stream * groups + z % low + low * core
                owner, at = block // 3, block % 3
                dst = core * groups + z
                if owner == z:
                    local.append((dst, dst, stream, at))
                else:
                    edges.append([core, owner, dst, stream, at])
    found = []
    for owner in range(groups):
        mine = [e for e in edges if e[1] == owner]
        quota = -(-len(mine) // 2)
        for core, _, dst, stream, at in mine:
            src = core * groups + owner
            if load[src] == quota:
                src = (1 - core) * groups + owner
            load[src] += 1
            found.append((src, dst, stream, at))
    return local, balance(colour(found, 2 * groups), groups)


def row_order(rows):
    seg = rows // SUB
    matrix = np.zeros((rows, rows), np.float32)
    for i in range(seg):
        for j in range(SUB):
            matrix[i * SUB + j, j * seg + i] = 1.0
    return matrix


def gate(value):
    small = jnp.exp(-jnp.abs(value))
    minor = small / (1.0 + small)
    major = 1.0 - minor
    up = value >= 0.0
    return jnp.where(up, major, minor), jnp.where(up, minor, major)


def kept_of(base, step, seg, bounds, channels):
    at = lax.broadcasted_iota(jnp.int32, (SUB, LANES), 0) * seg + (base + step)
    starts = at == bounds[0]
    for bound in bounds[1:]:
        starts = starts | (at == bound)
    kept = jnp.where(starts, 0.0, 1.0)
    return jnp.concatenate([kept] * (channels // LANES), axis=1)


class Info:
    def __init__(self):
        self.spots = {}
        self.columns = []

    def put(self, name, values):
        self.spots[name] = len(self.columns)
        self.columns += list(np.asarray(values, np.int32))

    def __getattr__(self, name):
        return self.spots[name]

    def table(self):
        return np.stack(self.columns, axis=1)


def bounds_of(lengths):
    starts = [0]
    for n in range(lengths.shape[0] - 1):
        starts.append(starts[-1] + lengths[n])
    return starts


def cut_kernel(count, s, *refs):
    for n in range(count):
        refs[count + n][...] = refs[n][...]


def pick_kernel(info, count, s, *refs):
    ins, outs = refs[: 2 * count], refs[2 * count :]
    totals, rounds = outs[:2], outs[2:]
    for n, total in enumerate(totals):
        mine = ins[n * count : (n + 1) * count]
        half = total.shape[0] // 2 if count == 6 else total.shape[0]
        groups_of = (mine[:3], mine[3:]) if count == 6 else (mine,)
        for m, parts in enumerate(groups_of):
            found = [part[...] if len(part.shape) == 2 else part[0] for part in parts]
            value = found[0].astype(F32)
            for part in found[1:]:
                value = value + part.astype(F32)
            total[m * half : (m + 1) * half] = value.astype(BF16)
    for r, out in enumerate(rounds):
        for n, total in enumerate(totals):

            @pl.when(s[info.back_stream + r] == n)
            def _():
                out[...] = total[...]


def norm_rows(x_ref, gain, bias, normed_ref, hat_ref, inv_ref):
    block = 32
    for r in range(x_ref.shape[0] // block):
        at = slice(r * block, (r + 1) * block)
        x = x_ref[at].astype(F32)
        average = jnp.mean(x, axis=1, keepdims=True)
        centred = x - average
        inv = lax.rsqrt(jnp.mean(centred * centred, axis=1, keepdims=True) + EPSILON)
        hat = centred * inv
        normed_ref[0, at] = (hat * gain + bias).astype(BF16)
        hat_ref[0, at] = hat.astype(BF16)
        inv_ref[0, at] = jnp.broadcast_to(inv, (block, LANES))


def group_columns(info, s, channels):
    return pl.ds(pl.multiple_of(s[info.g] * channels, channels), channels)


def norm_kernel(info, s, x_ref, gain_ref, bias_ref, *refs):
    normed_ref, hx_ref, hat_ref, inv_ref = refs[-4:]
    norm_rows(x_ref, gain_ref[...], bias_ref[...], normed_ref, hat_ref, inv_ref)
    hx_ref[0] = x_ref[:, group_columns(info, s, hx_ref.shape[2])]


def segment_maps(base, seg, lengths, mixed_ref, fp, fb):
    channels = mixed_ref.shape[3]
    run_decay = jnp.ones((SUB, channels), F32)
    run_state = jnp.zeros((SUB, channels), F32)
    bounds = bounds_of(lengths)
    for i in range(mixed_ref.shape[2] // SUB):
        at = slice(i * SUB, (i + 1) * SUB)
        candidate = mixed_ref[0, 0, at].astype(F32)
        forget, rest = gate(mixed_ref[0, 1, at].astype(F32) + fp * candidate + fb)
        decay = forget * kept_of(base, i, seg, bounds, channels)
        run_state = decay * run_state + rest * candidate
        run_decay = decay * run_decay
    return run_decay, run_state


def mix_kernel(info, low, planes, seg, here, away, split, s, lengths, normed_ref, fp_ref, fb_ref, *refs):
    part = refs[0].shape[-2]
    whole = [(d, 0, part) for d in range(planes)]
    if split:
        ends = [(3, 0, part // 2), (3, part // 2, part // 2)]
        here_parts = whole[:3] + ends
        away_parts = [(d, n * (part // 2), part // 2) for d in range(3) for n in range(2)] + ends
    else:
        here_parts = away_parts = whole
    count = here * len(here_parts) + len(away_parts)
    pieces = refs[:count]
    mixed_ref, map_ref, full_ref, w_ref, in_sem, out_sem = refs[count:]
    step = pl.program_id(0)

    def copies(slot):
        stream = s[info.slot_stream + slot]
        found = []
        for n, (d, start, size) in enumerate(here_parts if slot < here else away_parts):
            rows = pl.ds(pl.multiple_of((d ^ s[info.p]) * part + start, size), size)
            if slot < here:
                piece = pieces[slot * len(here_parts) + n]
            else:
                piece = pieces[here * len(here_parts) + n].at[slot - here]
            spot = slot * len(away_parts) + n
            found.append(pltpu.make_async_copy(piece, w_ref.at[stream, rows, :], in_sem.at[spot]))
        return found

    @pl.when(step == 0)
    def _():
        for slot in range(here + away):

            @pl.when(s[info.slot_stream + slot] >= 0)
            def _():
                for copy in copies(slot):
                    copy.start()

        for slot in range(here + away):

            @pl.when(s[info.slot_stream + slot] >= 0)
            def _():
                for copy in copies(slot):
                    copy.wait()

        pltpu.make_async_copy(w_ref, full_ref, out_sem).start()

    for stream in range(2):
        mixed_ref[0, stream] = jnp.dot(normed_ref[0], w_ref[stream], preferred_element_type=F32).astype(BF16)
    decay, state = segment_maps(s[info.base + step * low], seg, lengths, mixed_ref, fp_ref[...], fb_ref[...])
    map_ref[0, 0] = decay
    map_ref[0, 1] = state

    @pl.when(step == pl.num_programs(0) - 1)
    def _():
        pltpu.make_async_copy(w_ref, full_ref, out_sem).wait()


def mix_far_kernel(info, low, seg, order, sizes, s, lengths, w_ref, gain_ref, bias_ref, fp_ref, fb_ref, near_ref, *refs):
    count = len(order)
    pieces = refs[: len(sizes) * count]
    normed_ref, hx_ref, hat_ref, inv_ref, mixed_ref, map_ref, run_ref, x_ref, sem = refs[len(sizes) * count + 5 :]
    channels = w_ref.shape[2]
    step = pl.program_id(0)

    def copies(n):
        found, start = [], 0
        for m, size in enumerate(sizes):
            spot = n * len(sizes) + m
            found.append(pltpu.make_async_copy(pieces[spot], x_ref.at[n, pl.ds(start, size), :], sem.at[spot]))
            start += size
        return found

    @pl.when(step == 0)
    def _():
        for n in range(count):
            for copy in copies(n):
                copy.start()
        for dk in range(2):
            map_ref[dk * low] = near_ref[dk * low]

    for n in range(count):

        @pl.when(step == n)
        def _():
            for copy in copies(n):
                copy.wait()

    mine = x_ref.at[step]
    norm_rows(mine, gain_ref[...], bias_ref[...], normed_ref, hat_ref, inv_ref)
    hx_ref[0] = mine[:, group_columns(info, s, channels)]
    for stream in range(2):
        mixed_ref[0, stream] = jnp.dot(normed_ref[0], w_ref[stream], preferred_element_type=F32).astype(BF16)
    chunk = far_chunk(low, step)
    decay, state = segment_maps(s[info.base + chunk], seg, lengths, mixed_ref, fp_ref[...], fb_ref[...])
    map_ref[chunk, 0] = decay
    map_ref[chunk, 1] = state

    @pl.when(step == count - 1)
    def _():
        rows = []
        for dk in range(2):
            decay = jnp.ones((1, channels), F32)
            state = jnp.zeros((1, channels), F32)
            for zl in range(low):
                c = dk * low + (zl ^ s[info.zlo])
                for j in range(SUB):
                    d, b = map_ref[c, 0, j : j + 1, :], map_ref[c, 1, j : j + 1, :]
                    state = d * state + b
                    decay = d * decay
            rows += [decay, state]
        run_ref[...] = jnp.concatenate(rows + [jnp.zeros((4, channels), F32)], axis=0)


def reset_kernel(normed_ref, w_ref, *refs):
    refs[-1][0] = jnp.dot(normed_ref[0], w_ref[0], preferred_element_type=F32).astype(BF16)


def far_chunk(low, n):
    return n // (low - 1) * low + 1 + n % (low - 1)


def gathered_maps(info, planes, s, refs, into):
    for d in range(planes):
        plane = d ^ s[info.p]
        into[s[info.zhi] * planes + plane] = refs[d][...]
        into[(1 - s[info.zhi]) * planes + plane] = refs[planes][d]


def state_kernel(info, low, planes, seg, sizes, s, lengths, *refs):
    gathered_refs = refs[: planes + 1]
    map_ref, mixed_ref, reset_ref, hx_ref, og_ref, og_cross_ref = refs[planes + 1 : planes + 7]
    far_refs = refs[planes + 7 : planes + 7 + 2 * len(sizes)]
    (
        order_ref, fp_ref, rp_ref, fb_ref, rb_ref,
        out_ref, out_far_ref, prev_ref, direct_ref, rz_ref, skip_ref, binj_ref, sums_ref, runb_ref,
        cell_ref, prod_ref, gathered_ref, grad_ref, og_all_ref, og_sem,
    ) = refs[planes + 7 + 2 * len(sizes) :]
    chunks, channels = map_ref.shape[0], map_ref.shape[3]
    step = pl.program_id(0)
    last = pl.num_programs(0) - 1
    k, zlo = s[info.k], s[info.zlo]

    @pl.when(step == 0)
    def _():
        stays = s[info.zhi] == k
        here_copies = [
            pltpu.make_async_copy(ref, og_all_ref.at[n], og_sem.at[n, 0]) for n, ref in enumerate((og_ref, og_cross_ref))
        ]
        far_copies = []
        for n in range(2):
            start = 0
            for m, size in enumerate(sizes):
                target = og_all_ref.at[n, pl.ds(start, size), :]
                far_copies.append(pltpu.make_async_copy(far_refs[n * len(sizes) + m], target, og_sem.at[n, m]))
                start += size

        @pl.when(stays)
        def _():
            for copy in here_copies:
                copy.start()

        @pl.when(jnp.logical_not(stays))
        def _():
            for copy in far_copies:
                copy.start()

        gathered_maps(info, planes, s, gathered_refs, gathered_ref)
        carry = jnp.zeros((1, channels), F32)
        own = [carry, carry]
        for plane in range(planes):
            for core in range(2):
                for zh in range(2):
                    e = zh * planes + plane
                    mine = (plane == s[info.p]) & (zh == s[info.zhi])
                    own[core] = jnp.where(mine, carry, own[core])
                    decay = jnp.where(k == core, gathered_ref[e, 0:1, :], gathered_ref[e, 2:3, :])
                    state = jnp.where(k == core, gathered_ref[e, 1:2, :], gathered_ref[e, 3:4, :])
                    carry = decay * carry + state
        for dk in range(2):
            carry = jnp.where(k == 0, own[dk], own[1 - dk])
            for zl in range(low):
                c = dk * low + (zl ^ zlo)
                for j in range(SUB):
                    cell_ref[c, j : j + 1, :] = carry
                    carry = map_ref[c, 0, j : j + 1, :] * carry + map_ref[c, 1, j : j + 1, :]

        @pl.when(stays)
        def _():
            for copy in here_copies:
                copy.wait()

        @pl.when(jnp.logical_not(stays))
        def _():
            for copy in far_copies:
                copy.wait()

        chunk_rows = order_ref.shape[0]
        for c in range(chunks):
            dk, dz = c // low, c % low
            at = pl.ds(pl.multiple_of((dz ^ zlo) * chunk_rows, chunk_rows), chunk_rows)
            grad_ref[c] = jnp.dot(order_ref[...], og_all_ref[dk, at, :], preferred_element_type=F32).astype(BF16)
        prod_ref[...] = jnp.ones_like(prod_ref)
        binj_ref[...] = jnp.zeros_like(binj_ref)
        sums_ref[...] = jnp.zeros_like(sums_ref)

    rows = hx_ref.shape[1]
    bounds = bounds_of(lengths)
    fp, rp, fb, rb = fp_ref[...], rp_ref[...], fb_ref[...], rb_ref[...]
    rz_sum, peep_sum = sums_ref[0], sums_ref[1]
    first, second = slice(0, SUB), slice(SUB, 2 * SUB)
    for c in range(chunks):
        base = s[info.base + c]
        cell, prod, binj = cell_ref[c], prod_ref[c], binj_ref[c]
        for i in range(rows // (2 * SUB)):
            at = slice(2 * i * SUB, 2 * (i + 1) * SUB)
            now = step * (rows // SUB) + 2 * i
            candidate = mixed_ref[c, 0, at].astype(F32)
            forget, rest = gate(mixed_ref[c, 1, at].astype(F32) + fp * candidate + fb)
            inject = rest * candidate
            kept = [kept_of(base, now + n, seg, bounds, channels) for n in range(2)]
            previous = [kept[0] * cell]
            cells = [forget[first] * previous[0] + inject[first]]
            previous.append(kept[1] * cells[0])
            cell = forget[second] * previous[1] + inject[second]
            cells = jnp.concatenate([cells[0], cell], axis=0)
            previous = jnp.concatenate(previous, axis=0)
            reset, skip = gate(reset_ref[c, at].astype(F32) + rp * previous + rb)
            x = hx_ref[c, at].astype(F32)
            here = pl.ds(pl.multiple_of(step * rows + 2 * i * SUB, 2 * SUB), 2 * SUB)
            g = grad_ref[c, here, :].astype(F32)
            out = (reset * cells + skip * x).astype(BF16)
            (out_ref, out_far_ref)[c // low][(c % low) ^ zlo, here, :] = out
            direct = g * reset
            rz = direct * skip * (cells - x)
            prev_ref[c, at] = previous.astype(BF16)
            direct_ref[c, at] = direct.astype(BF16)
            rz_ref[c, at] = rz.astype(BF16)
            skip_ref[c, at] = (g * skip).astype(BF16)
            back = forget * direct + rz * rp
            for n, half in ((0, first), (1, second)):
                prod_kept = prod * kept[n]
                binj = binj + prod_kept * back[half]
                prod = prod_kept * forget[half]
            rz_sum = rz_sum + (rz[first] + rz[second])
            peep = rz * previous
            peep_sum = peep_sum + (peep[first] + peep[second])
        cell_ref[c] = cell
        prod_ref[c] = prod
        binj_ref[c] = binj
    sums_ref[0] = rz_sum
    sums_ref[1] = peep_sum

    @pl.when(step == last)
    def _():
        runs = []
        for dk in range(2):
            acc = jnp.zeros((1, channels), F32)
            for zl in reversed(range(low)):
                c = dk * low + (zl ^ zlo)
                for j in reversed(range(SUB)):
                    acc = binj_ref[c, j : j + 1, :] + map_ref[c, 0, j : j + 1, :] * acc
            runs.append(acc)
        runb_ref[...] = jnp.concatenate(runs + [jnp.zeros((6, channels), F32)], axis=0)


def back_kernel(info, low, planes, seg, s, lengths, *refs):
    gathered_refs, back_refs = refs[: planes + 1], refs[planes + 1 : 2 * planes + 2]
    (
        map_ref, binj_ref, mixed_ref, prev_ref, direct_ref, rz_ref, fp_ref, rp_ref, fb_ref,
        grad_c_ref, grad_f_ref, sums_ref,
        carry_ref, gathered_ref, back_ref,
    ) = refs[2 * planes + 2 :]
    chunks, channels = map_ref.shape[0], map_ref.shape[3]
    step = pl.program_id(0)
    count = pl.num_programs(0)
    k, zlo = s[info.k], s[info.zlo]

    @pl.when(step == 0)
    def _():
        gathered_maps(info, planes, s, gathered_refs, gathered_ref)
        gathered_maps(info, planes, s, back_refs, back_ref)
        carry = jnp.zeros((1, channels), F32)
        own = [carry, carry]
        for plane in reversed(range(planes)):
            for core in (1, 0):
                for zh in (1, 0):
                    e = zh * planes + plane
                    mine = (plane == s[info.p]) & (zh == s[info.zhi])
                    own[core] = jnp.where(mine, carry, own[core])
                    decay = jnp.where(k == core, gathered_ref[e, 0:1, :], gathered_ref[e, 2:3, :])
                    inject = jnp.where(k == core, back_ref[e, 0:1, :], back_ref[e, 1:2, :])
                    carry = decay * carry + inject
        for dk in range(2):
            carry = jnp.where(k == 0, own[dk], own[1 - dk])
            for zl in reversed(range(low)):
                c = dk * low + (zl ^ zlo)
                for j in reversed(range(SUB)):
                    carry_ref[c, j : j + 1, :] = carry
                    carry = map_ref[c, 0, j : j + 1, :] * carry + binj_ref[c, j : j + 1, :]
        sums_ref[...] = jnp.zeros_like(sums_ref)

    rows = prev_ref.shape[1]
    bounds = bounds_of(lengths)
    fp, rp, fb = fp_ref[...], rp_ref[...], fb_ref[...]
    fz_sum, peep_sum = sums_ref[0], sums_ref[1]
    first, second = slice(0, SUB), slice(SUB, 2 * SUB)
    for c in range(chunks):
        base = s[info.base + c]
        back = carry_ref[c]
        for i in reversed(range(rows // (2 * SUB))):
            at = slice(2 * i * SUB, 2 * (i + 1) * SUB)
            now = (count - 1 - step) * (rows // SUB) + 2 * i
            candidate = mixed_ref[c, 0, at].astype(F32)
            forget, rest = gate(mixed_ref[c, 1, at].astype(F32) + fp * candidate + fb)
            direct = direct_ref[c, at].astype(F32)
            prev_grad = rz_ref[c, at].astype(F32) * rp
            later = direct[second] + back
            back = kept_of(base, now + 1, seg, bounds, channels) * (forget[second] * later + prev_grad[second])
            sooner = direct[first] + back
            back = kept_of(base, now, seg, bounds, channels) * (forget[first] * sooner + prev_grad[first])
            held = jnp.concatenate([sooner, later], axis=0) * rest
            forget_z = held * forget * (prev_ref[c, at].astype(F32) - candidate)
            grad_c_ref[c, at] = (held + forget_z * fp).astype(BF16)
            grad_f_ref[c, at] = forget_z.astype(BF16)
            fz_sum = fz_sum + (forget_z[first] + forget_z[second])
            peep = forget_z * candidate
            peep_sum = peep_sum + (peep[first] + peep[second])
        carry_ref[c] = back
    sums_ref[0] = fz_sum
    sums_ref[1] = peep_sum


def input_kernel(info, count, s, w_ref, gain_ref, *refs):
    ins = [refs[6 * n : 6 * n + 6] for n in range(count)]
    outs = refs[6 * count :]
    v_refs, s_refs = outs[:count], outs[count : 2 * count]
    gb_ref, grad_ref, first_ref, second_ref = outs[2 * count :]
    tile = pl.program_id(0)
    nt = (((1,), (1,)), ((), ()))
    rows, width = grad_ref.shape[1:]
    flag = jnp.where(s[info.g] == tile, 1.0, 0.0)
    gain = gain_ref[...]
    block = 32
    gain_sum = jnp.zeros((SUB, width), F32)
    bias_sum = jnp.zeros((SUB, width), F32)

    @pl.when(tile == 0)
    def _():
        first_ref[...] = jnp.zeros_like(first_ref)
        second_ref[...] = jnp.zeros_like(second_ref)

    for n, (grad_c_ref, grad_f_ref, rz_ref, _, _, _) in enumerate(ins):
        grad = lax.dot_general(grad_c_ref[0], w_ref[0], nt, preferred_element_type=F32)
        grad = grad + lax.dot_general(grad_f_ref[0], w_ref[1], nt, preferred_element_type=F32)
        grad_ref[n] = grad + lax.dot_general(rz_ref[0], w_ref[2], nt, preferred_element_type=F32)
    for n, (_, _, _, hat_ref, inv_ref, skip_ref) in enumerate(ins):
        for r in range(rows // block):
            at = slice(r * block, (r + 1) * block)
            value = grad_ref[n, at]
            inv = jnp.concatenate([inv_ref[0, at]] * (width // LANES), axis=1)
            hat = hat_ref[0, at].astype(F32)
            scaled = value * gain
            product = scaled * hat
            first, second = first_ref[n, at], second_ref[n, at]
            for lane in range(width // LANES):
                first = first + scaled[:, lane * LANES : (lane + 1) * LANES]
                second = second + product[:, lane * LANES : (lane + 1) * LANES]
            first_ref[n, at] = first
            second_ref[n, at] = second
            matched = value * hat
            for i in range(block // SUB):
                gain_sum = gain_sum + matched[i * SUB : (i + 1) * SUB]
                bias_sum = bias_sum + value[i * SUB : (i + 1) * SUB]
            v_refs[n][at] = (scaled * inv + skip_ref[0, at].astype(F32) * flag).astype(BF16)
    gb_ref[0] = gain_sum
    gb_ref[1] = bias_sum

    @pl.when(tile == pl.num_programs(0) - 1)
    def _():
        lane = lax.broadcasted_iota(jnp.int32, (rows, LANES), 1)
        for n in range(count):
            first = jnp.sum(first_ref[n], axis=1, keepdims=True)
            second = jnp.sum(second_ref[n], axis=1, keepdims=True)
            s_refs[n][...] = jnp.where(lane == 0, first, jnp.where(lane == 1, second, 0.0)).T[:SUB]


def output_kernel(info, low, sizes, s, order_ref, stay_ref, *refs):
    came_refs, (out_ref, all_ref) = refs[: len(sizes)], refs[len(sizes) :]
    rows = order_ref.shape[0]
    start = 0
    for piece, size in zip(came_refs, sizes):
        all_ref[start : start + size] = piece[...]
        start += size
    order = order_ref[...]
    for n in range(low):
        at = slice(n * rows, (n + 1) * rows)
        out_ref[s[info.zhi], at] = jnp.dot(order, stay_ref[at], preferred_element_type=F32).astype(BF16)
        out_ref[1 - s[info.zhi], at] = jnp.dot(order, all_ref[at], preferred_element_type=F32).astype(BF16)


def input_part_kernel(x_ref, order_ref, own_ref, core_ref, s_ref, out_ref):
    width = x_ref.shape[1]
    x = x_ref[...].astype(F32)
    average = jnp.mean(x, axis=1, keepdims=True)
    centred = x - average
    inv = lax.rsqrt(jnp.mean(centred * centred, axis=1, keepdims=True) + EPSILON)
    order = order_ref[...]
    value = jnp.dot(order, own_ref[...], preferred_element_type=F32)
    value = value + jnp.dot(order, core_ref[...], preferred_element_type=F32)
    sums = lax.dot_general(
        order.astype(F32), s_ref[...], (((1,), (1,)), ((), ())),
        precision=lax.Precision.HIGHEST, preferred_element_type=F32,
    )
    first = sums[:, 0:1] * (1.0 / width)
    second = sums[:, 1:2] * (1.0 / width)
    out_ref[...] = value - inv * (first + centred * inv * second)


def last_kernel(starts, part_ref, order_ref, *refs):
    pieces, out_ref = refs[: len(starts)], refs[len(starts)]
    order = order_ref[...]
    value = part_ref[...]
    for start, piece in zip(starts, pieces):
        value = value + jnp.dot(order[:, start : start + piece.shape[0]], piece[...], preferred_element_type=F32)
    out_ref[...] = value


def weight_grad_kernel(count, order, s, normed_ref, *refs):
    grads, outs = refs[:count], refs[count:]
    each = len(outs) // count
    tn = (((0,), (0,)), ((), ()))
    for n in range(count):
        total = lax.dot_general(normed_ref[0], grads[n][0], tn, preferred_element_type=F32)
        for c in range(1, normed_ref.shape[0]):
            total = total + lax.dot_general(normed_ref[c], grads[n][c], tn, preferred_element_type=F32)
        low = total.astype(BF16)
        half = low.shape[0] // 2
        for at, places in enumerate(order):

            @pl.when(pl.program_id(0) == at)
            def _():
                for ref, place, rows in places:
                    outs[n * each + ref][place] = (low, low[:half], low[half:])[rows]


def owned_kernel(info, count, s, *refs):
    came, outs, total_ref, slot_ref, sem = refs[:count], refs[count : count + 2], *refs[count + 2 :]
    total_ref[...] = jnp.zeros_like(total_ref)
    for wait in (False, True):
        for n in range(count):

            @pl.when(s[info.owned + n] >= 0)
            def _():
                copy = pltpu.make_async_copy(came[n], slot_ref.at[n], sem.at[n])
                if not wait:
                    copy.start()
                else:
                    copy.wait()
                    total_ref[s[info.owned + n]] += slot_ref[n].astype(F32)

    half = total_ref.shape[1] // 2
    for n, out in enumerate(outs):
        core = s[info.k] if n == 0 else 1 - s[info.k]
        rows = pl.ds(pl.multiple_of(core * half, half), half)
        for block in range(3):
            out[block] = total_ref[block, rows, :].astype(BF16)


def spread_kernel(count, steps, s, *refs):
    pieces, out_ref = refs[:count], refs[-1]
    rows, channels = out_ref.shape[0], pieces[0].shape[2]
    for n, (piece, start) in enumerate(steps):

        @pl.when(pl.program_id(0) == n)
        def _():
            for block in range(3):
                values = pieces[piece][block, start : start + rows]
                out_ref[:, block * channels : (block + 1) * channels] = values.astype(F32)


def cost(flops, moved, exps=0):
    return pl.CostEstimate(flops=int(flops) // 20, bytes_accessed=int(moved) // 20, transcendentals=int(exps) // 20)


def per_device(
    inputs, norm_gain, norm_bias, weight, forget_peep, reset_peep, forget_bias, reset_bias, seq_lengths, out_grad
):
    rows, width = inputs.shape
    seqs, groups = lax.axis_size("seq"), lax.axis_size("col")
    planes, low = seqs // 2, groups // 2
    channels = width // groups
    chunks = groups
    seg = rows // SUB
    part = width // planes
    half, quarter = part // 2, part // 4
    seq, z = lax.axis_index("seq"), lax.axis_index("col")
    k, zhi = seq % 2, z // low
    params = functools.partial(pltpu.CompilerParams, vmem_limit_bytes=VMEM_LIMIT)
    others = range(1, planes)
    short = planes == 4
    anywhere = pl.BlockSpec(memory_space=pl.ANY)
    full = lambda shape: pl.BlockSpec(shape, lambda *_: (0,) * len(shape))
    shape_of = jax.ShapeDtypeStruct

    def move(value, to):
        pairs = []
        for a in range(seqs):
            for b in range(groups):
                target = to(a // 2, a % 2, b)
                if target is not None:
                    pairs.append((a * groups + b, (target[0] * 2 + target[1]) * groups + target[2]))
        return lax.ppermute(value, ("seq", "col"), pairs)

    def cross_core(value):
        return move(value, lambda p, k, z: (p, 1 - k, z))

    def cross_low(value, dz):
        return move(value, lambda p, k, z: (p, k, z ^ dz))

    def cross_high(value):
        return move(value, lambda p, k, z: (p, k, (z + low) % groups))

    def cross_plane(value, dp):
        return move(value, lambda p, k, z: (p ^ dp, k, z))

    def move_nodes(value, pairs):
        spot = lambda p, n: (2 * p + n // groups) * groups + n % groups
        return lax.ppermute(
            value, ("seq", "col"), [(spot(p, src), spot(p, dst)) for p in range(planes) for src, dst in pairs]
        )

    def after(values, *first):
        return lax.optimization_barrier((values, first))[0]

    def add_up(values):
        total = values[0].astype(F32)
        for value in values[1:]:
            total = total + value.astype(F32)
        return total.astype(BF16)

    device = np.arange(seqs * groups)
    dev_p, dev_k, dev_z = device // groups // 2, device // groups % 2, device % groups
    dev_zhi, dev_zlo = dev_z // low, dev_z % low
    info = Info()
    for name, value in (("p", dev_p), ("k", dev_k), ("zhi", dev_zhi), ("zlo", dev_zlo), ("g", dev_zlo + low * dev_k)):
        info.put(name, [value])
    info.put(
        "base",
        [((2 * dev_p + (dev_k ^ (c // low))) * groups + dev_zhi * low + (dev_zlo ^ (c % low))) * rows for c in range(chunks)],
    )
    node = dev_k * groups + dev_z
    at_dev = lambda table: np.asarray(table, np.int32)[:, node]
    local, plan = routes(groups, range(3))
    rounds = len(plan)
    here = max(sum(e[1] == n for e in local) for n in range(2 * groups))
    slot_stream = np.full((here + rounds, 2 * groups), -1)
    cut_block = np.zeros((rounds + here, 2 * groups))
    for r, edges in enumerate(plan):
        for src, dst, stream, at in edges:
            cut_block[r, src] = at
            slot_stream[here + r, dst] = stream
    for n in range(2 * groups):
        for at, edge in enumerate(edge for edge in local if edge[1] == n):
            slot_stream[at, n] = edge[2]
            cut_block[rounds + at, n] = edge[3]
    info.put("slot_stream", at_dev(slot_stream))
    info.put("cut_block", at_dev(cut_block))
    back_routes = [(streams, *routes(groups, streams)) for streams in ([0, 2], [1])]
    owned, back_stream = [], []
    for streams, back_local, back_plan in back_routes:
        for edges in back_plan:
            takes = np.full(2 * groups, -1)
            source = np.zeros(2 * groups)
            for src, dst, stream, at in edges:
                takes[src] = at
                source[dst] = streams.index(stream)
            owned.append(takes)
            back_stream.append(source)
        for stream in streams:
            takes = np.full(2 * groups, -1)
            for src, _, found, at in back_local:
                if found == stream:
                    takes[src] = at
            owned.append(takes)
    info.put("owned", at_dev(owned))
    info.put("back_stream", at_dev(back_stream[: len(back_routes[0][2])]))
    visits = [3, 1, 2, 0] if short else list(range(planes))
    info.put("visits", [dev_p ^ d for d in visits])
    def piece_rows(d, dk):
        return [((dev_p ^ d) * 2 + (dev_k ^ dk)) * 2 + n for n in range(2)]

    whole_planes = range(3 if short else planes)
    near_rows = sum([piece_rows(d, 0) for d in whole_planes[1:]], []) + sum([piece_rows(d, 1) for d in whole_planes], [])
    info.put("own_rows", piece_rows(0, 0))
    info.put("near_rows", near_rows)
    info.put("far_rows", piece_rows(3, 0) if short else [])
    info.put("last_rows", piece_rows(3, 1) if short else [])
    scalars = lax.dynamic_index_in_dim(jnp.asarray(info.table()), seq * groups + z, 0, keepdims=False)

    order = jnp.asarray(row_order(rows), BF16)
    back_order = jnp.asarray(row_order(rows).T.copy(), BF16)

    tile = 128 if rows % 128 == 0 else rows
    tiles = rows // tile

    def call(kernel, out_shape, in_specs, out_specs, grid=(1,), scratch=(), lengths=False, aliases=None, **rest):
        return pl.pallas_call(
            kernel,
            grid_spec=pltpu.PrefetchScalarGridSpec(
                num_scalar_prefetch=2 if lengths else 1,
                grid=grid,
                in_specs=in_specs,
                out_specs=out_specs,
                scratch_shapes=list(scratch),
            ),
            out_shape=out_shape,
            input_output_aliases=aliases or {},
            compiler_params=params(),
            **rest,
        )

    def settle(*values):
        return lax.optimization_barrier(values)

    gain2, bias2 = norm_gain[None, :], norm_bias[None, :]

    row_shapes = (
        shape_of((chunks, rows, width), BF16),
        shape_of((chunks, rows, channels), BF16),
        shape_of((chunks, rows, width), BF16),
        shape_of((chunks, rows, LANES), F32),
    )
    mix_shapes = (shape_of((chunks, 2, rows, channels), BF16), shape_of((chunks, 2, SUB, channels), F32))
    wide = 256 if rows % 256 == 0 else rows

    def normalise(c, value, held):
        return call(
            functools.partial(norm_kernel, info),
            row_shapes,
            [pl.BlockSpec((wide, width), lambda t, s: (t, 0)), full((1, width)), full((1, width))]
            + [anywhere] * len(held),
            [
                pl.BlockSpec((1, wide, width), lambda t, s: (c, t, 0)),
                pl.BlockSpec((1, wide, channels), lambda t, s: (c, t, 0)),
                pl.BlockSpec((1, wide, width), lambda t, s: (c, t, 0)),
                pl.BlockSpec((1, wide, LANES), lambda t, s: (c, t, 0)),
            ],
            grid=(rows // wide,),
            aliases={4 + n: n for n in range(len(held))},
            cost_estimate=cost(12 * rows * width, 7 * rows * width),
            name="norm_chunk",
        )(scalars, value, gain2, bias2, *held)

    blocks_out = call(
        functools.partial(cut_kernel, rounds + here),
        [shape_of((part, channels), BF16)] * (rounds + here),
        [
            pl.BlockSpec((part, channels), lambda t, s, n=n: (s[info.p], s[info.cut_block + n]))
            for n in range(rounds + here)
        ],
        [full((part, channels))] * (rounds + here),
        cost_estimate=cost(0, 0),
        name="cut_weight",
    )(scalars, *[weight] * (rounds + here))
    arrived = [move_nodes(blocks_out[r], [(e[0], e[1]) for e in plan[r]]) for r in range(rounds)]
    permuted = jnp.dot(order, after(inputs, blocks_out), preferred_element_type=F32).astype(BF16)
    held = normalise(0, permuted, ())
    locals_here = blocks_out[rounds:]
    if short:
        local_near = [[cross_plane(value, 1), cross_plane(value, 2)] for value in locals_here]
    else:
        local_near = [[cross_plane(value, d) for d in others] for value in locals_here]
    x_core = cross_core(permuted)
    quad = rows // 4
    x_cuts = [(0, quad), (quad, 3 * quad)]
    x_sends = [permuted[start : start + size] for start, size in x_cuts]
    lows = range(1, low)
    x_sends = after(x_sends, x_core)
    x_far = [[cross_low(x_sends[0], dz) for dz in lows]]
    local_near, x_core, held = settle(local_near, x_core, held)

    local_ends = []
    if short:
        local_ends = [[cross_plane(one[:half], 2), cross_plane(two[half:], 1)] for one, two in local_near]
    if short:
        taken = [jnp.stack([value[:half] for value in arrived]), jnp.stack([value[half:] for value in arrived])]
    else:
        taken = [jnp.stack(arrived)]
    taken, local_ends, x_far, held, x_core, x_sends, cotangent = settle(
        taken, local_ends, x_far, held, x_core, x_sends, out_grad
    )
    half_rows = low * rows
    own_half = lax.dynamic_slice_in_dim(cotangent, zhi * half_rows, half_rows, 0)
    unit = half_rows // 32
    far_parts = []
    for start, size in ((0, 7), (7, 25)):
        far_parts.append(lax.dynamic_slice_in_dim(cotangent, (1 - zhi) * half_rows + start * unit, size * unit, 0))
    taken_full = [taken] + [[cross_plane(value, d) for value in taken] for d in (others[:2] if short else others)]
    x_far.append([cross_low(x_sends[1], dz) for dz in lows])
    held = normalise(low, x_core, held)
    gates = jnp.stack([forget_peep, reset_peep, forget_bias, reset_bias])
    taken_full, far_parts, held, gates = settle(taken_full, far_parts, held, gates)

    taken_ends = [cross_plane(taken_full[1][0], 2), cross_plane(taken_full[2][1], 1)] if short else []
    far_came = [cross_high(far_parts[0])]
    gates_far = cross_high(gates)
    taken_full, taken_ends, x_far, far_came, far_parts, gates_far = settle(
        taken_full, taken_ends, x_far, far_came, far_parts, gates_far
    )
    gates = jnp.where(zhi == k, gates, gates_far)
    fp, rp, fb, rb = (gates[n : n + 1] for n in range(4))
    x_cross = []

    x_cross += [[cross_core(value) for value in values] for values in x_far]
    far_cross = [cross_core(far_came[0])]
    own_cross = cross_core(own_half)
    far_came.append(cross_high(far_parts[1]))
    weight_pieces = []
    for n, value in enumerate(locals_here):
        weight_pieces += [value] + local_near[n] + (local_ends[n] if short else [])
    weight_pieces += sum(taken_full, []) + taken_ends
    mix_cost = cost(3 * chunks * rows * width * channels, 4 * chunks * rows * width + 12 * width * channels)
    mixed, maps, full_weight = call(
        functools.partial(mix_kernel, info, low, planes, seg, here, rounds, short),
        mix_shapes + (shape_of((3, width, channels), BF16),),
        [pl.BlockSpec((1, rows, width), lambda t, *_: (t * low, 0, 0)), full((1, channels)), full((1, channels))]
        + [anywhere] * len(weight_pieces),
        [
            pl.BlockSpec((1, 2, rows, channels), lambda t, *_: (t * low, 0, 0, 0)),
            pl.BlockSpec((1, 2, SUB, channels), lambda t, *_: (t * low, 0, 0, 0)),
            anywhere,
        ],
        grid=(2,),
        scratch=[
            pltpu.VMEM((3, width, channels), BF16),
            pltpu.SemaphoreType.DMA(((here + rounds) * (8 if short else planes),)),
            pltpu.SemaphoreType.DMA,
        ],
        lengths=True,
        cost_estimate=mix_cost,
        name="mix_near",
    )(scalars, seq_lengths, held[0], fp, fb, *weight_pieces)

    mixed, maps, full_weight, x_far, x_cross, far_cross, own_cross = settle(
        mixed, maps, full_weight, x_far, x_cross, far_cross, own_cross
    )

    far_order = [far_chunk(low, n) for n in range(2 * (low - 1))]
    far_pieces = [(x_far, x_cross)[c // low][n][c % low - 1] for c in far_order for n in range(len(x_cuts))]
    far_at = lambda t: far_chunk(low, t)
    *held, mixed, maps, run_maps = call(
        functools.partial(mix_far_kernel, info, low, seg, far_order, [size for _, size in x_cuts]),
        row_shapes + mix_shapes + (shape_of((SUB, channels), F32),),
        [full((2, width, channels)), full((1, width)), full((1, width)), full((1, channels)), full((1, channels))]
        + [full((chunks, 2, SUB, channels))]
        + [anywhere] * len(far_pieces)
        + [anywhere] * 5,
        [
            pl.BlockSpec((1, rows, width), lambda t, *_: (far_at(t), 0, 0)),
            pl.BlockSpec((1, rows, channels), lambda t, *_: (far_at(t), 0, 0)),
            pl.BlockSpec((1, rows, width), lambda t, *_: (far_at(t), 0, 0)),
            pl.BlockSpec((1, rows, LANES), lambda t, *_: (far_at(t), 0, 0)),
            pl.BlockSpec((1, 2, rows, channels), lambda t, *_: (far_at(t), 0, 0, 0)),
            full((chunks, 2, SUB, channels)),
            full((SUB, channels)),
        ],
        grid=(len(far_order),),
        scratch=[
            pltpu.VMEM((len(far_order), rows, width), BF16),
            pltpu.SemaphoreType.DMA((len(far_pieces),)),
        ],
        lengths=True,
        aliases={8 + len(far_pieces) + n: n for n in range(5)},
        cost_estimate=mix_cost,
        name="mix_far",
    )(
        scalars, seq_lengths, full_weight, gain2, bias2, fp, fb, maps,
        *far_pieces, *held, mixed,
    )
    normed, highway, hats, invs = held

    def reset_product(chosen, first, held):
        at = lambda t: sum(jnp.where(t == n, c, 0) for n, c in enumerate(chosen))
        return pl.pallas_call(
            reset_kernel,
            grid=(len(chosen),),
            in_specs=[
                pl.BlockSpec((1, rows, width), lambda t: (at(t), 0, 0)),
                pl.BlockSpec((1, width, channels), lambda t: (2, 0, 0)),
            ]
            + [anywhere] * len(held),
            out_specs=pl.BlockSpec((1, rows, channels), lambda t: (at(t), 0, 0)),
            out_shape=shape_of((chunks, rows, channels), BF16),
            input_output_aliases={2: 0} if held else {},
            compiler_params=params(),
            cost_estimate=cost(2 * len(chosen) * rows * width * channels, 2 * len(chosen) * rows * width),
            name="mix_reset",
        )(after(normed, first), full_weight, *held)

    near_chunks = [0, low]
    near_maps = [run_maps] + [cross_plane(run_maps, d) for d in others]
    reset_mixed = reset_product(near_chunks, run_maps, ())
    near_maps, far_came, reset_mixed = settle(near_maps, far_came, reset_mixed)
    far_maps = cross_high(jnp.stack(near_maps))
    far_cross.append(cross_core(far_came[1]))
    reset_mixed = reset_product([c for c in range(chunks) if c not in near_chunks], near_maps, (reset_mixed,))
    near_maps, far_maps, far_cross, reset_mixed = settle(near_maps, far_maps, far_cross, reset_mixed)
    gathered = near_maps + [far_maps]

    map_specs = [full((SUB, channels))] * planes + [full((planes, SUB, channels))]
    block = 128 if rows % 128 == 0 else rows
    blocks = rows // block
    elements = chunks * rows * channels
    runs = (low, rows, channels)
    part_rows = (chunks, block, channels)
    at_block = lambda t, *_: (0, t, 0)
    state_out = call(
        functools.partial(state_kernel, info, low, planes, seg, [value.shape[0] for value in far_came]),
        (
            shape_of(runs, BF16),
            shape_of(runs, BF16),
            shape_of((chunks, rows, channels), BF16),
            shape_of((chunks, rows, channels), BF16),
            shape_of((chunks, rows, channels), BF16),
            shape_of((chunks, rows, channels), BF16),
            shape_of((chunks, SUB, channels), F32),
            shape_of((2, SUB, channels), F32),
            shape_of((SUB, channels), F32),
        ),
        map_specs
        + [
            full((chunks, 2, SUB, channels)),
            pl.BlockSpec((chunks, 2, block, channels), lambda t, *_: (0, 0, t, 0)),
            pl.BlockSpec(part_rows, at_block),
            pl.BlockSpec(part_rows, at_block),
            anywhere,
            anywhere,
        ]
        + [anywhere] * (2 * len(far_came))
        + [
            full((rows, rows)),
        ]
        + [full((1, channels))] * 4,
        [full(runs), full(runs)]
        + [pl.BlockSpec(part_rows, at_block)] * 4
        + [full((chunks, SUB, channels)), full((2, SUB, channels)), full((SUB, channels))],
        grid=(blocks,),
        scratch=[
            pltpu.VMEM((chunks, SUB, channels), F32),
            pltpu.VMEM((chunks, SUB, channels), F32),
            pltpu.VMEM((2 * planes, SUB, channels), F32),
            pltpu.VMEM((chunks, rows, channels), BF16),
            pltpu.VMEM((2, low * rows, channels), BF16),
            pltpu.SemaphoreType.DMA((2, len(far_came))),
        ],
        lengths=True,
        cost_estimate=cost(60 * elements, 30 * elements, 4 * elements),
        name="states",
    )(
        scalars, seq_lengths, *gathered, maps, mixed, reset_mixed, highway, own_half, own_cross, *far_came, *far_cross,
        order, fp, rp, fb, rb,
    )
    out_own, out_far, previous, direct, reset_z, skip, binj, reset_sums, run_back = state_out

    if short:
        places = [[(0, 1, 1), (1, 1, 2)], [(0, 0, 1), (3, 1, 2)], [(2, 1, 1), (1, 0, 2)], [(2, 0, 1), (3, 0, 2)]]
        part_shapes = [(2, half, channels)] * 4
    else:
        places = [[(d, 0, 0)] for d in visits]
        part_shapes = [(1, part, channels)] * planes

    def weight_part(sources, name):
        found = call(
            functools.partial(weight_grad_kernel, len(sources), places),
            [shape_of(shape, BF16) for shape in part_shapes] * len(sources),
            [pl.BlockSpec((chunks, rows, part), lambda t, s: (0, 0, s[info.visits + t]))]
            + [full((chunks, rows, channels))] * len(sources),
            [full(shape) for shape in part_shapes] * len(sources),
            grid=(planes,),
            cost_estimate=cost(2 * chunks * rows * width * channels * len(sources), 4 * chunks * rows * width),
            name=name,
        )(scalars, normed, *sources)
        return [found[n * len(part_shapes) : (n + 1) * len(part_shapes)] for n in range(len(sources))]

    def first_sends(parts):
        if short:
            return [cross_plane(parts[0], 1), cross_plane(parts[1], 2)]
        return [cross_plane(parts[d], d) for d in others]

    def second_start(parts, came):
        if not short:
            return came
        return [add_up([parts[2][1], came[0][1]]), add_up([parts[3][1], came[1][1]])]

    def second_sends(over):
        return [cross_plane(over[0], 2), cross_plane(over[1], 1)] if short else []

    def ends_of(parts, came, over):
        if not short:
            return [parts[0]] + came
        return [parts[2], came[0], over[0][None], parts[3], came[1], over[1][None]]

    def second_end(parts, came, over):
        ends = [value[0] for value in ends_of(parts, came, over)]
        if not short:
            return add_up(ends)
        return jnp.concatenate([add_up(ends[:3]), add_up(ends[3:])], axis=0)

    def to_owners(which, values, chosen):
        back_plan = back_routes[which][2]
        return [
            move_nodes(values[r], [(e[1], e[0]) for e in back_plan[r]]) for r in range(len(back_plan))[chosen]
        ]

    near_back = [run_back] + [cross_plane(run_back, d) for d in others]
    out_core = cross_core(out_far)
    (reset_wg,) = weight_part([reset_z], "weight_grad_reset")
    near_back, reset_wg, out_core, out_own = settle(near_back, reset_wg, out_core, out_own)

    far_back = cross_high(jnp.stack(near_back))
    reset_came = first_sends(reset_wg)
    stay = jnp.where(k == zhi, out_own, out_core)
    leave = jnp.where(k == zhi, out_core, out_own).reshape(half_rows, channels)
    near_back, far_back, leave, binj = settle(near_back, far_back, leave, binj)
    gathered_back = near_back + [far_back]

    leave = [leave[: half_rows // 2], leave[half_rows // 2 :]]
    out_came = [cross_high(leave[0])]

    grad_c, grad_f, forget_sums = call(
        functools.partial(back_kernel, info, low, planes, seg),
        (
            shape_of((chunks, rows, channels), BF16),
            shape_of((chunks, rows, channels), BF16),
            shape_of((2, SUB, channels), F32),
        ),
        map_specs * 2
        + [
            full((chunks, 2, SUB, channels)),
            full((chunks, SUB, channels)),
            pl.BlockSpec((chunks, 2, block, channels), lambda t, *_: (0, 0, blocks - 1 - t, 0)),
        ]
        + [pl.BlockSpec(part_rows, lambda t, *_: (0, blocks - 1 - t, 0))] * 3
        + [full((1, channels))] * 3,
        [pl.BlockSpec(part_rows, lambda t, *_: (0, blocks - 1 - t, 0))] * 2 + [full((2, SUB, channels))],
        grid=(blocks,),
        scratch=[
            pltpu.VMEM((chunks, SUB, channels), F32),
            pltpu.VMEM((2 * planes, SUB, channels), F32),
            pltpu.VMEM((2 * planes, SUB, channels), F32),
        ],
        lengths=True,
        cost_estimate=cost(30 * elements, 20 * elements, 2 * elements),
        name="state_grads",
    )(scalars, seq_lengths, *gathered, *gathered_back, maps, binj, mixed, previous, direct, reset_z, fp, rp, fb)

    def chunk_grads(chosen, sources):
        each = []
        for c in chosen:
            chunk_block = pl.BlockSpec((1, rows, channels), lambda t, s, c=c: (c, 0, 0))
            each += [chunk_block] * 3
            each += [
                pl.BlockSpec((1, rows, channels), lambda t, s, c=c: (c, 0, t)),
                pl.BlockSpec((1, rows, LANES), lambda t, s, c=c: (c, 0, 0)),
                chunk_block,
            ]
        count = len(chosen)
        found = call(
            functools.partial(input_kernel, info, count),
            [shape_of((rows, width), BF16)] * count
            + [shape_of((SUB, rows), F32)] * count
            + [shape_of((2, SUB, width), F32)],
            [
                pl.BlockSpec((3, channels, channels), lambda t, s: (0, t, 0)),
                pl.BlockSpec((1, channels), lambda t, s: (0, t)),
            ]
            + each,
            [pl.BlockSpec((rows, channels), lambda t, s: (0, t))] * count
            + [full((SUB, rows))] * count
            + [pl.BlockSpec((2, SUB, channels), lambda t, s: (0, 0, t))],
            grid=(groups,),
            scratch=[
                pltpu.VMEM((count, rows, channels), F32),
                pltpu.VMEM((count, rows, LANES), F32),
                pltpu.VMEM((count, rows, LANES), F32),
            ],
            cost_estimate=cost(6 * count * rows * width * channels, (8 * rows * count + 6 * channels) * width),
            name="chunk_grads",
        )(scalars, full_weight, gain2, *(list(sources) + [hats, invs, skip]) * count)
        norm_sums.append(found[2 * count])
        return found[:count], found[count : 2 * count]

    norm_sums = []

    grad_c, grad_f, reset_came = settle(grad_c, grad_f, reset_came)
    over = second_start(reset_wg, reset_came)
    grad_c, over = settle(grad_c, over)

    reset_over = second_sends(over)
    (candidate_wg,) = weight_part([grad_c], "weight_grad_candidate")
    candidate_wg, reset_over, out_came, leave = settle(candidate_wg, reset_over, out_came, leave)
    out_came.append(cross_high(leave[1]))
    candidate_wg, grad_f = settle(candidate_wg, grad_f)

    candidate_came = first_sends(candidate_wg)
    (forget_wg,) = weight_part([grad_f], "weight_grad_forget")
    forget_wg, candidate_came = settle(forget_wg, candidate_came)
    over = second_start(candidate_wg, candidate_came)
    sources = (grad_c, grad_f, reset_z)
    over, forget_wg, sources = settle(over, forget_wg, sources)

    candidate_over = second_sends(over)
    forget_came = first_sends(forget_wg)
    far_pairs = [chunk_grads([low + dz, dz], sources) for dz in lows]
    far_pairs, candidate_over, forget_came, out_came, sources = settle(
        far_pairs, candidate_over, forget_came, out_came, sources
    )
    over = second_start(forget_wg, forget_came)
    ends = ends_of(candidate_wg, candidate_came, candidate_over) + ends_of(reset_wg, reset_came, reset_over)
    candidate_part, reset_part, *sends = call(
        functools.partial(pick_kernel, info, len(ends) // 2),
        [shape_of((part, channels), BF16)] * (2 + len(back_routes[0][2])),
        [full((1,) + value.shape[1:]) for value in ends],
        [full((part, channels))] * (2 + len(back_routes[0][2])),
        cost_estimate=cost(0, 3 * part * channels),
        name="pick_parts",
    )(scalars, *ends)
    sends, over, sources, far_pairs = settle(sends, over, sources, far_pairs)

    forget_over = second_sends(over)
    owned_parts = to_owners(0, sends, slice(0, 1))
    from_core = [cross_core(values[0]) for values, _ in far_pairs]
    (other_value,), (other_sums,) = chunk_grads([low], sources)
    other_value, other_sums, forget_over, owned_parts, from_core, sends, sources = settle(
        other_value, other_sums, forget_over, owned_parts, from_core, sends, sources
    )
    forget_part = second_end(forget_wg, forget_came, forget_over)
    forget_part, sends, sources, far_pairs, from_core = settle(forget_part, sends, sources, far_pairs, from_core)

    owned_parts = owned_parts + to_owners(0, sends, slice(1, None))
    last_parts = to_owners(1, [forget_part] * len(back_routes[1][2]), slice(0, 1))
    value_core, sums_core = cross_core(other_value), cross_core(other_sums)
    sums_across = [cross_core(sums[0]) for _, sums in far_pairs]
    (own_value,), (own_sums,) = chunk_grads([0], sources)
    sixteen = rows // 32
    v_cuts = [(0, rows)]
    (
        own_value, own_sums, owned_parts, last_parts, value_core, sums_core, sums_across, far_pairs, from_core, forget_part,
    ) = settle(
        own_value, own_sums, owned_parts, last_parts, value_core, sums_core, sums_across, far_pairs, from_core, forget_part
    )
    far_sums = [sums[1] + sums_across[n] for n, (_, sums) in enumerate(far_pairs)]
    v_sends = [
        [
            add_up([values[1][start : start + size], from_core[n][start : start + size]])
            for n, (values, _) in enumerate(far_pairs)
        ]
        for start, size in v_cuts
    ]

    gate_sums = jnp.sum(jnp.concatenate([forget_sums, reset_sums]), axis=1)
    spread_sums = lax.dynamic_update_slice(
        jnp.zeros((4, width), F32), gate_sums, (0, (z % low + low * k) * channels)
    )
    small = jnp.concatenate([jnp.sum(sum(norm_sums[1:], norm_sums[0]), axis=1), spread_sums], axis=0)
    last_parts = last_parts + to_owners(1, [forget_part] * len(back_routes[1][2]), slice(1, None))
    small_came = cross_low(small, 1)
    far_sums = [cross_low(sums, dz) for dz, sums in zip(lows, far_sums)]
    last_parts, small, small_came, far_sums, v_sends = settle(last_parts, small, small_came, far_sums, v_sends)
    v_came = [[cross_low(value, dz) for dz, value in zip(lows, v_sends[0])]]
    small = small + small_came
    sums = sum([sums_core] + far_sums, own_sums)
    owned_parts = owned_parts + [candidate_part, reset_part] + last_parts + [forget_part]

    block_piece = (3, half, channels)
    own_blocks, give_blocks = call(
        functools.partial(owned_kernel, info, len(owned_parts)),
        [shape_of(block_piece, BF16)] * 2,
        [anywhere] * len(owned_parts),
        [full(block_piece)] * 2,
        scratch=[
            pltpu.VMEM((3, part, channels), F32),
            pltpu.VMEM((len(owned_parts), part, channels), BF16),
            pltpu.SemaphoreType.DMA((len(owned_parts),)),
        ],
        cost_estimate=cost(0, 6 * part * channels),
        name="own_blocks",
    )(scalars, *owned_parts)
    own_blocks, give_blocks, small = settle(own_blocks, give_blocks, small)

    give_blocks = cross_core(give_blocks)
    own_blocks, give_blocks = settle(own_blocks, give_blocks)
    own_sum = add_up([own_blocks, give_blocks])
    own_sum, small, sums = settle(own_sum, small, sums)

    def spread(name, values, steps, held):
        return call(
            functools.partial(spread_kernel, len(values), steps),
            shape_of((width, 3 * channels), F32),
            [full(value.shape) for value in values] + [anywhere] * len(held),
            pl.BlockSpec((quarter, 3 * channels), lambda t, s: (s[getattr(info, name) + t], 0)),
            grid=(len(steps),),
            aliases={1 + len(values): 0} if held else None,
            cost_estimate=cost(0, 9 * width * channels),
            name="spread_" + name,
        )(scalars, *values, *held)

    whole = [own_sum] + [cross_plane(own_sum, d) for d in (others[:2] if short else others)]
    whole_core = [cross_core(own_sum)]
    small_came = cross_core(small)
    output = call(
        functools.partial(output_kernel, info, low, [value.shape[0] for value in out_came]),
        shape_of((2, half_rows, channels), BF16),
        [full((rows, rows)), full((half_rows, channels))] + [full(value.shape) for value in out_came],
        full((2, half_rows, channels)),
        scratch=[pltpu.VMEM((half_rows, channels), BF16)],
        cost_estimate=cost(4 * low * rows * rows * channels, 8 * half_rows * channels),
        name="output",
    )(scalars, back_order, stay.reshape(half_rows, channels), *out_came)
    weight_grad = spread("own_rows", [own_sum], [(0, 0), (0, quarter)], ())
    input_part = pl.pallas_call(
        input_part_kernel,
        grid=(rows // wide,),
        in_specs=[
            pl.BlockSpec((wide, width), lambda t: (t, 0)),
            pl.BlockSpec((wide, rows), lambda t: (t, 0)),
            full((rows, width)),
            full((rows, width)),
            full((SUB, rows)),
        ],
        out_specs=pl.BlockSpec((wide, width), lambda t: (t, 0)),
        out_shape=shape_of((rows, width), F32),
        compiler_params=params(),
        cost_estimate=cost(4 * rows * rows * width, 10 * rows * width),
        name="input_part",
    )(inputs, back_order, own_value, value_core, sums)
    whole, whole_core, small, small_came, input_part, output, weight_grad = settle(
        whole, whole_core, small, small_came, input_part, output, weight_grad
    )
    small = small + small_came
    output = output.reshape(groups * rows, channels)

    split = []
    if short:
        split = [whole[1][:, :quarter], whole[2][:, quarter:]]
        whole, split, small = settle(whole, split, small)
        split = [cross_plane(split[0], 2), cross_plane(split[1], 1)]
    whole_core += [cross_core(value) for value in whole[1:]]
    values = whole[1:] + whole_core
    steps = [(n, at) for n in range(len(values)) for at in (0, quarter)]
    weight_grad = spread("near_rows", values, steps, (weight_grad,))
    weight_grad, split, whole_core, small = settle(weight_grad, split, whole_core, small)

    bits = bits_of(planes)
    small_came = cross_plane(small, bits[0])
    split_core = [cross_core(value) for value in split]
    if short:
        weight_grad = spread("far_rows", split, [(0, 0), (1, 0)], (weight_grad,))
    split_core, small, small_came, weight_grad = settle(split_core, small, small_came, weight_grad)
    small = small + small_came

    small_came = [cross_plane(small, bit) for bit in bits[1:2]]
    if short:
        weight_grad = spread("last_rows", split_core, [(0, 0), (1, 0)], (weight_grad,))
    small, small_came, weight_grad, v_came = settle(small, small_came, weight_grad, v_came)
    small = sum(small_came, small)
    for bit in bits[2:]:
        small = small + cross_plane(small, bit)
    for bit in bits_of(groups)[1:]:
        small = small + cross_low(small, bit)

    parts = [(start, value) for (start, _), came_now in zip(v_cuts, v_came) for value in came_now]
    input_grad = pl.pallas_call(
        functools.partial(last_kernel, [start for start, _ in parts]),
        grid=(rows // wide,),
        in_specs=[pl.BlockSpec((wide, width), lambda t: (t, 0)), pl.BlockSpec((wide, rows), lambda t: (t, 0))]
        + [full(value.shape) for _, value in parts],
        out_specs=pl.BlockSpec((wide, width), lambda t: (t, 0)),
        out_shape=shape_of((rows, width), F32),
        input_output_aliases={0: 0},
        compiler_params=params(),
        cost_estimate=cost(2 * rows * rows * width, 10 * rows * width),
        name="input_grad",
    )(input_part, back_order, *[value for _, value in parts])
    gate_block = lax.dynamic_slice_in_dim(small[2:], z * channels, channels, 1)
    return (
        output,
        input_grad,
        weight_grad,
        small[0],
        small[1],
        gate_block[1],
        gate_block[3],
        gate_block[0],
        gate_block[2],
    )


def solution(mesh):
    placed = (
        P(("seq", "col"), None),
        P(),
        P(),
        P(None, "col"),
        P("col"),
        P("col"),
        P("col"),
        P("col"),
        P(),
        P("seq", "col"),
    )
    return jax.shard_map(
        per_device,
        mesh=mesh,
        in_specs=placed,
        out_specs=(
            P("seq", "col"),
            P(("seq", "col"), None),
            P(None, "col"),
            P(),
            P(),
            P("col"),
            P("col"),
            P("col"),
            P("col"),
        ),
        check_vma=False,
    )
```

```python
import functools

import jax
import jax.numpy as jnp
import numpy as np
from jax import lax
from jax.experimental import pallas as pl
from jax.experimental.pallas import tpu as pltpu
from jax.sharding import PartitionSpec as P

EPSILON = 1e-05
F32 = jnp.float32
BF16 = jnp.bfloat16
LANES = 128
SUB = 8
VMEM_LIMIT = 56 * 1024 * 1024


def bits_of(count):
    return [1 << b for b in range(count.bit_length() - 1)]


def colour(edges, count):
    degree = max([sum(e[0] == n for e in edges) for n in range(count)] + [sum(e[1] == n for e in edges) for n in range(count)])
    out = [[None] * degree for _ in range(count)]
    into = [[None] * degree for _ in range(count)]
    taken = {}
    for at, edge in enumerate(edges):
        src, dst = edge[0], edge[1]
        first = next(c for c in range(degree) if out[src][c] is None)
        second = next(c for c in range(degree) if into[dst][c] is None)
        if first != second:
            path, node, at_dst, look = [], dst, True, first
            while True:
                found = (into if at_dst else out)[node][look]
                if found is None:
                    break
                path.append(found)
                node = edges[found][0] if at_dst else edges[found][1]
                at_dst = not at_dst
                look = second if look == first else first
            for found in path:
                old = taken[found]
                out[edges[found][0]][old] = None
                into[edges[found][1]][old] = None
            for found in path:
                new = second if taken[found] == first else first
                taken[found] = new
                out[edges[found][0]][new] = found
                into[edges[found][1]][new] = found
        taken[at] = first
        out[src][first] = at
        into[dst][first] = at
    rounds = [[] for _ in range(degree)]
    for at, edge in enumerate(edges):
        rounds[taken[at]].append(edge)
    return rounds


def busiest(edges, groups):
    links = {}
    for src, dst, _, _ in edges:
        a, b = src % groups, dst % groups
        for n in range(min(a, b), max(a, b)):
            links[n, a < b] = links.get((n, a < b), 0) + 1
    return max(links.values(), default=0)


def balance(rounds, groups):
    if len(rounds) != 2:
        return rounds
    paths = []
    left = [(r, e) for r in range(2) for e in rounds[r]]
    while left:
        path = [left.pop()]
        grown = True
        while grown:
            near = [x for x in left if any(x[1][0] == y[1][0] or x[1][1] == y[1][1] for y in path)]
            left = [x for x in left if x not in near]
            path += near
            grown = bool(near)
        paths.append(path)
    best = None
    for flips in range(2 ** len(paths)):
        tried = [[], []]
        for n, path in enumerate(paths):
            for r, edge in path:
                tried[r ^ (flips >> n & 1)].append(edge)
        score = sum(busiest(edges, groups) for edges in tried)
        score = (max(busiest(edges, groups) for edges in tried), score)
        if best is None or score < best[0]:
            best = (score, tried)
    return best[1]


def routes(groups, streams):
    low = groups // 2
    local, edges = [], []
    load = [0] * (2 * groups)
    for core in range(2):
        for z in range(groups):
            for stream in streams:
                block = stream * groups + z % low + low * core
                owner, at = block // 3, block % 3
                dst = core * groups + z
                if owner == z:
                    local.append((dst, dst, stream, at))
                else:
                    edges.append([core, owner, dst, stream, at])
    found = []
    for owner in range(groups):
        mine = [e for e in edges if e[1] == owner]
        quota = -(-len(mine) // 2)
        for core, _, dst, stream, at in mine:
            src = core * groups + owner
            if load[src] == quota:
                src = (1 - core) * groups + owner
            load[src] += 1
            found.append((src, dst, stream, at))
    return local, balance(colour(found, 2 * groups), groups)


def row_order(rows):
    seg = rows // SUB
    matrix = np.zeros((rows, rows), np.float32)
    for i in range(seg):
        for j in range(SUB):
            matrix[i * SUB + j, j * seg + i] = 1.0
    return matrix


def gate(value):
    small = jnp.exp(-jnp.abs(value))
    minor = small / (1.0 + small)
    major = 1.0 - minor
    up = value >= 0.0
    return jnp.where(up, major, minor), jnp.where(up, minor, major)


def kept_of(base, step, seg, bounds, channels):
    at = lax.broadcasted_iota(jnp.int32, (SUB, LANES), 0) * seg + (base + step)
    starts = at == bounds[0]
    for bound in bounds[1:]:
        starts = starts | (at == bound)
    kept = jnp.where(starts, 0.0, 1.0)
    return jnp.concatenate([kept] * (channels // LANES), axis=1)


class Info:
    def __init__(self):
        self.spots = {}
        self.columns = []

    def put(self, name, values):
        self.spots[name] = len(self.columns)
        self.columns += list(np.asarray(values, np.int32))

    def __getattr__(self, name):
        return self.spots[name]

    def table(self):
        return np.stack(self.columns, axis=1)


def bounds_of(lengths):
    starts = [0]
    for n in range(lengths.shape[0] - 1):
        starts.append(starts[-1] + lengths[n])
    return starts


def cut_kernel(count, s, *refs):
    for n in range(count):
        refs[count + n][...] = refs[n][...]


def pick_kernel(info, count, s, *refs):
    ins, outs = refs[: 2 * count], refs[2 * count :]
    totals, rounds = outs[:2], outs[2:]
    for n, total in enumerate(totals):
        mine = ins[n * count : (n + 1) * count]
        half = total.shape[0] // 2 if count == 6 else total.shape[0]
        groups_of = (mine[:3], mine[3:]) if count == 6 else (mine,)
        for m, parts in enumerate(groups_of):
            found = [part[...] if len(part.shape) == 2 else part[0] for part in parts]
            value = found[0].astype(F32)
            for part in found[1:]:
                value = value + part.astype(F32)
            total[m * half : (m + 1) * half] = value.astype(BF16)
    for r, out in enumerate(rounds):
        for n, total in enumerate(totals):

            @pl.when(s[info.back_stream + r] == n)
            def _():
                out[...] = total[...]


def norm_rows(x_ref, gain, bias, normed_ref, hat_ref, inv_ref):
    block = 32
    for r in range(x_ref.shape[0] // block):
        at = slice(r * block, (r + 1) * block)
        x = x_ref[at].astype(F32)
        average = jnp.mean(x, axis=1, keepdims=True)
        centred = x - average
        inv = lax.rsqrt(jnp.mean(centred * centred, axis=1, keepdims=True) + EPSILON)
        hat = centred * inv
        normed_ref[0, at] = (hat * gain + bias).astype(BF16)
        hat_ref[0, at] = hat.astype(BF16)
        inv_ref[0, at] = jnp.broadcast_to(inv, (block, LANES))


def group_columns(info, s, channels):
    return pl.ds(pl.multiple_of(s[info.g] * channels, channels), channels)


def norm_kernel(info, s, x_ref, gain_ref, bias_ref, *refs):
    normed_ref, hx_ref, hat_ref, inv_ref = refs[-4:]
    norm_rows(x_ref, gain_ref[...], bias_ref[...], normed_ref, hat_ref, inv_ref)
    hx_ref[0] = x_ref[:, group_columns(info, s, hx_ref.shape[2])]


def segment_maps(base, seg, lengths, mixed_ref, fp, fb):
    channels = mixed_ref.shape[3]
    run_decay = jnp.ones((SUB, channels), F32)
    run_state = jnp.zeros((SUB, channels), F32)
    bounds = bounds_of(lengths)
    for i in range(mixed_ref.shape[2] // SUB):
        at = slice(i * SUB, (i + 1) * SUB)
        candidate = mixed_ref[0, 0, at].astype(F32)
        forget, rest = gate(mixed_ref[0, 1, at].astype(F32) + fp * candidate + fb)
        decay = forget * kept_of(base, i, seg, bounds, channels)
        run_state = decay * run_state + rest * candidate
        run_decay = decay * run_decay
    return run_decay, run_state


def mix_kernel(info, low, planes, seg, here, away, split, s, lengths, normed_ref, fp_ref, fb_ref, *refs):
    part = refs[0].shape[-2]
    whole = [(d, 0, part) for d in range(planes)]
    if split:
        ends = [(3, 0, part // 2), (3, part // 2, part // 2)]
        here_parts = whole[:3] + ends
        away_parts = [(d, n * (part // 2), part // 2) for d in range(3) for n in range(2)] + ends
    else:
        here_parts = away_parts = whole
    count = here * len(here_parts) + len(away_parts)
    pieces = refs[:count]
    mixed_ref, map_ref, full_ref, w_ref, in_sem, out_sem = refs[count:]
    step = pl.program_id(0)

    def copies(slot):
        stream = s[info.slot_stream + slot]
        found = []
        for n, (d, start, size) in enumerate(here_parts if slot < here else away_parts):
            rows = pl.ds(pl.multiple_of((d ^ s[info.p]) * part + start, size), size)
            if slot < here:
                piece = pieces[slot * len(here_parts) + n]
            else:
                piece = pieces[here * len(here_parts) + n].at[slot - here]
            spot = slot * len(away_parts) + n
            found.append(pltpu.make_async_copy(piece, w_ref.at[stream, rows, :], in_sem.at[spot]))
        return found

    @pl.when(step == 0)
    def _():
        for slot in range(here + away):

            @pl.when(s[info.slot_stream + slot] >= 0)
            def _():
                for copy in copies(slot):
                    copy.start()

        for slot in range(here + away):

            @pl.when(s[info.slot_stream + slot] >= 0)
            def _():
                for copy in copies(slot):
                    copy.wait()

        pltpu.make_async_copy(w_ref, full_ref, out_sem).start()

    for stream in range(2):
        mixed_ref[0, stream] = jnp.dot(normed_ref[0], w_ref[stream], preferred_element_type=F32).astype(BF16)
    decay, state = segment_maps(s[info.base + step * low], seg, lengths, mixed_ref, fp_ref[...], fb_ref[...])
    map_ref[0, 0] = decay
    map_ref[0, 1] = state

    @pl.when(step == pl.num_programs(0) - 1)
    def _():
        pltpu.make_async_copy(w_ref, full_ref, out_sem).wait()


def mix_far_kernel(info, low, seg, order, sizes, s, lengths, w_ref, gain_ref, bias_ref, fp_ref, fb_ref, near_ref, *refs):
    count = len(order)
    pieces = refs[: len(sizes) * count]
    normed_ref, hx_ref, hat_ref, inv_ref, mixed_ref, map_ref, run_ref, x_ref, sem = refs[len(sizes) * count + 5 :]
    channels = w_ref.shape[2]
    step = pl.program_id(0)

    def copies(n):
        found, start = [], 0
        for m, size in enumerate(sizes):
            spot = n * len(sizes) + m
            found.append(pltpu.make_async_copy(pieces[spot], x_ref.at[n, pl.ds(start, size), :], sem.at[spot]))
            start += size
        return found

    @pl.when(step == 0)
    def _():
        for n in range(count):
            for copy in copies(n):
                copy.start()
        for dk in range(2):
            map_ref[dk * low] = near_ref[dk * low]

    for n in range(count):

        @pl.when(step == n)
        def _():
            for copy in copies(n):
                copy.wait()

    mine = x_ref.at[step]
    norm_rows(mine, gain_ref[...], bias_ref[...], normed_ref, hat_ref, inv_ref)
    hx_ref[0] = mine[:, group_columns(info, s, channels)]
    for stream in range(2):
        mixed_ref[0, stream] = jnp.dot(normed_ref[0], w_ref[stream], preferred_element_type=F32).astype(BF16)
    chunk = far_chunk(low, step)
    decay, state = segment_maps(s[info.base + chunk], seg, lengths, mixed_ref, fp_ref[...], fb_ref[...])
    map_ref[chunk, 0] = decay
    map_ref[chunk, 1] = state

    @pl.when(step == count - 1)
    def _():
        rows = []
        for dk in range(2):
            decay = jnp.ones((1, channels), F32)
            state = jnp.zeros((1, channels), F32)
            for zl in range(low):
                c = dk * low + (zl ^ s[info.zlo])
                for j in range(SUB):
                    d, b = map_ref[c, 0, j : j + 1, :], map_ref[c, 1, j : j + 1, :]
                    state = d * state + b
                    decay = d * decay
            rows += [decay, state]
        run_ref[...] = jnp.concatenate(rows + [jnp.zeros((4, channels), F32)], axis=0)


def reset_kernel(normed_ref, w_ref, *refs):
    refs[-1][0] = jnp.dot(normed_ref[0], w_ref[0], preferred_element_type=F32).astype(BF16)


def far_chunk(low, n):
    return n // (low - 1) * low + 1 + n % (low - 1)


def gathered_maps(info, planes, s, refs, into):
    for d in range(planes):
        plane = d ^ s[info.p]
        into[s[info.zhi] * planes + plane] = refs[d][...]
        into[(1 - s[info.zhi]) * planes + plane] = refs[planes][d]


def state_kernel(info, low, planes, seg, sizes, s, lengths, *refs):
    gathered_refs = refs[: planes + 1]
    map_ref, mixed_ref, reset_ref, hx_ref, og_ref, og_cross_ref = refs[planes + 1 : planes + 7]
    far_refs = refs[planes + 7 : planes + 7 + 2 * len(sizes)]
    (
        order_ref, fp_ref, rp_ref, fb_ref, rb_ref,
        out_ref, out_far_ref, prev_ref, direct_ref, rz_ref, skip_ref, binj_ref, sums_ref, runb_ref,
        cell_ref, prod_ref, gathered_ref, grad_ref, og_all_ref, og_sem,
    ) = refs[planes + 7 + 2 * len(sizes) :]
    chunks, channels = map_ref.shape[0], map_ref.shape[3]
    step = pl.program_id(0)
    last = pl.num_programs(0) - 1
    k, zlo = s[info.k], s[info.zlo]

    @pl.when(step == 0)
    def _():
        stays = s[info.zhi] == k
        here_copies = [
            pltpu.make_async_copy(ref, og_all_ref.at[n], og_sem.at[n, 0]) for n, ref in enumerate((og_ref, og_cross_ref))
        ]
        far_copies = []
        for n in range(2):
            start = 0
            for m, size in enumerate(sizes):
                target = og_all_ref.at[n, pl.ds(start, size), :]
                far_copies.append(pltpu.make_async_copy(far_refs[n * len(sizes) + m], target, og_sem.at[n, m]))
                start += size

        @pl.when(stays)
        def _():
            for copy in here_copies:
                copy.start()

        @pl.when(jnp.logical_not(stays))
        def _():
            for copy in far_copies:
                copy.start()

        gathered_maps(info, planes, s, gathered_refs, gathered_ref)
        carry = jnp.zeros((1, channels), F32)
        own = [carry, carry]
        for plane in range(planes):
            for core in range(2):
                for zh in range(2):
                    e = zh * planes + plane
                    mine = (plane == s[info.p]) & (zh == s[info.zhi])
                    own[core] = jnp.where(mine, carry, own[core])
                    decay = jnp.where(k == core, gathered_ref[e, 0:1, :], gathered_ref[e, 2:3, :])
                    state = jnp.where(k == core, gathered_ref[e, 1:2, :], gathered_ref[e, 3:4, :])
                    carry = decay * carry + state
        for dk in range(2):
            carry = jnp.where(k == 0, own[dk], own[1 - dk])
            for zl in range(low):
                c = dk * low + (zl ^ zlo)
                for j in range(SUB):
                    cell_ref[c, j : j + 1, :] = carry
                    carry = map_ref[c, 0, j : j + 1, :] * carry + map_ref[c, 1, j : j + 1, :]

        @pl.when(stays)
        def _():
            for copy in here_copies:
                copy.wait()

        @pl.when(jnp.logical_not(stays))
        def _():
            for copy in far_copies:
                copy.wait()

        chunk_rows = order_ref.shape[0]
        for c in range(chunks):
            dk, dz = c // low, c % low
            at = pl.ds(pl.multiple_of((dz ^ zlo) * chunk_rows, chunk_rows), chunk_rows)
            grad_ref[c] = jnp.dot(order_ref[...], og_all_ref[dk, at, :], preferred_element_type=F32).astype(BF16)
        prod_ref[...] = jnp.ones_like(prod_ref)
        binj_ref[...] = jnp.zeros_like(binj_ref)
        sums_ref[...] = jnp.zeros_like(sums_ref)

    rows = hx_ref.shape[1]
    bounds = bounds_of(lengths)
    fp, rp, fb, rb = fp_ref[...], rp_ref[...], fb_ref[...], rb_ref[...]
    rz_sum, peep_sum = sums_ref[0], sums_ref[1]
    first, second = slice(0, SUB), slice(SUB, 2 * SUB)
    for c in range(chunks):
        base = s[info.base + c]
        cell, prod, binj = cell_ref[c], prod_ref[c], binj_ref[c]
        for i in range(rows // (2 * SUB)):
            at = slice(2 * i * SUB, 2 * (i + 1) * SUB)
            now = step * (rows // SUB) + 2 * i
            candidate = mixed_ref[c, 0, at].astype(F32)
            forget, rest = gate(mixed_ref[c, 1, at].astype(F32) + fp * candidate + fb)
            inject = rest * candidate
            kept = [kept_of(base, now + n, seg, bounds, channels) for n in range(2)]
            previous = [kept[0] * cell]
            cells = [forget[first] * previous[0] + inject[first]]
            previous.append(kept[1] * cells[0])
            cell = forget[second] * previous[1] + inject[second]
            cells = jnp.concatenate([cells[0], cell], axis=0)
            previous = jnp.concatenate(previous, axis=0)
            reset, skip = gate(reset_ref[c, at].astype(F32) + rp * previous + rb)
            x = hx_ref[c, at].astype(F32)
            here = pl.ds(pl.multiple_of(step * rows + 2 * i * SUB, 2 * SUB), 2 * SUB)
            g = grad_ref[c, here, :].astype(F32)
            out = (reset * cells + skip * x).astype(BF16)
            (out_ref, out_far_ref)[c // low][(c % low) ^ zlo, here, :] = out
            direct = g * reset
            rz = direct * skip * (cells - x)
            prev_ref[c, at] = previous.astype(BF16)
            direct_ref[c, at] = direct.astype(BF16)
            rz_ref[c, at] = rz.astype(BF16)
            skip_ref[c, at] = (g * skip).astype(BF16)
            back = forget * direct + rz * rp
            for n, half in ((0, first), (1, second)):
                prod_kept = prod * kept[n]
                binj = binj + prod_kept * back[half]
                prod = prod_kept * forget[half]
            rz_sum = rz_sum + (rz[first] + rz[second])
            peep = rz * previous
            peep_sum = peep_sum + (peep[first] + peep[second])
        cell_ref[c] = cell
        prod_ref[c] = prod
        binj_ref[c] = binj
    sums_ref[0] = rz_sum
    sums_ref[1] = peep_sum

    @pl.when(step == last)
    def _():
        runs = []
        for dk in range(2):
            acc = jnp.zeros((1, channels), F32)
            for zl in reversed(range(low)):
                c = dk * low + (zl ^ zlo)
                for j in reversed(range(SUB)):
                    acc = binj_ref[c, j : j + 1, :] + map_ref[c, 0, j : j + 1, :] * acc
            runs.append(acc)
        runb_ref[...] = jnp.concatenate(runs + [jnp.zeros((6, channels), F32)], axis=0)


def back_kernel(info, low, planes, seg, s, lengths, *refs):
    gathered_refs, back_refs = refs[: planes + 1], refs[planes + 1 : 2 * planes + 2]
    (
        map_ref, binj_ref, mixed_ref, prev_ref, direct_ref, rz_ref, fp_ref, rp_ref, fb_ref,
        grad_c_ref, grad_f_ref, sums_ref,
        carry_ref, gathered_ref, back_ref,
    ) = refs[2 * planes + 2 :]
    chunks, channels = map_ref.shape[0], map_ref.shape[3]
    step = pl.program_id(0)
    count = pl.num_programs(0)
    k, zlo = s[info.k], s[info.zlo]

    @pl.when(step == 0)
    def _():
        gathered_maps(info, planes, s, gathered_refs, gathered_ref)
        gathered_maps(info, planes, s, back_refs, back_ref)
        carry = jnp.zeros((1, channels), F32)
        own = [carry, carry]
        for plane in reversed(range(planes)):
            for core in (1, 0):
                for zh in (1, 0):
                    e = zh * planes + plane
                    mine = (plane == s[info.p]) & (zh == s[info.zhi])
                    own[core] = jnp.where(mine, carry, own[core])
                    decay = jnp.where(k == core, gathered_ref[e, 0:1, :], gathered_ref[e, 2:3, :])
                    inject = jnp.where(k == core, back_ref[e, 0:1, :], back_ref[e, 1:2, :])
                    carry = decay * carry + inject
        for dk in range(2):
            carry = jnp.where(k == 0, own[dk], own[1 - dk])
            for zl in reversed(range(low)):
                c = dk * low + (zl ^ zlo)
                for j in reversed(range(SUB)):
                    carry_ref[c, j : j + 1, :] = carry
                    carry = map_ref[c, 0, j : j + 1, :] * carry + binj_ref[c, j : j + 1, :]
        sums_ref[...] = jnp.zeros_like(sums_ref)

    rows = prev_ref.shape[1]
    bounds = bounds_of(lengths)
    fp, rp, fb = fp_ref[...], rp_ref[...], fb_ref[...]
    fz_sum, peep_sum = sums_ref[0], sums_ref[1]
    first, second = slice(0, SUB), slice(SUB, 2 * SUB)
    for c in range(chunks):
        base = s[info.base + c]
        back = carry_ref[c]
        for i in reversed(range(rows // (2 * SUB))):
            at = slice(2 * i * SUB, 2 * (i + 1) * SUB)
            now = (count - 1 - step) * (rows // SUB) + 2 * i
            candidate = mixed_ref[c, 0, at].astype(F32)
            forget, rest = gate(mixed_ref[c, 1, at].astype(F32) + fp * candidate + fb)
            direct = direct_ref[c, at].astype(F32)
            prev_grad = rz_ref[c, at].astype(F32) * rp
            later = direct[second] + back
            back = kept_of(base, now + 1, seg, bounds, channels) * (forget[second] * later + prev_grad[second])
            sooner = direct[first] + back
            back = kept_of(base, now, seg, bounds, channels) * (forget[first] * sooner + prev_grad[first])
            held = jnp.concatenate([sooner, later], axis=0) * rest
            forget_z = held * forget * (prev_ref[c, at].astype(F32) - candidate)
            grad_c_ref[c, at] = (held + forget_z * fp).astype(BF16)
            grad_f_ref[c, at] = forget_z.astype(BF16)
            fz_sum = fz_sum + (forget_z[first] + forget_z[second])
            peep = forget_z * candidate
            peep_sum = peep_sum + (peep[first] + peep[second])
        carry_ref[c] = back
    sums_ref[0] = fz_sum
    sums_ref[1] = peep_sum


def input_kernel(info, count, s, w_ref, gain_ref, *refs):
    ins = [refs[6 * n : 6 * n + 6] for n in range(count)]
    outs = refs[6 * count :]
    v_refs, s_refs = outs[:count], outs[count : 2 * count]
    gb_ref, grad_ref, first_ref, second_ref = outs[2 * count :]
    tile = pl.program_id(0)
    nt = (((1,), (1,)), ((), ()))
    rows, width = grad_ref.shape[1:]
    flag = jnp.where(s[info.g] == tile, 1.0, 0.0)
    gain = gain_ref[...]
    block = 32
    gain_sum = jnp.zeros((SUB, width), F32)
    bias_sum = jnp.zeros((SUB, width), F32)

    @pl.when(tile == 0)
    def _():
        first_ref[...] = jnp.zeros_like(first_ref)
        second_ref[...] = jnp.zeros_like(second_ref)

    for n, (grad_c_ref, grad_f_ref, rz_ref, _, _, _) in enumerate(ins):
        grad = lax.dot_general(grad_c_ref[0], w_ref[0], nt, preferred_element_type=F32)
        grad = grad + lax.dot_general(grad_f_ref[0], w_ref[1], nt, preferred_element_type=F32)
        grad_ref[n] = grad + lax.dot_general(rz_ref[0], w_ref[2], nt, preferred_element_type=F32)
    for n, (_, _, _, hat_ref, inv_ref, skip_ref) in enumerate(ins):
        for r in range(rows // block):
            at = slice(r * block, (r + 1) * block)
            value = grad_ref[n, at]
            inv = jnp.concatenate([inv_ref[0, at]] * (width // LANES), axis=1)
            hat = hat_ref[0, at].astype(F32)
            scaled = value * gain
            product = scaled * hat
            first, second = first_ref[n, at], second_ref[n, at]
            for lane in range(width // LANES):
                first = first + scaled[:, lane * LANES : (lane + 1) * LANES]
                second = second + product[:, lane * LANES : (lane + 1) * LANES]
            first_ref[n, at] = first
            second_ref[n, at] = second
            matched = value * hat
            for i in range(block // SUB):
                gain_sum = gain_sum + matched[i * SUB : (i + 1) * SUB]
                bias_sum = bias_sum + value[i * SUB : (i + 1) * SUB]
            v_refs[n][at] = (scaled * inv + skip_ref[0, at].astype(F32) * flag).astype(BF16)
    gb_ref[0] = gain_sum
    gb_ref[1] = bias_sum

    @pl.when(tile == pl.num_programs(0) - 1)
    def _():
        lane = lax.broadcasted_iota(jnp.int32, (rows, LANES), 1)
        for n in range(count):
            first = jnp.sum(first_ref[n], axis=1, keepdims=True)
            second = jnp.sum(second_ref[n], axis=1, keepdims=True)
            s_refs[n][...] = jnp.where(lane == 0, first, jnp.where(lane == 1, second, 0.0)).T[:SUB]


def output_kernel(info, low, sizes, s, order_ref, stay_ref, *refs):
    came_refs, (out_ref, all_ref) = refs[: len(sizes)], refs[len(sizes) :]
    rows = order_ref.shape[0]
    start = 0
    for piece, size in zip(came_refs, sizes):
        all_ref[start : start + size] = piece[...]
        start += size
    order = order_ref[...]
    for n in range(low):
        at = slice(n * rows, (n + 1) * rows)
        out_ref[s[info.zhi], at] = jnp.dot(order, stay_ref[at], preferred_element_type=F32).astype(BF16)
        out_ref[1 - s[info.zhi], at] = jnp.dot(order, all_ref[at], preferred_element_type=F32).astype(BF16)


def input_part_kernel(x_ref, order_ref, own_ref, core_ref, s_ref, out_ref):
    width = x_ref.shape[1]
    x = x_ref[...].astype(F32)
    average = jnp.mean(x, axis=1, keepdims=True)
    centred = x - average
    inv = lax.rsqrt(jnp.mean(centred * centred, axis=1, keepdims=True) + EPSILON)
    order = order_ref[...]
    value = jnp.dot(order, own_ref[...], preferred_element_type=F32)
    value = value + jnp.dot(order, core_ref[...], preferred_element_type=F32)
    sums = lax.dot_general(
        order.astype(F32), s_ref[...], (((1,), (1,)), ((), ())),
        precision=lax.Precision.HIGHEST, preferred_element_type=F32,
    )
    first = sums[:, 0:1] * (1.0 / width)
    second = sums[:, 1:2] * (1.0 / width)
    out_ref[...] = value - inv * (first + centred * inv * second)


def last_kernel(starts, part_ref, order_ref, *refs):
    pieces, out_ref = refs[: len(starts)], refs[len(starts)]
    order = order_ref[...]
    value = part_ref[...]
    for start, piece in zip(starts, pieces):
        value = value + jnp.dot(order[:, start : start + piece.shape[0]], piece[...], preferred_element_type=F32)
    out_ref[...] = value


def weight_grad_kernel(count, order, s, normed_ref, *refs):
    grads, outs = refs[:count], refs[count:]
    each = len(outs) // count
    tn = (((0,), (0,)), ((), ()))
    for n in range(count):
        total = lax.dot_general(normed_ref[0], grads[n][0], tn, preferred_element_type=F32)
        for c in range(1, normed_ref.shape[0]):
            total = total + lax.dot_general(normed_ref[c], grads[n][c], tn, preferred_element_type=F32)
        low = total.astype(BF16)
        half = low.shape[0] // 2
        for at, places in enumerate(order):

            @pl.when(pl.program_id(0) == at)
            def _():
                for ref, place, rows in places:
                    outs[n * each + ref][place] = (low, low[:half], low[half:])[rows]


def owned_kernel(info, count, s, *refs):
    came, outs, total_ref, slot_ref, sem = refs[:count], refs[count : count + 2], *refs[count + 2 :]
    total_ref[...] = jnp.zeros_like(total_ref)
    for wait in (False, True):
        for n in range(count):

            @pl.when(s[info.owned + n] >= 0)
            def _():
                copy = pltpu.make_async_copy(came[n], slot_ref.at[n], sem.at[n])
                if not wait:
                    copy.start()
                else:
                    copy.wait()
                    total_ref[s[info.owned + n]] += slot_ref[n].astype(F32)

    half = total_ref.shape[1] // 2
    for n, out in enumerate(outs):
        core = s[info.k] if n == 0 else 1 - s[info.k]
        rows = pl.ds(pl.multiple_of(core * half, half), half)
        for block in range(3):
            out[block] = total_ref[block, rows, :].astype(BF16)


def spread_kernel(count, steps, s, *refs):
    pieces, out_ref = refs[:count], refs[-1]
    rows, channels = out_ref.shape[0], pieces[0].shape[2]
    for n, (piece, start) in enumerate(steps):

        @pl.when(pl.program_id(0) == n)
        def _():
            for block in range(3):
                values = pieces[piece][block, start : start + rows]
                out_ref[:, block * channels : (block + 1) * channels] = values.astype(F32)


def cost(flops, moved, exps=0):
    return pl.CostEstimate(flops=int(flops) // 20, bytes_accessed=int(moved) // 20, transcendentals=int(exps) // 20)


def per_device(
    inputs, norm_gain, norm_bias, weight, forget_peep, reset_peep, forget_bias, reset_bias, seq_lengths, out_grad
):
    rows, width = inputs.shape
    seqs, groups = lax.axis_size("seq"), lax.axis_size("col")
    planes, low = seqs // 2, groups // 2
    channels = width // groups
    chunks = groups
    seg = rows // SUB
    part = width // planes
    half, quarter = part // 2, part // 4
    seq, z = lax.axis_index("seq"), lax.axis_index("col")
    k, zhi = seq % 2, z // low
    params = functools.partial(pltpu.CompilerParams, vmem_limit_bytes=VMEM_LIMIT)
    others = range(1, planes)
    short = planes == 4
    anywhere = pl.BlockSpec(memory_space=pl.ANY)
    full = lambda shape: pl.BlockSpec(shape, lambda *_: (0,) * len(shape))
    shape_of = jax.ShapeDtypeStruct

    def move(value, to):
        pairs = []
        for a in range(seqs):
            for b in range(groups):
                target = to(a // 2, a % 2, b)
                if target is not None:
                    pairs.append((a * groups + b, (target[0] * 2 + target[1]) * groups + target[2]))
        return lax.ppermute(value, ("seq", "col"), pairs)

    def cross_core(value):
        return move(value, lambda p, k, z: (p, 1 - k, z))

    def cross_low(value, dz):
        return move(value, lambda p, k, z: (p, k, z ^ dz))

    def cross_high(value):
        return move(value, lambda p, k, z: (p, k, (z + low) % groups))

    def cross_plane(value, dp):
        return move(value, lambda p, k, z: (p ^ dp, k, z))

    def move_nodes(value, pairs):
        spot = lambda p, n: (2 * p + n // groups) * groups + n % groups
        return lax.ppermute(
            value, ("seq", "col"), [(spot(p, src), spot(p, dst)) for p in range(planes) for src, dst in pairs]
        )

    def after(values, *first):
        return lax.optimization_barrier((values, first))[0]

    def add_up(values):
        total = values[0].astype(F32)
        for value in values[1:]:
            total = total + value.astype(F32)
        return total.astype(BF16)

    device = np.arange(seqs * groups)
    dev_p, dev_k, dev_z = device // groups // 2, device // groups % 2, device % groups
    dev_zhi, dev_zlo = dev_z // low, dev_z % low
    info = Info()
    for name, value in (("p", dev_p), ("k", dev_k), ("zhi", dev_zhi), ("zlo", dev_zlo), ("g", dev_zlo + low * dev_k)):
        info.put(name, [value])
    info.put(
        "base",
        [((2 * dev_p + (dev_k ^ (c // low))) * groups + dev_zhi * low + (dev_zlo ^ (c % low))) * rows for c in range(chunks)],
    )
    node = dev_k * groups + dev_z
    at_dev = lambda table: np.asarray(table, np.int32)[:, node]
    local, plan = routes(groups, range(3))
    rounds = len(plan)
    here = max(sum(e[1] == n for e in local) for n in range(2 * groups))
    slot_stream = np.full((here + rounds, 2 * groups), -1)
    cut_block = np.zeros((rounds + here, 2 * groups))
    for r, edges in enumerate(plan):
        for src, dst, stream, at in edges:
            cut_block[r, src] = at
            slot_stream[here + r, dst] = stream
    for n in range(2 * groups):
        for at, edge in enumerate(edge for edge in local if edge[1] == n):
            slot_stream[at, n] = edge[2]
            cut_block[rounds + at, n] = edge[3]
    info.put("slot_stream", at_dev(slot_stream))
    info.put("cut_block", at_dev(cut_block))
    back_routes = [(streams, *routes(groups, streams)) for streams in ([0, 2], [1])]
    owned, back_stream = [], []
    for streams, back_local, back_plan in back_routes:
        for edges in back_plan:
            takes = np.full(2 * groups, -1)
            source = np.zeros(2 * groups)
            for src, dst, stream, at in edges:
                takes[src] = at
                source[dst] = streams.index(stream)
            owned.append(takes)
            back_stream.append(source)
        for stream in streams:
            takes = np.full(2 * groups, -1)
            for src, _, found, at in back_local:
                if found == stream:
                    takes[src] = at
            owned.append(takes)
    info.put("owned", at_dev(owned))
    info.put("back_stream", at_dev(back_stream[: len(back_routes[0][2])]))
    visits = [3, 1, 2, 0] if short else list(range(planes))
    info.put("visits", [dev_p ^ d for d in visits])
    def piece_rows(d, dk):
        return [((dev_p ^ d) * 2 + (dev_k ^ dk)) * 2 + n for n in range(2)]

    whole_planes = range(3 if short else planes)
    def half_rows_of(d, dk):
        return [(dev_p ^ d) * 2 + (dev_k ^ dk)]

    info.put("own_rows", half_rows_of(0, 0))
    info.put("near_rows", sum([half_rows_of(d, 0) for d in whole_planes[1:]] + [half_rows_of(d, 1) for d in whole_planes], []))
    info.put("far_rows", piece_rows(3, 0) if short else [])
    info.put("last_rows", piece_rows(3, 1) if short else [])
    scalars = lax.dynamic_index_in_dim(jnp.asarray(info.table()), seq * groups + z, 0, keepdims=False)

    order = jnp.asarray(row_order(rows), BF16)
    back_order = jnp.asarray(row_order(rows).T.copy(), BF16)

    tile = 128 if rows % 128 == 0 else rows
    tiles = rows // tile

    def call(kernel, out_shape, in_specs, out_specs, grid=(1,), scratch=(), lengths=False, aliases=None, **rest):
        return pl.pallas_call(
            kernel,
            grid_spec=pltpu.PrefetchScalarGridSpec(
                num_scalar_prefetch=2 if lengths else 1,
                grid=grid,
                in_specs=in_specs,
                out_specs=out_specs,
                scratch_shapes=list(scratch),
            ),
            out_shape=out_shape,
            input_output_aliases=aliases or {},
            compiler_params=params(),
            **rest,
        )

    def settle(*values):
        return lax.optimization_barrier(values)

    gain2, bias2 = norm_gain[None, :], norm_bias[None, :]

    row_shapes = (
        shape_of((chunks, rows, width), BF16),
        shape_of((chunks, rows, channels), BF16),
        shape_of((chunks, rows, width), BF16),
        shape_of((chunks, rows, LANES), F32),
    )
    mix_shapes = (shape_of((chunks, 2, rows, channels), BF16), shape_of((chunks, 2, SUB, channels), F32))
    wide = 256 if rows % 256 == 0 else rows

    def normalise(c, value, held):
        return call(
            functools.partial(norm_kernel, info),
            row_shapes,
            [pl.BlockSpec((wide, width), lambda t, s: (t, 0)), full((1, width)), full((1, width))]
            + [anywhere] * len(held),
            [
                pl.BlockSpec((1, wide, width), lambda t, s: (c, t, 0)),
                pl.BlockSpec((1, wide, channels), lambda t, s: (c, t, 0)),
                pl.BlockSpec((1, wide, width), lambda t, s: (c, t, 0)),
                pl.BlockSpec((1, wide, LANES), lambda t, s: (c, t, 0)),
            ],
            grid=(rows // wide,),
            aliases={4 + n: n for n in range(len(held))},
            cost_estimate=cost(12 * rows * width, 7 * rows * width),
            name="norm_chunk",
        )(scalars, value, gain2, bias2, *held)

    blocks_out = call(
        functools.partial(cut_kernel, rounds + here),
        [shape_of((part, channels), BF16)] * (rounds + here),
        [
            pl.BlockSpec((part, channels), lambda t, s, n=n: (s[info.p], s[info.cut_block + n]))
            for n in range(rounds + here)
        ],
        [full((part, channels))] * (rounds + here),
        cost_estimate=cost(0, 0),
        name="cut_weight",
    )(scalars, *[weight] * (rounds + here))
    arrived = [move_nodes(blocks_out[r], [(e[0], e[1]) for e in plan[r]]) for r in range(rounds)]
    permuted = jnp.dot(order, after(inputs, blocks_out), preferred_element_type=F32).astype(BF16)
    held = normalise(0, permuted, ())
    locals_here = blocks_out[rounds:]
    if short:
        local_near = [[cross_plane(value, 1), cross_plane(value, 2)] for value in locals_here]
    else:
        local_near = [[cross_plane(value, d) for d in others] for value in locals_here]
    x_core = cross_core(permuted)
    quad = rows // 4
    x_cuts = [(0, quad), (quad, 3 * quad)]
    x_sends = [permuted[start : start + size] for start, size in x_cuts]
    lows = range(1, low)
    x_sends = after(x_sends, x_core)
    x_far = [[cross_low(x_sends[0], dz) for dz in lows]]
    local_near, x_core, held = settle(local_near, x_core, held)

    local_ends = []
    if short:
        local_ends = [[cross_plane(one[:half], 2), cross_plane(two[half:], 1)] for one, two in local_near]
    if short:
        taken = [jnp.stack([value[:half] for value in arrived]), jnp.stack([value[half:] for value in arrived])]
    else:
        taken = [jnp.stack(arrived)]
    taken, local_ends, x_far, held, x_core, x_sends, cotangent = settle(
        taken, local_ends, x_far, held, x_core, x_sends, out_grad
    )
    half_rows = low * rows
    own_half = lax.dynamic_slice_in_dim(cotangent, zhi * half_rows, half_rows, 0)
    unit = half_rows // 32
    far_parts = []
    for start, size in ((0, 7), (7, 25)):
        far_parts.append(lax.dynamic_slice_in_dim(cotangent, (1 - zhi) * half_rows + start * unit, size * unit, 0))
    taken_full = [taken] + [[cross_plane(value, d) for value in taken] for d in (others[:2] if short else others)]
    x_far.append([cross_low(x_sends[1], dz) for dz in lows])
    held = normalise(low, x_core, held)
    gates = jnp.stack([forget_peep, reset_peep, forget_bias, reset_bias])
    taken_full, far_parts, held, gates = settle(taken_full, far_parts, held, gates)

    taken_ends = [cross_plane(taken_full[1][0], 2), cross_plane(taken_full[2][1], 1)] if short else []
    far_came = [cross_high(far_parts[0])]
    gates_far = cross_high(gates)
    taken_full, taken_ends, x_far, far_came, far_parts, gates_far = settle(
        taken_full, taken_ends, x_far, far_came, far_parts, gates_far
    )
    gates = jnp.where(zhi == k, gates, gates_far)
    fp, rp, fb, rb = (gates[n : n + 1] for n in range(4))
    x_cross = []

    x_cross += [[cross_core(value) for value in values] for values in x_far]
    far_cross = [cross_core(far_came[0])]
    own_cross = cross_core(own_half)
    far_came.append(cross_high(far_parts[1]))
    weight_pieces = []
    for n, value in enumerate(locals_here):
        weight_pieces += [value] + local_near[n] + (local_ends[n] if short else [])
    weight_pieces += sum(taken_full, []) + taken_ends
    mix_cost = cost(3 * chunks * rows * width * channels, 4 * chunks * rows * width + 12 * width * channels)
    mixed, maps, full_weight = call(
        functools.partial(mix_kernel, info, low, planes, seg, here, rounds, short),
        mix_shapes + (shape_of((3, width, channels), BF16),),
        [pl.BlockSpec((1, rows, width), lambda t, *_: (t * low, 0, 0)), full((1, channels)), full((1, channels))]
        + [anywhere] * len(weight_pieces),
        [
            pl.BlockSpec((1, 2, rows, channels), lambda t, *_: (t * low, 0, 0, 0)),
            pl.BlockSpec((1, 2, SUB, channels), lambda t, *_: (t * low, 0, 0, 0)),
            anywhere,
        ],
        grid=(2,),
        scratch=[
            pltpu.VMEM((3, width, channels), BF16),
            pltpu.SemaphoreType.DMA(((here + rounds) * (8 if short else planes),)),
            pltpu.SemaphoreType.DMA,
        ],
        lengths=True,
        cost_estimate=mix_cost,
        name="mix_near",
    )(scalars, seq_lengths, held[0], fp, fb, *weight_pieces)

    mixed, maps, full_weight, x_far, x_cross, far_cross, own_cross = settle(
        mixed, maps, full_weight, x_far, x_cross, far_cross, own_cross
    )

    far_order = [far_chunk(low, n) for n in range(2 * (low - 1))]
    far_pieces = [(x_far, x_cross)[c // low][n][c % low - 1] for c in far_order for n in range(len(x_cuts))]
    far_at = lambda t: far_chunk(low, t)
    *held, mixed, maps, run_maps = call(
        functools.partial(mix_far_kernel, info, low, seg, far_order, [size for _, size in x_cuts]),
        row_shapes + mix_shapes + (shape_of((SUB, channels), F32),),
        [full((2, width, channels)), full((1, width)), full((1, width)), full((1, channels)), full((1, channels))]
        + [full((chunks, 2, SUB, channels))]
        + [anywhere] * len(far_pieces)
        + [anywhere] * 5,
        [
            pl.BlockSpec((1, rows, width), lambda t, *_: (far_at(t), 0, 0)),
            pl.BlockSpec((1, rows, channels), lambda t, *_: (far_at(t), 0, 0)),
            pl.BlockSpec((1, rows, width), lambda t, *_: (far_at(t), 0, 0)),
            pl.BlockSpec((1, rows, LANES), lambda t, *_: (far_at(t), 0, 0)),
            pl.BlockSpec((1, 2, rows, channels), lambda t, *_: (far_at(t), 0, 0, 0)),
            full((chunks, 2, SUB, channels)),
            full((SUB, channels)),
        ],
        grid=(len(far_order),),
        scratch=[
            pltpu.VMEM((len(far_order), rows, width), BF16),
            pltpu.SemaphoreType.DMA((len(far_pieces),)),
        ],
        lengths=True,
        aliases={8 + len(far_pieces) + n: n for n in range(5)},
        cost_estimate=mix_cost,
        name="mix_far",
    )(
        scalars, seq_lengths, full_weight, gain2, bias2, fp, fb, maps,
        *far_pieces, *held, mixed,
    )
    normed, highway, hats, invs = held

    def reset_product(chosen, first, held):
        at = lambda t: sum(jnp.where(t == n, c, 0) for n, c in enumerate(chosen))
        return pl.pallas_call(
            reset_kernel,
            grid=(len(chosen),),
            in_specs=[
                pl.BlockSpec((1, rows, width), lambda t: (at(t), 0, 0)),
                pl.BlockSpec((1, width, channels), lambda t: (2, 0, 0)),
            ]
            + [anywhere] * len(held),
            out_specs=pl.BlockSpec((1, rows, channels), lambda t: (at(t), 0, 0)),
            out_shape=shape_of((chunks, rows, channels), BF16),
            input_output_aliases={2: 0} if held else {},
            compiler_params=params(),
            cost_estimate=cost(2 * len(chosen) * rows * width * channels, 2 * len(chosen) * rows * width),
            name="mix_reset",
        )(after(normed, first), full_weight, *held)

    near_chunks = [0, low]
    near_maps = [run_maps] + [cross_plane(run_maps, d) for d in others]
    reset_mixed = reset_product(near_chunks, run_maps, ())
    near_maps, far_came, reset_mixed = settle(near_maps, far_came, reset_mixed)
    far_maps = cross_high(jnp.stack(near_maps))
    far_cross.append(cross_core(far_came[1]))
    reset_mixed = reset_product([c for c in range(chunks) if c not in near_chunks], near_maps, (reset_mixed,))
    near_maps, far_maps, far_cross, reset_mixed = settle(near_maps, far_maps, far_cross, reset_mixed)
    gathered = near_maps + [far_maps]

    map_specs = [full((SUB, channels))] * planes + [full((planes, SUB, channels))]
    block = 128 if rows % 128 == 0 else rows
    blocks = rows // block
    elements = chunks * rows * channels
    runs = (low, rows, channels)
    part_rows = (chunks, block, channels)
    at_block = lambda t, *_: (0, t, 0)
    state_out = call(
        functools.partial(state_kernel, info, low, planes, seg, [value.shape[0] for value in far_came]),
        (
            shape_of(runs, BF16),
            shape_of(runs, BF16),
            shape_of((chunks, rows, channels), BF16),
            shape_of((chunks, rows, channels), BF16),
            shape_of((chunks, rows, channels), BF16),
            shape_of((chunks, rows, channels), BF16),
            shape_of((chunks, SUB, channels), F32),
            shape_of((2, SUB, channels), F32),
            shape_of((SUB, channels), F32),
        ),
        map_specs
        + [
            full((chunks, 2, SUB, channels)),
            pl.BlockSpec((chunks, 2, block, channels), lambda t, *_: (0, 0, t, 0)),
            pl.BlockSpec(part_rows, at_block),
            pl.BlockSpec(part_rows, at_block),
            anywhere,
            anywhere,
        ]
        + [anywhere] * (2 * len(far_came))
        + [
            full((rows, rows)),
        ]
        + [full((1, channels))] * 4,
        [full(runs), full(runs)]
        + [pl.BlockSpec(part_rows, at_block)] * 4
        + [full((chunks, SUB, channels)), full((2, SUB, channels)), full((SUB, channels))],
        grid=(blocks,),
        scratch=[
            pltpu.VMEM((chunks, SUB, channels), F32),
            pltpu.VMEM((chunks, SUB, channels), F32),
            pltpu.VMEM((2 * planes, SUB, channels), F32),
            pltpu.VMEM((chunks, rows, channels), BF16),
            pltpu.VMEM((2, low * rows, channels), BF16),
            pltpu.SemaphoreType.DMA((2, len(far_came))),
        ],
        lengths=True,
        cost_estimate=cost(60 * elements, 30 * elements, 4 * elements),
        name="states",
    )(
        scalars, seq_lengths, *gathered, maps, mixed, reset_mixed, highway, own_half, own_cross, *far_came, *far_cross,
        order, fp, rp, fb, rb,
    )
    out_own, out_far, previous, direct, reset_z, skip, binj, reset_sums, run_back = state_out

    if short:
        places = [[(0, 1, 1), (1, 1, 2)], [(0, 0, 1), (3, 1, 2)], [(2, 1, 1), (1, 0, 2)], [(2, 0, 1), (3, 0, 2)]]
        part_shapes = [(2, half, channels)] * 4
    else:
        places = [[(d, 0, 0)] for d in visits]
        part_shapes = [(1, part, channels)] * planes

    def weight_part(sources, name):
        found = call(
            functools.partial(weight_grad_kernel, len(sources), places),
            [shape_of(shape, BF16) for shape in part_shapes] * len(sources),
            [pl.BlockSpec((chunks, rows, part), lambda t, s: (0, 0, s[info.visits + t]))]
            + [full((chunks, rows, channels))] * len(sources),
            [full(shape) for shape in part_shapes] * len(sources),
            grid=(planes,),
            cost_estimate=cost(2 * chunks * rows * width * channels * len(sources), 4 * chunks * rows * width),
            name=name,
        )(scalars, normed, *sources)
        return [found[n * len(part_shapes) : (n + 1) * len(part_shapes)] for n in range(len(sources))]

    def first_sends(parts):
        if short:
            return [cross_plane(parts[0], 1), cross_plane(parts[1], 2)]
        return [cross_plane(parts[d], d) for d in others]

    def second_start(parts, came):
        if not short:
            return came
        return [add_up([parts[2][1], came[0][1]]), add_up([parts[3][1], came[1][1]])]

    def second_sends(over):
        return [cross_plane(over[0], 2), cross_plane(over[1], 1)] if short else []

    def ends_of(parts, came, over):
        if not short:
            return [parts[0]] + came
        return [parts[2], came[0], over[0][None], parts[3], came[1], over[1][None]]

    def second_end(parts, came, over):
        ends = [value[0] for value in ends_of(parts, came, over)]
        if not short:
            return add_up(ends)
        return jnp.concatenate([add_up(ends[:3]), add_up(ends[3:])], axis=0)

    def to_owners(which, values, chosen):
        back_plan = back_routes[which][2]
        return [
            move_nodes(values[r], [(e[1], e[0]) for e in back_plan[r]]) for r in range(len(back_plan))[chosen]
        ]

    near_back = [run_back] + [cross_plane(run_back, d) for d in others]
    out_core = cross_core(out_far)
    (reset_wg,) = weight_part([reset_z], "weight_grad_reset")
    near_back, reset_wg, out_core, out_own = settle(near_back, reset_wg, out_core, out_own)

    far_back = cross_high(jnp.stack(near_back))
    reset_came = first_sends(reset_wg)
    stay = jnp.where(k == zhi, out_own, out_core)
    leave = jnp.where(k == zhi, out_core, out_own).reshape(half_rows, channels)
    near_back, far_back, leave, binj = settle(near_back, far_back, leave, binj)
    gathered_back = near_back + [far_back]

    leave = [leave[: half_rows // 2], leave[half_rows // 2 :]]
    out_came = [cross_high(leave[0])]

    grad_c, grad_f, forget_sums = call(
        functools.partial(back_kernel, info, low, planes, seg),
        (
            shape_of((chunks, rows, channels), BF16),
            shape_of((chunks, rows, channels), BF16),
            shape_of((2, SUB, channels), F32),
        ),
        map_specs * 2
        + [
            full((chunks, 2, SUB, channels)),
            full((chunks, SUB, channels)),
            pl.BlockSpec((chunks, 2, block, channels), lambda t, *_: (0, 0, blocks - 1 - t, 0)),
        ]
        + [pl.BlockSpec(part_rows, lambda t, *_: (0, blocks - 1 - t, 0))] * 3
        + [full((1, channels))] * 3,
        [pl.BlockSpec(part_rows, lambda t, *_: (0, blocks - 1 - t, 0))] * 2 + [full((2, SUB, channels))],
        grid=(blocks,),
        scratch=[
            pltpu.VMEM((chunks, SUB, channels), F32),
            pltpu.VMEM((2 * planes, SUB, channels), F32),
            pltpu.VMEM((2 * planes, SUB, channels), F32),
        ],
        lengths=True,
        cost_estimate=cost(30 * elements, 20 * elements, 2 * elements),
        name="state_grads",
    )(scalars, seq_lengths, *gathered, *gathered_back, maps, binj, mixed, previous, direct, reset_z, fp, rp, fb)

    def chunk_grads(chosen, sources):
        each = []
        for c in chosen:
            chunk_block = pl.BlockSpec((1, rows, channels), lambda t, s, c=c: (c, 0, 0))
            each += [chunk_block] * 3
            each += [
                pl.BlockSpec((1, rows, channels), lambda t, s, c=c: (c, 0, t)),
                pl.BlockSpec((1, rows, LANES), lambda t, s, c=c: (c, 0, 0)),
                chunk_block,
            ]
        count = len(chosen)
        found = call(
            functools.partial(input_kernel, info, count),
            [shape_of((rows, width), BF16)] * count
            + [shape_of((SUB, rows), F32)] * count
            + [shape_of((2, SUB, width), F32)],
            [
                pl.BlockSpec((3, channels, channels), lambda t, s: (0, t, 0)),
                pl.BlockSpec((1, channels), lambda t, s: (0, t)),
            ]
            + each,
            [pl.BlockSpec((rows, channels), lambda t, s: (0, t))] * count
            + [full((SUB, rows))] * count
            + [pl.BlockSpec((2, SUB, channels), lambda t, s: (0, 0, t))],
            grid=(groups,),
            scratch=[
                pltpu.VMEM((count, rows, channels), F32),
                pltpu.VMEM((count, rows, LANES), F32),
                pltpu.VMEM((count, rows, LANES), F32),
            ],
            cost_estimate=cost(6 * count * rows * width * channels, (8 * rows * count + 6 * channels) * width),
            name="chunk_grads",
        )(scalars, full_weight, gain2, *(list(sources) + [hats, invs, skip]) * count)
        norm_sums.append(found[2 * count])
        return found[:count], found[count : 2 * count]

    norm_sums = []

    grad_c, grad_f, reset_came = settle(grad_c, grad_f, reset_came)
    over = second_start(reset_wg, reset_came)
    grad_c, over = settle(grad_c, over)

    reset_over = second_sends(over)
    (candidate_wg,) = weight_part([grad_c], "weight_grad_candidate")
    candidate_wg, reset_over, out_came, leave = settle(candidate_wg, reset_over, out_came, leave)
    out_came.append(cross_high(leave[1]))
    candidate_wg, grad_f = settle(candidate_wg, grad_f)

    candidate_came = first_sends(candidate_wg)
    (forget_wg,) = weight_part([grad_f], "weight_grad_forget")
    forget_wg, candidate_came = settle(forget_wg, candidate_came)
    over = second_start(candidate_wg, candidate_came)
    sources = (grad_c, grad_f, reset_z)
    over, forget_wg, sources = settle(over, forget_wg, sources)

    candidate_over = second_sends(over)
    forget_came = first_sends(forget_wg)
    far_pairs = [chunk_grads([low + dz, dz], sources) for dz in lows]
    far_pairs, candidate_over, forget_came, out_came, sources = settle(
        far_pairs, candidate_over, forget_came, out_came, sources
    )
    over = second_start(forget_wg, forget_came)
    ends = ends_of(candidate_wg, candidate_came, candidate_over) + ends_of(reset_wg, reset_came, reset_over)
    candidate_part, reset_part, *sends = call(
        functools.partial(pick_kernel, info, len(ends) // 2),
        [shape_of((part, channels), BF16)] * (2 + len(back_routes[0][2])),
        [full((1,) + value.shape[1:]) for value in ends],
        [full((part, channels))] * (2 + len(back_routes[0][2])),
        cost_estimate=cost(0, 3 * part * channels),
        name="pick_parts",
    )(scalars, *ends)
    sends, over, sources, far_pairs = settle(sends, over, sources, far_pairs)

    forget_over = second_sends(over)
    owned_parts = to_owners(0, sends, slice(0, 1))
    from_core = [cross_core(values[0]) for values, _ in far_pairs]
    (other_value,), (other_sums,) = chunk_grads([low], sources)
    other_value, other_sums, forget_over, owned_parts, from_core, sends, sources = settle(
        other_value, other_sums, forget_over, owned_parts, from_core, sends, sources
    )
    forget_part = second_end(forget_wg, forget_came, forget_over)
    forget_part, sends, sources, far_pairs, from_core = settle(forget_part, sends, sources, far_pairs, from_core)

    owned_parts = owned_parts + to_owners(0, sends, slice(1, None))
    last_parts = to_owners(1, [forget_part] * len(back_routes[1][2]), slice(0, 1))
    value_core, sums_core = cross_core(other_value), cross_core(other_sums)
    sums_across = [cross_core(sums[0]) for _, sums in far_pairs]
    (own_value,), (own_sums,) = chunk_grads([0], sources)
    sixteen = rows // 32
    v_cuts = [(0, rows)]
    (
        own_value, own_sums, owned_parts, last_parts, value_core, sums_core, sums_across, far_pairs, from_core, forget_part,
    ) = settle(
        own_value, own_sums, owned_parts, last_parts, value_core, sums_core, sums_across, far_pairs, from_core, forget_part
    )
    far_sums = [sums[1] + sums_across[n] for n, (_, sums) in enumerate(far_pairs)]
    v_sends = [
        [
            add_up([values[1][start : start + size], from_core[n][start : start + size]])
            for n, (values, _) in enumerate(far_pairs)
        ]
        for start, size in v_cuts
    ]

    gate_sums = jnp.sum(jnp.concatenate([forget_sums, reset_sums]), axis=1)
    spread_sums = lax.dynamic_update_slice(
        jnp.zeros((4, width), F32), gate_sums, (0, (z % low + low * k) * channels)
    )
    small = jnp.concatenate([jnp.sum(sum(norm_sums[1:], norm_sums[0]), axis=1), spread_sums], axis=0)
    last_parts = last_parts + to_owners(1, [forget_part] * len(back_routes[1][2]), slice(1, None))
    small_came = cross_low(small, 1)
    far_sums = [cross_low(sums, dz) for dz, sums in zip(lows, far_sums)]
    last_parts, small, small_came, far_sums, v_sends = settle(last_parts, small, small_came, far_sums, v_sends)
    v_came = [[cross_low(value, dz) for dz, value in zip(lows, v_sends[0])]]
    small = small + small_came
    sums = sum([sums_core] + far_sums, own_sums)
    owned_parts = owned_parts + [candidate_part, reset_part] + last_parts + [forget_part]

    block_piece = (3, half, channels)
    own_blocks, give_blocks = call(
        functools.partial(owned_kernel, info, len(owned_parts)),
        [shape_of(block_piece, BF16)] * 2,
        [anywhere] * len(owned_parts),
        [full(block_piece)] * 2,
        scratch=[
            pltpu.VMEM((3, part, channels), F32),
            pltpu.VMEM((len(owned_parts), part, channels), BF16),
            pltpu.SemaphoreType.DMA((len(owned_parts),)),
        ],
        cost_estimate=cost(0, 6 * part * channels),
        name="own_blocks",
    )(scalars, *owned_parts)
    own_blocks, give_blocks, small = settle(own_blocks, give_blocks, small)

    give_blocks = cross_core(give_blocks)
    own_blocks, give_blocks = settle(own_blocks, give_blocks)
    own_sum = add_up([own_blocks, give_blocks])
    own_sum, small, sums = settle(own_sum, small, sums)

    def spread(name, values, steps, held, size=quarter):
        return call(
            functools.partial(spread_kernel, len(values), steps),
            shape_of((width, 3 * channels), F32),
            [full(value.shape) for value in values] + [anywhere] * len(held),
            pl.BlockSpec((size, 3 * channels), lambda t, s: (s[getattr(info, name) + t], 0)),
            grid=(len(steps),),
            aliases={1 + len(values): 0} if held else None,
            cost_estimate=cost(0, 9 * width * channels),
            name="spread_" + name,
        )(scalars, *values, *held)

    whole = [own_sum] + [cross_plane(own_sum, d) for d in (others[:2] if short else others)]
    whole_core = [cross_core(own_sum)]
    small_came = cross_core(small)
    output = call(
        functools.partial(output_kernel, info, low, [value.shape[0] for value in out_came]),
        shape_of((2, half_rows, channels), BF16),
        [full((rows, rows)), full((half_rows, channels))] + [full(value.shape) for value in out_came],
        full((2, half_rows, channels)),
        scratch=[pltpu.VMEM((half_rows, channels), BF16)],
        cost_estimate=cost(4 * low * rows * rows * channels, 8 * half_rows * channels),
        name="output",
    )(scalars, back_order, stay.reshape(half_rows, channels), *out_came)
    weight_grad = spread("own_rows", [own_sum], [(0, 0)], (), half)
    input_part = pl.pallas_call(
        input_part_kernel,
        grid=(rows // wide,),
        in_specs=[
            pl.BlockSpec((wide, width), lambda t: (t, 0)),
            pl.BlockSpec((wide, rows), lambda t: (t, 0)),
            full((rows, width)),
            full((rows, width)),
            full((SUB, rows)),
        ],
        out_specs=pl.BlockSpec((wide, width), lambda t: (t, 0)),
        out_shape=shape_of((rows, width), F32),
        compiler_params=params(),
        cost_estimate=cost(4 * rows * rows * width, 10 * rows * width),
        name="input_part",
    )(inputs, back_order, own_value, value_core, sums)
    whole, whole_core, small, small_came, input_part, output, weight_grad = settle(
        whole, whole_core, small, small_came, input_part, output, weight_grad
    )
    small = small + small_came
    output = output.reshape(groups * rows, channels)

    split = []
    if short:
        split = [whole[1][:, :quarter], whole[2][:, quarter:]]
        whole, split, small = settle(whole, split, small)
        split = [cross_plane(split[0], 2), cross_plane(split[1], 1)]
    whole_core += [cross_core(value) for value in whole[1:]]
    values = whole[1:] + whole_core
    steps = [(n, 0) for n in range(len(values))]
    weight_grad = spread("near_rows", values, steps, (weight_grad,), half)
    weight_grad, split, whole_core, small = settle(weight_grad, split, whole_core, small)

    bits = bits_of(planes)
    small_came = cross_plane(small, bits[0])
    split_core = [cross_core(value) for value in split]
    if short:
        weight_grad = spread("far_rows", split, [(0, 0), (1, 0)], (weight_grad,))
    split_core, small, small_came, weight_grad = settle(split_core, small, small_came, weight_grad)
    small = small + small_came

    small_came = [cross_plane(small, bit) for bit in bits[1:2]]
    if short:
        weight_grad = spread("last_rows", split_core, [(0, 0), (1, 0)], (weight_grad,))
    small, small_came, weight_grad, v_came = settle(small, small_came, weight_grad, v_came)
    small = sum(small_came, small)
    for bit in bits[2:]:
        small = small + cross_plane(small, bit)
    for bit in bits_of(groups)[1:]:
        small = small + cross_low(small, bit)

    parts = [(start, value) for (start, _), came_now in zip(v_cuts, v_came) for value in came_now]
    input_grad = pl.pallas_call(
        functools.partial(last_kernel, [start for start, _ in parts]),
        grid=(rows // wide,),
        in_specs=[pl.BlockSpec((wide, width), lambda t: (t, 0)), pl.BlockSpec((wide, rows), lambda t: (t, 0))]
        + [full(value.shape) for _, value in parts],
        out_specs=pl.BlockSpec((wide, width), lambda t: (t, 0)),
        out_shape=shape_of((rows, width), F32),
        input_output_aliases={0: 0},
        compiler_params=params(),
        cost_estimate=cost(2 * rows * rows * width, 10 * rows * width),
        name="input_grad",
    )(input_part, back_order, *[value for _, value in parts])
    gate_block = lax.dynamic_slice_in_dim(small[2:], z * channels, channels, 1)
    return (
        output,
        input_grad,
        weight_grad,
        small[0],
        small[1],
        gate_block[1],
        gate_block[3],
        gate_block[0],
        gate_block[2],
    )


def solution(mesh):
    placed = (
        P(("seq", "col"), None),
        P(),
        P(),
        P(None, "col"),
        P("col"),
        P("col"),
        P("col"),
        P("col"),
        P(),
        P("seq", "col"),
    )
    return jax.shard_map(
        per_device,
        mesh=mesh,
        in_specs=placed,
        out_specs=(
            P("seq", "col"),
            P(("seq", "col"), None),
            P(None, "col"),
            P(),
            P(),
            P("col"),
            P("col"),
            P("col"),
            P("col"),
        ),
        check_vma=False,
    )
```
